128 devices in a mesh: dp: 4 (over x), expert: 2 (over core), mp: 16 (over z, y).
Axes of the slice: x: 4, y: 4, z: 4, core: 2. Of those that a mesh axis runs over, the one named last changes fastest.
Arguments:
- block_input: bfloat16 [16384, 1024], P(('dp', 'expert', 'mp')), may hold values from -6 to 6
- attn_gain: float32 [1024], replicated, may hold values from 0.5 to 1.5
- qkv_weight: float32 [1024, 3072], replicated, may hold values from -0.1875 to 0.1875
- out_weight: float32 [1024, 1024], replicated, may hold values from -3 to 3
- moe_gain: float32 [1024], replicated, may hold values from 0.5 to 1.5
- router_weight: float32 [1024, 8], replicated, may hold values from -0.125 to 0.125
- gate_weight: float32 [8, 1024, 2816], P('expert', 'dp', 'mp'), may hold values from -0.1875 to 0.1875
- up_weight: float32 [8, 1024, 2816], P('expert', 'dp', 'mp'), may hold values from -0.1875 to 0.1875
- down_weight: float32 [8, 2816, 1024], P('expert', 'mp', 'dp'), may hold values from -0.15625 to 0.15625
- routes: int32 [16384, 2], P(('dp', 'expert', 'mp')), may hold values from 0 to 7, as said below
- slot_index: int32 [16384, 2], P(('dp', 'expert', 'mp')), may hold values from 0 to 127, as said below
- cotangent: bfloat16 [16384, 1024], P(('dp', 'expert', 'mp')), may hold values from -6 to 6
Outputs:
- block_output: bfloat16 [16384, 1024], P(('dp', 'expert', 'mp'))
- input_grad: float32 [16384, 1024], P(('dp', 'expert', 'mp'))
- attn_gain_grad: float32 [1024], replicated
- qkv_grad: float32 [1024, 3072], replicated
- out_grad: float32 [1024, 1024], replicated
- moe_gain_grad: float32 [1024], replicated
- router_grad: float32 [1024, 8], replicated
- gate_grad: float32 [8, 1024, 2816], P('expert', 'dp', 'mp')
- up_grad: float32 [8, 1024, 2816], P('expert', 'dp', 'mp')
- down_grad: float32 [8, 2816, 1024], P('expert', 'mp', 'dp')
The draws below stay inside these ranges and needn't reach their ends.
Inputs may be any that keep to these rules, and one draw needn't show every extreme that they name: routes[t, 0] and routes[t, 1] differ; in one aligned block of 128 rows, chosen at random, every token names one common expert; in the other blocks the routes vary. slot_index[t, j] is the number of pairs (t2, j2) in the same aligned block of 128 rows, with t2 < t, or t2 = t and j2 < j, whose expert equals routes[t, j].
All inputs are finite; a program needn't handle non-finite values.
Results may differ from the reference program's by a relative error of at most 0.019.
Values may be sent and summed in bfloat16 or wider, within the bound.
A program may use at most 256 MiB of HBM per device.

```python
import jax
import jax.numpy as jnp
from jax import lax

D = 1024
FF = 2816
HEADS = 16
HEAD_DIM = 64
TOK_DEV = 128
EXPERT_TOTAL = 8
CAP = 40
SEQ = 2048
TOKENS = 16384


def route_pair(key):
    extra_score_key, jitter_key, block_random_key, favored_expert_key = jax.random.split(key, 4)
    expert_ordering = jax.random.permutation(extra_score_key, EXPERT_TOTAL).astype(jnp.int32)
    extra_score = expert_ordering * expert_ordering * 200 // EXPERT_TOTAL
    jitter_values = jax.random.randint(jitter_key, (TOKENS, EXPERT_TOTAL), 0, 65536, dtype=jnp.int32)
    full_block = jax.random.randint(block_random_key, (), 0, TOKENS // TOK_DEV, dtype=jnp.int32)
    hot_expert = jax.random.randint(favored_expert_key, (), 0, EXPERT_TOTAL, dtype=jnp.int32)
    row_block = (jnp.arange(TOKENS, dtype=jnp.int32) // TOK_DEV)[:, None]
    column_entry = jnp.arange(EXPERT_TOTAL, dtype=jnp.int32)[None, :]
    forced_choice = jnp.where((row_block == full_block) & (column_entry == hot_expert), 16777216, 0).astype(jnp.int32)
    router_scores = (jitter_values + extra_score[None, :] + forced_choice) * EXPERT_TOTAL + column_entry
    return lax.top_k(router_scores, 2)[1].astype(jnp.int32)


def draw_routes(key, part):
    return route_pair(key)


def draw_slot_index(key, part):
    chosen = route_pair(key)
    onehot = (chosen[:, :, None] == jnp.arange(EXPERT_TOTAL, dtype=jnp.int32)[None, None, :]).astype(jnp.int32)
    blocks = onehot.reshape(TOKENS // TOK_DEV, TOK_DEV * 2, EXPERT_TOTAL)
    earlier = jnp.cumsum(blocks, axis=1) - blocks
    ranks = jnp.sum(earlier * blocks, axis=2)
    return ranks.reshape(TOKENS, 2).astype(jnp.int32)


def level_of(stream_key, dims, pieces, least, top_value):
    def one(dim, shards_of):
        heights = jax.random.uniform(jax.random.fold_in(jax.random.fold_in(stream_key, 6), dim), (shards_of,), jnp.float32, least / len(pieces), top_value / len(pieces))
        return jnp.repeat(jnp.exp(heights), dims[dim] // shards_of).reshape((-1,) + (1,) * (len(dims) - dim - 1))

    loudness = one(*pieces[0])
    for cut in pieces[1:]:
        loudness = loudness * one(*cut)
    return loudness


def noise(own_key, extent, width, reach, shards=(), held_as=jnp.bfloat16):
    level = level_of(own_key, extent, shards, -0.22, 0.18) if shards else 1.0
    array = jax.random.normal(own_key, extent, jnp.float32) * width * level
    return jnp.minimum(jnp.maximum(array, -reach), reach).astype(held_as)


def setup_inputs(seed: int = 0) -> dict:
    key_list = jax.random.split(jax.random.key(seed), 13)
    return {
        "block_input": noise(key_list[0], (TOKENS, D), 1.0, 6.0, ((0, 128),)),
        "attn_gain": jnp.clip(1.0 + 0.1 * jax.random.normal(key_list[1], (D,), jnp.float32), 0.5, 1.5),
        "qkv_weight": noise(key_list[2], (D, 3 * D), D ** -0.5, 0.1875, (), jnp.float32),
        "out_weight": noise(key_list[3], (D, D), (max(D // 256, 1)) ** -0.5, 3.0, (), jnp.float32),
        "moe_gain": jnp.clip(1.0 + 0.1 * jax.random.normal(key_list[4], (D,), jnp.float32), 0.5, 1.5),
        "router_weight": noise(key_list[5], (D, EXPERT_TOTAL), (2 * D) ** -0.5, 0.125, (), jnp.float32),
        "gate_weight": noise(key_list[6], (EXPERT_TOTAL, D, FF), D ** -0.5, 0.1875, ((0, 2), (1, 4), (2, 16)), jnp.float32),
        "up_weight": noise(key_list[7], (EXPERT_TOTAL, D, FF), D ** -0.5, 0.1875, ((0, 2), (1, 4), (2, 16)), jnp.float32),
        "down_weight": noise(key_list[8], (EXPERT_TOTAL, FF, D), (FF // 2) ** -0.5, 0.15625, ((0, 2), (1, 16), (2, 4)), jnp.float32),
        "routes": draw_routes(jax.random.fold_in(key_list[12], 71), 0),
        "slot_index": draw_slot_index(jax.random.fold_in(key_list[12], 71), 0),
        "cotangent": noise(key_list[11], (TOKENS, D), 1.0, 6.0, ((0, 128),)),
    }


EPSILON = 1e-06
HIGHEST = lax.Precision.HIGHEST

@jax.custom_vjp
def low(v):
    return lax.optimization_barrier(v.astype(jnp.bfloat16)).astype(jnp.float32)

@jax.custom_vjp
def low_back(v):
    return v

def low_keep(v):
    return (low(v), None)

def low_pass(kept, grad):
    return (grad,)

def back_keep(v):
    return (v, None)

def back_low(kept, grad):
    return (low(grad),)
low.defvjp(low_keep, low_pass)
low_back.defvjp(back_keep, back_low)

def rms_norm(values, gain):
    return values * lax.rsqrt(lax.optimization_barrier(jnp.mean(values * values, axis=-1, keepdims=True)) + EPSILON) * gain

def attend(packed):
    queries = packed[:, :D].reshape(SEQ, HEADS, HEAD_DIM)
    key_rows = packed[:, D:2 * D].reshape(SEQ, HEADS, HEAD_DIM)
    value_rows = packed[:, 2 * D:].reshape(SEQ, HEADS, HEAD_DIM)
    router_scores = low_back(jnp.einsum('qhd,khd->hqk', queries, key_rows, precision=HIGHEST) * 0.125)
    probs = low(jax.nn.softmax(router_scores, axis=-1))
    context = jnp.einsum('hqk,khd->qhd', probs, value_rows, precision=HIGHEST)
    return context.reshape(SEQ, D)

def expert_apply(operands):
    rows, gate_mat, up_mat, down_mat = operands
    gate_pre = low_back(jnp.dot(rows, low(gate_mat), precision=HIGHEST, preferred_element_type=jnp.float32))
    up_pre = low_back(jnp.dot(rows, low(up_mat), precision=HIGHEST, preferred_element_type=jnp.float32))
    hidden = low(jax.nn.gelu(gate_pre, approximate=True) * up_pre)
    return low(low_back(jnp.dot(hidden, low(down_mat), precision=HIGHEST, preferred_element_type=jnp.float32)))

def forward(block_input, attn_gain, qkv_weight, out_weight, moe_gain, router_weight, gate_weight, up_weight, down_weight, routes, slot_index):
    normed = low(rms_norm(block_input, attn_gain))
    packed = jnp.dot(normed, low(qkv_weight), precision=HIGHEST, preferred_element_type=jnp.float32)
    packed = low(low_back(packed))
    context = lax.map(jax.checkpoint(attend), packed.reshape(TOKENS // SEQ, SEQ, 3 * D)).reshape(TOKENS, D)
    context = low(low_back(context))
    branch = low_back(jnp.dot(context, low(out_weight), precision=HIGHEST, preferred_element_type=jnp.float32))
    middle = block_input + branch
    moe_in = rms_norm(middle, moe_gain)
    logits = jnp.dot(moe_in, router_weight, precision=HIGHEST, preferred_element_type=jnp.float32)
    probs = jax.nn.softmax(logits, axis=-1)
    chosen = jnp.take_along_axis(probs, routes, axis=1)
    gates = chosen / lax.optimization_barrier(jnp.sum(chosen, axis=1, keepdims=True))
    rounded = low(moe_in)
    source = (jnp.arange(TOKENS) // TOK_DEV).astype(jnp.int32)
    valid = slot_index < CAP
    place = jnp.where(valid, slot_index, 0).astype(jnp.int32)
    buffer = jnp.zeros((TOKENS // TOK_DEV, EXPERT_TOTAL, CAP, D), jnp.float32)
    for member in range(2):
        sent = jnp.where(valid[:, member, None], low_back(rounded), 0.0)
        buffer = buffer.at[source, routes[:, member], place[:, member]].add(sent)
    by_expert = jnp.swapaxes(buffer, 0, 1).reshape(EXPERT_TOTAL, TOKENS // TOK_DEV * CAP, D)
    results = lax.map(jax.checkpoint(expert_apply), (by_expert, gate_weight, up_weight, down_weight))
    results = jnp.swapaxes(results.reshape(EXPERT_TOTAL, TOKENS // TOK_DEV, CAP, D), 0, 1)
    mixture = jnp.zeros((TOKENS, D), jnp.float32)
    for member in range(2):
        fetched = results[source, routes[:, member], place[:, member]]
        mixture = mixture + gates[:, member, None] * jnp.where(valid[:, member, None], fetched, 0.0)
    return middle + mixture

def reference(block_input, attn_gain, qkv_weight, out_weight, moe_gain, router_weight, gate_weight, up_weight, down_weight, routes, slot_index, cotangent):
    floats = (block_input.astype(jnp.float32), attn_gain, qkv_weight, out_weight, moe_gain, router_weight, gate_weight, up_weight, down_weight)

    def apply_block(input_rows, gain_one, qkv_mat, out_mat, gain_two, router_mat, gate_mat, up_mat, down_mat):
        return forward(input_rows, gain_one, qkv_mat, out_mat, gain_two, router_mat, gate_mat, up_mat, down_mat, routes, slot_index)
    result, pullback = jax.vjp(apply_block, *floats)
    grads = pullback(cotangent.astype(jnp.float32))
    return (result.astype(jnp.bfloat16), grads[0], grads[1], grads[2], grads[3], grads[4], grads[5], grads[6], grads[7], grads[8])
```

```python
from functools import partial

import jax
import jax.numpy as jnp
from jax import lax
from jax.experimental import pallas as pl
from jax.experimental.pallas import tpu as pltpu
from jax.sharding import PartitionSpec as P

HEADS = 16
EPSILON = 1e-06
HIGHEST = lax.Precision.HIGHEST
MESH = pl.DeviceIdType.MESH
F32 = jnp.float32
BF16 = jnp.bfloat16
VMEM = pltpu.VMEM
ROWS = 40
FFB = 176
FFQ = 704
DB = 256
NT = (((1,), (1,)), ((), ()))
TN = (((0,), (0,)), ((), ()))


def dot(a, b):
    return jnp.dot(a, b, preferred_element_type=F32)


def dot_nt(a, b):
    return lax.dot_general(a, b, NT, preferred_element_type=F32)


def dot_tn(a, b):
    return lax.dot_general(a, b, TN, preferred_element_type=F32)


def spot():
    m = lax.axis_index("mp")
    return lax.axis_index("dp"), lax.axis_index("expert"), m, m // 4, m % 4


def params(cid, mb=60):
    return pltpu.CompilerParams(
        collective_id=cid, has_side_effects=True, vmem_limit_bytes=mb * 1024 * 1024
    )


def swapped(c, z):
    return z % 2, 2 * (z // 2) + c


def weight_kernel(w_ref, out_ref, stage, s_send, s_recv, x_send, x_recv, here):
    x, c, m, z, y = spot()
    pc, pz = swapped(c, z)
    away = (pc - c) * (pc - c)
    barrier = pltpu.get_barrier_semaphore()

    def remote(el):
        return (away == 1) | (el != y)

    for el in range(4):

        @pl.when(remote(el))
        def _():
            pl.semaphore_signal(
                barrier, inc=1, device_id={"expert": pc, "mp": pz * 4 + el}, device_id_type=MESH
            )

    for d in range(1, 4):
        pl.semaphore_signal(barrier, inc=1, device_id={"dp": (x + d) % 4}, device_id_type=MESH)
    pl.semaphore_wait(barrier, 6 + away)

    def rows(at):
        return stage.at[:, pl.ds(pl.multiple_of(at * FFB, 16), FFB), :]

    def hop(el):
        return pltpu.make_async_remote_copy(
            src_ref=w_ref.at[el],
            dst_ref=rows(y),
            send_sem=s_send.at[el],
            recv_sem=s_recv.at[y],
            device_id={"expert": pc, "mp": pz * 4 + el},
            device_id_type=MESH,
        )

    def landed(el):
        return pltpu.make_async_remote_copy(
            src_ref=w_ref.at[el],
            dst_ref=rows(el),
            send_sem=s_send.at[el],
            recv_sem=s_recv.at[el],
            device_id={"expert": pc, "mp": pz * 4 + el},
            device_id_type=MESH,
        )

    for el in range(4):

        @pl.when(remote(el))
        def _():
            hop(el).start()

    @pl.when(away == 0)
    def _():
        own = pltpu.make_async_copy(w_ref.at[y], rows(y), here.at[0])
        own.start()
        own.wait()

    for el in range(4):

        @pl.when(remote(el))
        def _():
            landed(el).wait_recv()

    def columns(at):
        return out_ref.at[:, :, pl.ds(pl.multiple_of(at * DB, DB), DB)]

    def fan(d, at):
        return pltpu.make_async_remote_copy(
            src_ref=stage,
            dst_ref=columns(at),
            send_sem=x_send.at[d],
            recv_sem=x_recv.at[d],
            device_id={"dp": (x + d) % 4},
            device_id_type=MESH,
        )

    for d in (2, 1, 3):
        fan(d, x).start()
    own = pltpu.make_async_copy(stage, columns(x), here.at[0])
    own.start()
    own.wait()
    for d in range(1, 4):
        fan(d, (x + 4 - d) % 4).wait_recv()
    for d in range(1, 4):
        fan(d, x).wait_send()
    for el in range(4):

        @pl.when(remote(el))
        def _():
            hop(el).wait_send()


def fetch_weights(blocks):
    return pl.pallas_call(
        weight_kernel,
        out_shape=jax.ShapeDtypeStruct((3, FFQ, 4 * DB), BF16),
        in_specs=[pl.BlockSpec(memory_space=VMEM)],
        out_specs=pl.BlockSpec(memory_space=pl.ANY),
        scratch_shapes=[
            VMEM((3, FFQ, DB), BF16),
            pltpu.SemaphoreType.DMA((4,)),
            pltpu.SemaphoreType.DMA((4,)),
            pltpu.SemaphoreType.DMA((4,)),
            pltpu.SemaphoreType.DMA((4,)),
            pltpu.SemaphoreType.DMA((1,)),
        ],
        compiler_params=params(1, 32),
    )(blocks)


def grad_kernel(g_ref, out_ref, s_send, s_recv, here):
    x, c, m, z, y = spot()
    pc, pz = swapped(c, z)
    away = (pc - c) * (pc - c)
    barrier = pltpu.get_barrier_semaphore()

    def remote(at):
        return (away == 1) | (at != y)

    for at in range(4):

        @pl.when(remote(at))
        def _():
            pl.semaphore_signal(
                barrier, inc=1, device_id={"expert": pc, "mp": pz * 4 + at}, device_id_type=MESH
            )

    pl.semaphore_wait(barrier, 3 + away)

    def hop(at, slot):
        return pltpu.make_async_remote_copy(
            src_ref=g_ref.at[:, pl.ds(at * FFB, FFB), :],
            dst_ref=out_ref.at[slot],
            send_sem=s_send.at[at],
            recv_sem=s_recv.at[slot],
            device_id={"expert": pc, "mp": pz * 4 + at},
            device_id_type=MESH,
        )

    for at in range(4):

        @pl.when(remote(at))
        def _():
            hop(at, y).start()

    @pl.when(away == 0)
    def _():
        own = pltpu.make_async_copy(
            g_ref.at[:, pl.ds(pl.multiple_of(y * FFB, 16), FFB), :], out_ref.at[y], here.at[0]
        )
        own.start()
        own.wait()

    for at in range(4):

        @pl.when(remote(at))
        def _():
            hop(at, at).wait_recv()

    for at in range(4):

        @pl.when(remote(at))
        def _():
            hop(at, y).wait_send()


def return_grads(grads):
    return pl.pallas_call(
        grad_kernel,
        out_shape=jax.ShapeDtypeStruct((4, 3, FFB, DB), BF16),
        in_specs=[pl.BlockSpec(memory_space=VMEM)],
        out_specs=pl.BlockSpec(memory_space=VMEM),
        scratch_shapes=[
            pltpu.SemaphoreType.DMA((4,)),
            pltpu.SemaphoreType.DMA((4,)),
            pltpu.SemaphoreType.DMA((1,)),
        ],
        compiler_params=params(2, 32),
    )(grads)


GELU_A = 0.7978845608
GELU_B = 0.044715


def moe_kernel(
    send_ref,
    w_ref,
    ret_ref,
    grad_ref,
    recv,
    own_part,
    sib_send,
    sib_recv,
    back,
    xs,
    cs,
    hid,
    gcs,
    ucs,
    d_send,
    d_recv,
    f_send,
    f_recv,
    p_send,
    p_recv,
    r_send,
    r_recv,
):
    x, c, m, z, y = spot()
    barrier = pltpu.get_barrier_semaphore()

    def greet(k, carry):
        pl.semaphore_signal(barrier, inc=1, device_id={"mp": (m + k) % 16}, device_id_type=MESH)
        return carry

    lax.fori_loop(1, 16, greet, 0)
    pl.semaphore_signal(barrier, inc=1, device_id={"expert": 1 - c}, device_id_type=MESH)
    pl.semaphore_wait(barrier, 16)

    def expert_of(t):
        return ((t // 4) % 2) * 4 + t % 4

    def dispatch(k):
        t = (m + k) % 16
        return pltpu.make_async_remote_copy(
            src_ref=send_ref.at[expert_of(t)],
            dst_ref=recv.at[0, k],
            send_sem=d_send.at[k],
            recv_sem=d_recv.at[k],
            device_id={"mp": t},
            device_id_type=MESH,
        )

    def forward(k):
        return pltpu.make_async_remote_copy(
            src_ref=recv.at[0, k],
            dst_ref=recv.at[1, k],
            send_sem=f_send.at[k],
            recv_sem=f_recv.at[k],
            device_id={"expert": 1 - c},
            device_id_type=MESH,
        )

    def partials(j):
        return pltpu.make_async_remote_copy(
            src_ref=sib_send.at[j],
            dst_ref=sib_recv.at[j],
            send_sem=p_send.at[j],
            recv_sem=p_recv.at[j],
            device_id={"expert": 1 - c},
            device_id_type=MESH,
        )

    def giving(k):
        return pltpu.make_async_remote_copy(
            src_ref=back.at[k],
            dst_ref=ret_ref.at[m],
            send_sem=r_send.at[k],
            recv_sem=r_recv.at[k],
            device_id={"mp": (m + 16 - k) % 16},
            device_id_type=MESH,
        )

    def start_dispatch(k, carry):
        dispatch(k).start()
        return carry

    lax.fori_loop(1, 16, start_dispatch, 0)
    recv[0, 0] = send_ref[expert_of(m)]

    def finish(j):
        partials(j).wait_recv()
        back[pl.ds(4 * j, 4)] = (own_part[...] + sib_recv[j].astype(F32)).astype(BF16)
        for i in range(4):
            k = 4 * j + i

            @pl.when(k > 0)
            def _():
                giving(k).start()

            @pl.when(k == 0)
            def _():
                ret_ref[m] = back[0]

    def chunk(j, carry):
        for i in range(4):
            k = 4 * j + i

            @pl.when(k > 0)
            def _():
                dispatch(k).wait_recv()

            forward(k).start()

        @pl.when(j > 0)
        def _():
            finish(j - 1)

        for i in range(4):
            forward(4 * j + i).wait_recv()
        blk = recv[:, pl.ds(4 * j, 4)].astype(F32)
        span = pl.ds(pl.multiple_of(j * 8 * ROWS, 16), 8 * ROWS)
        xs[span] = blk[:, :, :ROWS].reshape(8 * ROWS, 4 * DB).astype(BF16)
        cs[span] = blk[:, :, ROWS:].reshape(8 * ROWS, 4 * DB).astype(BF16)
        gate = dot_nt(xs[span], w_ref[0])
        up = dot_nt(xs[span], w_ref[1])
        hid_cot = dot_nt(cs[span], w_ref[2])
        sq = gate * gate
        th = jnp.tanh(GELU_A * (gate + GELU_B * (gate * sq)))
        half = 0.5 * (1.0 + th)
        act = gate * half
        slope = half + 0.5 * gate * (1.0 - th * th) * (GELU_A * (1.0 + 3.0 * GELU_B * sq))
        hid[span] = (act * up).astype(BF16)
        gcs[span] = (hid_cot * up * slope).astype(BF16)
        ucs[span] = (hid_cot * act).astype(BF16)
        out = dot(hid[span], w_ref[2]).reshape(2, 4, ROWS, 4 * DB)
        rows = (dot(gcs[span], w_ref[0]) + dot(ucs[span], w_ref[1])).reshape(2, 4, ROWS, 4 * DB)
        own_part[:, :ROWS] = out[0]
        own_part[:, ROWS:] = rows[0]
        sib_send[j] = jnp.concatenate([out[1], rows[1]], axis=1).astype(BF16)
        partials(j).start()
        return carry

    lax.fori_loop(0, 4, chunk, 0)
    finish(3)
    for i, (a, b) in enumerate(((gcs, xs), (ucs, xs), (hid, cs))):
        g = dot_tn(a[...], b[...])
        for at in range(4):
            grad_ref[at, i] = g[:, at * DB : (at + 1) * DB].astype(BF16)

    def drain(k, carry):
        pltpu.make_async_remote_copy(
            src_ref=back.at[k],
            dst_ref=ret_ref.at[(m + k) % 16],
            send_sem=r_send.at[k],
            recv_sem=r_recv.at[k],
            device_id={"mp": (m + 16 - k) % 16},
            device_id_type=MESH,
        ).wait()
        dispatch(k).wait_send()
        forward(k).wait_send()
        return carry

    lax.fori_loop(1, 16, drain, 0)
    forward(0).wait_send()
    for j in range(4):
        partials(j).wait_send()


def moe(send, weights):
    dma = pltpu.SemaphoreType.DMA
    block = (2 * ROWS, 4 * DB)
    return pl.pallas_call(
        moe_kernel,
        out_shape=(
            jax.ShapeDtypeStruct((16, *block), BF16),
            jax.ShapeDtypeStruct((4, 3, FFQ, DB), BF16),
        ),
        in_specs=[pl.BlockSpec(memory_space=VMEM)] * 2,
        out_specs=(pl.BlockSpec(memory_space=VMEM),) * 2,
        scratch_shapes=[
            VMEM((2, 16, *block), BF16),
            VMEM((4, *block), F32),
            VMEM((4, 4, *block), BF16),
            VMEM((4, 4, *block), BF16),
            VMEM((16, *block), BF16),
            VMEM((32 * ROWS, 4 * DB), BF16),
            VMEM((32 * ROWS, 4 * DB), BF16),
            VMEM((32 * ROWS, FFQ), BF16),
            VMEM((32 * ROWS, FFQ), BF16),
            VMEM((32 * ROWS, FFQ), BF16),
            dma((16,)),
            dma((16,)),
            dma((16,)),
            dma((16,)),
            dma((4,)),
            dma((4,)),
            dma((16,)),
            dma((16,)),
        ],
        compiler_params=params(3, 62),
    )(send, weights)


def rms_norm(values, gain):
    return values * lax.rsqrt(jnp.mean(values * values, axis=-1, keepdims=True) + EPSILON) * gain


def gating(moe_in, router_weight, routes):
    logits = jnp.dot(moe_in, router_weight, precision=HIGHEST, preferred_element_type=F32)
    probs = jax.nn.softmax(logits, axis=-1)
    onehot = (routes[:, :, None] == jnp.arange(8, dtype=routes.dtype)).astype(F32)
    chosen = jnp.sum(probs[:, None, :] * onehot, axis=2)
    return chosen / jnp.sum(chosen, axis=1, keepdims=True)


def to_heads(rows):
    return lax.all_to_all(rows, "mp", split_axis=2, concat_axis=0, tiled=True)


def to_tokens(rows):
    return lax.all_to_all(rows, "mp", split_axis=0, concat_axis=2, tiled=True)


def attention_forward(queries, key_heads, value_heads):
    router_scores = jnp.einsum("qhd,khd->hqk", queries, key_heads, preferred_element_type=F32) * 0.125
    log_total = jax.nn.logsumexp(router_scores, axis=-1, keepdims=True)
    probs_low = jnp.exp(router_scores - log_total).astype(BF16)
    context = jnp.einsum("hqk,khd->qhd", probs_low, value_heads, preferred_element_type=F32)
    return (context.astype(BF16), log_total)


def attention_backward(queries, key_heads, value_heads, log_total, context_cot):
    scores_again = jnp.einsum("qhd,khd->hqk", queries, key_heads, preferred_element_type=F32) * 0.125
    probs_full = jnp.exp(scores_again - log_total)
    probs_again = probs_full.astype(BF16)
    probs_cot = jnp.einsum("qhd,khd->hqk", context_cot, value_heads, preferred_element_type=F32)
    inner = jnp.sum(probs_full * probs_cot, axis=-1, keepdims=True)
    score_cot = (probs_full * (probs_cot - inner)).astype(BF16)
    query_cot = jnp.einsum("hqk,khd->qhd", score_cot, key_heads, preferred_element_type=F32) * 0.125
    key_part = jnp.einsum("hqk,qhd->khd", score_cot, queries, preferred_element_type=F32) * 0.125
    value_part = jnp.einsum("hqk,qhd->khd", probs_again, context_cot, preferred_element_type=F32)
    return (query_cot, key_part, value_part)


def body(
    block_input,
    attn_gain,
    qkv_weight,
    out_weight,
    moe_gain,
    router_weight,
    gate_weight,
    up_weight,
    down_weight,
    routes,
    slot_index,
    cotangent,
):
    tok_rows, width = block_input.shape
    head_size = width // HEADS
    blocks = jnp.stack(
        [
            jnp.swapaxes(gate_weight, 1, 2).astype(BF16),
            jnp.swapaxes(up_weight, 1, 2).astype(BF16),
            down_weight.astype(BF16),
        ],
        axis=1,
    )
    weights = fetch_weights(blocks)
    inputs = block_input.astype(F32)
    qkv_low = qkv_weight.astype(BF16)
    out_low = out_weight.astype(BF16)
    normed, norm_back = jax.vjp(rms_norm, inputs, attn_gain)
    normed_low = normed.astype(BF16)
    packed = dot(normed_low, qkv_low).astype(BF16)
    by_head = to_heads(packed.reshape(tok_rows, 3, HEADS, head_size))
    queries = by_head[:, 0]
    key_heads = by_head[:, 1]
    value_heads = by_head[:, 2]
    context_here, log_total = attention_forward(queries, key_heads, value_heads)
    context = to_tokens(context_here[:, None]).reshape(tok_rows, width)
    middle = inputs + dot(context, out_low)
    moe_in, moe_back = jax.vjp(rms_norm, middle, moe_gain)
    gates, gate_back = jax.vjp(partial(gating, routes=routes), moe_in, router_weight)
    valid = slot_index < ROWS
    place = routes * (2 * ROWS) + slot_index
    keep = valid.astype(F32)
    upstream = cotangent.astype(F32)
    pair_rows = jnp.repeat(moe_in.astype(BF16), 2, axis=0)
    pair_cots = (gates[:, :, None] * upstream[:, None, :]).astype(BF16).reshape(2 * tok_rows, width)
    target = jnp.where(valid, place, 16 * ROWS).reshape(-1)
    cot_target = jnp.where(valid, place + ROWS, 16 * ROWS).reshape(-1)
    send = jnp.zeros((16 * ROWS, width), BF16)
    send = send.at[target].set(pair_rows, mode="drop").at[cot_target].set(pair_cots, mode="drop")
    returned, grads = moe(send.reshape(8, 2 * ROWS, width), weights)
    returned = returned.reshape(2, 8 * 2 * ROWS, width).astype(F32)
    returned = (returned[0] + returned[1]).astype(BF16)
    fetch_at = jnp.where(valid, place, 0)
    fetched = jnp.take(returned, fetch_at, axis=0).astype(F32) * keep[:, :, None]
    block_output = (middle + jnp.sum(gates[:, :, None] * fetched, axis=1)).astype(BF16)
    gate_cot = jnp.sum(upstream[:, None, :] * fetched, axis=2)
    moe_cot = jnp.sum(
        jnp.take(returned, fetch_at + ROWS, axis=0).astype(F32) * keep[:, :, None], axis=1
    )
    router_in_cot, router_term = gate_back(gate_cot)
    middle_norm_cot, moe_gain_term = moe_back(moe_cot + router_in_cot)
    middle_cot = upstream + middle_norm_cot
    branch_cot = middle_cot.astype(BF16)
    out_term = dot_tn(context, branch_cot)
    context_cot = dot_nt(branch_cot, out_low)
    context_cot = context_cot.astype(BF16).reshape(tok_rows, HEADS, head_size)
    cot_heads = to_heads(context_cot[:, None])[:, 0]
    query_cot, key_part, value_part = attention_backward(
        queries, key_heads, value_heads, log_total, cot_heads
    )
    stacked = jnp.stack(
        [query_cot.astype(BF16), key_part.astype(BF16), value_part.astype(BF16)], axis=1
    )
    packed_cot = to_tokens(stacked).reshape(tok_rows, 3 * width)
    qkv_term = dot_tn(normed_low, packed_cot)
    normed_cot = dot_nt(packed_cot, qkv_low)
    input_norm_cot, attn_gain_term = norm_back(normed_cot)
    input_grad = middle_cot + input_norm_cot
    everyone = ("dp", "expert", "mp")
    out_grad = lax.psum(out_term.astype(BF16), everyone).astype(F32)
    qkv_grad = lax.psum(qkv_term.astype(BF16), everyone).astype(F32)
    small = jnp.concatenate([attn_gain_term, moe_gain_term, router_term.reshape(-1)])
    small = lax.psum(small, everyone)
    mine = lax.psum_scatter(grads, "dp", scatter_dimension=0, tiled=True)
    mine = return_grads(mine.reshape(3, FFQ, DB)).astype(F32)
    return (
        block_output,
        input_grad,
        small[:width],
        qkv_grad,
        out_grad,
        small[width : 2 * width],
        small[2 * width :].reshape(width, 8),
        jnp.swapaxes(mine[:, 0], 1, 2),
        jnp.swapaxes(mine[:, 1], 1, 2),
        mine[:, 2],
    )


def solution(mesh):
    tokens = P(("dp", "expert", "mp"), None)
    cols = P("expert", "dp", "mp")
    rows = P("expert", "mp", "dp")
    return jax.shard_map(
        body,
        mesh=mesh,
        in_specs=(tokens, P(), P(), P(), P(), P(), cols, cols, rows, tokens, tokens, tokens),
        out_specs=(tokens, tokens, P(), P(), P(), P(), P(), cols, cols, rows),
        check_vma=False,
    )
```

```python
from functools import partial

import jax
import jax.numpy as jnp
from jax import lax
from jax.experimental import pallas as pl
from jax.experimental.pallas import tpu as pltpu
from jax.sharding import PartitionSpec as P

HEADS = 16
EPSILON = 1e-06
HIGHEST = lax.Precision.HIGHEST
MESH = pl.DeviceIdType.MESH
F32 = jnp.float32
BF16 = jnp.bfloat16
VMEM = pltpu.VMEM
ROWS = 40
FFB = 176
FFQ = 704
DB = 256
NT = (((1,), (1,)), ((), ()))
TN = (((0,), (0,)), ((), ()))


def dot(a, b):
    return jnp.dot(a, b, preferred_element_type=F32)


def dot_nt(a, b):
    return lax.dot_general(a, b, NT, preferred_element_type=F32)


def dot_tn(a, b):
    return lax.dot_general(a, b, TN, preferred_element_type=F32)


def spot():
    m = lax.axis_index("mp")
    return lax.axis_index("dp"), lax.axis_index("expert"), m, m // 4, m % 4


def params(cid, mb=60):
    return pltpu.CompilerParams(
        collective_id=cid, has_side_effects=True, vmem_limit_bytes=mb * 1024 * 1024
    )


def swapped(c, z):
    return z % 2, 2 * (z // 2) + c


def mp_at(m, k):
    return {"mp": (m + k) % 16}


def y_at(z, y, d):
    return {"mp": z * 4 + (y + d) % 4}


def z_at(z, y, d):
    return {"mp": ((z + d) % 4) * 4 + y}


def push(src, dst, send, recv, device):
    return pltpu.make_async_remote_copy(
        src_ref=src, dst_ref=dst, send_sem=send, recv_sem=recv, device_id=device, device_id_type=MESH
    )


def lanes(at, size):
    return pl.ds(pl.multiple_of(at * size, size), size)


def greet_mp(barrier, m):
    def one(k, carry):
        pl.semaphore_signal(barrier, inc=1, device_id=mp_at(m, k), device_id_type=MESH)
        return carry

    lax.fori_loop(1, 16, one, 0)


def attend_kernel(
    x_ref,
    gain_ref,
    wq_ref,
    gate_ref,
    up_ref,
    down_ref,
    ctx_ref,
    qkv_ref,
    ctx_here_ref,
    lse_ref,
    nall_ref,
    w_out_ref,
    down_out_ref,
    normed,
    heads,
    blocks,
    stage,
    key_rows,
    ctx_low,
    here,
    s_send,
    s_recv,
    x_send,
    x_recv,
    a_send,
    a_recv,
    n_send,
    n_recv,
    c_send,
    c_recv,
):
    x, c, m, z, y = spot()
    pc, pz = swapped(c, z)
    away = (pc - c) * (pc - c)
    barrier = pltpu.get_barrier_semaphore()

    def remote(el):
        return (away == 1) | (el != y)

    def partner(el):
        return {"expert": pc, "mp": pz * 4 + el}

    greet_mp(barrier, m)
    for el in range(4):

        @pl.when(remote(el))
        def _():
            pl.semaphore_signal(barrier, inc=1, device_id=partner(el), device_id_type=MESH)

    for d in range(1, 4):
        pl.semaphore_signal(barrier, inc=1, device_id={"dp": (x + d) % 4}, device_id_type=MESH)

    for el in range(4):
        blocks[el, 0] = gate_ref[el].T.astype(BF16)
        blocks[el, 1] = up_ref[el].T.astype(BF16)
        blocks[el, 2] = down_ref[el].astype(BF16)
    pl.semaphore_wait(barrier, 15 + 6 + away)

    def units(at):
        return stage.at[:, pl.ds(pl.multiple_of(at * FFB, 16), FFB), :]

    def block_out(el):
        return push(blocks.at[el], units(y), s_send.at[el], s_recv.at[y], partner(el))

    def block_in(el):
        return push(blocks.at[el], units(el), s_send.at[el], s_recv.at[el], partner(el))

    for el in range(4):

        @pl.when(remote(el))
        def _():
            block_out(el).start()

    xf = x_ref[...].astype(F32)
    scale = lax.rsqrt(jnp.mean(xf * xf, axis=-1, keepdims=True) + EPSILON)
    normed[...] = (xf * scale * gain_ref[...]).astype(BF16)
    half = 512

    def near(part, d):
        cols = pl.ds(part * half, half)
        device = y_at(z, y, d) if part == 0 else z_at(z, y, d)
        return lambda at: push(
            normed.at[:, cols],
            nall_ref.at[at // 4, at % 4, :, cols],
            n_send.at[part, 0, d],
            n_recv.at[part, 0, d],
            device,
        )

    def far(part, d):
        cols = pl.ds(part * half, half)
        if part == 0:
            return lambda at: push(
                nall_ref.at[z, :, :, cols],
                nall_ref.at[at // 4, :, :, cols],
                n_send.at[part, 1, d],
                n_recv.at[part, 1, d],
                z_at(z, y, d),
            )
        return lambda at: push(
            nall_ref.at[:, y, :, cols],
            nall_ref.at[:, at % 4, :, cols],
            n_send.at[part, 1, d],
            n_recv.at[part, 1, d],
            y_at(z, y, d),
        )

    y_from = [z * 4 + (y + 4 - d) % 4 for d in range(4)]
    z_from = [((z + 4 - d) % 4) * 4 + y for d in range(4)]

    wide = 512
    for i in range(6):
        part = dot(normed[...], wq_ref[:, i * wide : (i + 1) * wide])
        heads[i // 2, (i % 2) * 8 : (i % 2) * 8 + 8] = part.T.astype(BF16).reshape(8, 64, 128)

    def head_out(k):
        t = (m + k) % 16
        return push(
            heads.at[:, t],
            qkv_ref.at[:, :, lanes(m, 128)],
            a_send.at[k],
            a_recv.at[k],
            mp_at(m, k),
        )

    def head_in(k):
        return push(
            heads.at[:, 0],
            qkv_ref.at[:, :, lanes((m + 16 - k) % 16, 128)],
            a_send.at[k],
            a_recv.at[k],
            mp_at(m, k),
        )

    def each(lo, hi, f):
        def one(k, carry):
            f(k)
            return carry

        lax.fori_loop(lo, hi, one, 0)

    each(1, 16, lambda k: head_out(k).start())
    own = pltpu.make_async_copy(heads.at[:, m], qkv_ref.at[:, :, lanes(m, 128)], here.at[0])
    own.start()
    mine = pltpu.make_async_copy(normed, nall_ref.at[z, y], here.at[1])
    mine.start()
    for d in (2, 1, 3):
        near(0, d)(m).start()
        near(1, d)(m).start()

    @pl.when(away == 0)
    def _():
        kept = pltpu.make_async_copy(blocks.at[y], units(y), here.at[2])
        kept.start()
        kept.wait()

    for el in range(4):

        @pl.when(remote(el))
        def _():
            block_in(el).wait_recv()

    def fan(d, at):
        return push(
            stage.at[:2],
            w_out_ref.at[:, :, lanes(at, DB)],
            x_send.at[d],
            x_recv.at[d],
            {"dp": (x + d) % 4},
        )

    for d in (2, 1, 3):
        fan(d, x).start()
    stay = pltpu.make_async_copy(stage.at[:2], w_out_ref.at[:, :, lanes(x, DB)], here.at[3])
    stay.start()
    down_out_ref[...] = stage[2]

    own.wait()
    each(1, 16, lambda k: head_in(k).wait_recv())
    for d in (2, 1, 3):
        near(0, d)(y_from[d]).wait_recv()
        near(1, d)(z_from[d]).wait_recv()
    mine.wait()
    for d in (2, 1, 3):
        far(0, d)(m).start()
        far(1, d)(m).start()

    key_rows[...] = qkv_ref[1].astype(F32).T.astype(BF16)

    def ctx_out(t):
        return push(
            ctx_low.at[:, lanes(t, 128)],
            ctx_ref.at[pl.ds(pl.multiple_of(m * 64, 64), 64), :],
            c_send.at[(t + 16 - m) % 16],
            c_recv.at[(t + 16 - m) % 16],
            {"mp": t},
        )

    def ctx_in(k):
        s = (m + 16 - k) % 16
        return push(
            ctx_low.at[:, pl.ds(0, 128)],
            ctx_ref.at[pl.ds(pl.multiple_of(s * 64, 64), 64), :],
            c_send.at[k],
            c_recv.at[k],
            {"mp": s},
        )

    def queries(i):
        b = (m // 2 + i) % 8
        cols = lanes(b, 256)
        q = (qkv_ref[0, :, cols].astype(F32) * 0.125).astype(BF16)
        s = dot(key_rows[...], q)
        top = jnp.max(s, axis=0, keepdims=True)
        p = jnp.exp(s - top)
        total = jnp.sum(p, axis=0, keepdims=True)
        ctx = dot(qkv_ref[2], p.astype(BF16)) / total
        lse_ref[:, cols] = top + jnp.log(total)
        ctx_here_ref[:, cols] = ctx
        ctx_low[:, cols] = ctx.astype(BF16)

    def pair(i, carry):
        queries(2 * i)
        queries(2 * i + 1)
        for u in range(2):
            b = (m // 2 + 2 * i + u) % 8
            for v in range(2):
                t = 2 * b + v

                @pl.when(t != m)
                def _():
                    ctx_out(t).start()

        return carry

    lax.fori_loop(0, 4, pair, 0)
    ctx_ref[pl.ds(pl.multiple_of(m * 64, 64), 64), :] = ctx_low[:, lanes(m, 128)]
    each(1, 16, lambda k: ctx_in(k).wait_recv())

    for d in (1, 2, 3):
        far(0, d)(z_from[d]).wait_recv()
        far(1, d)(y_from[d]).wait_recv()
        fan(d, (x + 4 - d) % 4).wait_recv()
    for d in (1, 2, 3):
        near(0, d)(m).wait_send()
        near(1, d)(m).wait_send()
        far(0, d)(m).wait_send()
        far(1, d)(m).wait_send()
        fan(d, x).wait_send()
    stay.wait()
    each(1, 16, lambda k: head_out(k).wait_send())
    each(1, 16, lambda k: ctx_in(k).wait_send())
    for el in range(4):

        @pl.when(remote(el))
        def _():
            block_out(el).wait_send()


def attend(block_input, gain, qkv_low, gate_weight, up_weight, down_weight):
    dma = pltpu.SemaphoreType.DMA
    vm = pl.BlockSpec(memory_space=VMEM)
    hbm = pl.BlockSpec(memory_space=pl.ANY)
    shape = jax.ShapeDtypeStruct
    return pl.pallas_call(
        attend_kernel,
        out_shape=(
            shape((1024, 128), BF16),
            shape((3, 64, 2048), BF16),
            shape((64, 2048), F32),
            shape((1, 2048), F32),
            shape((4, 4, 128, 1024), BF16),
            shape((2, FFQ, 4 * DB), BF16),
            shape((FFQ, DB), BF16),
        ),
        in_specs=[vm] * 6,
        out_specs=(vm, vm, vm, vm, hbm, hbm, vm),
        scratch_shapes=[
            VMEM((128, 1024), BF16),
            VMEM((3, 16, 64, 128), BF16),
            VMEM((4, 3, FFB, DB), BF16),
            VMEM((3, FFQ, DB), BF16),
            VMEM((2048, 64), BF16),
            VMEM((64, 2048), BF16),
            dma((4,)),
            dma((4,)),
            dma((4,)),
            dma((4,)),
            dma((4,)),
            dma((16,)),
            dma((16,)),
            dma((2, 2, 4)),
            dma((2, 2, 4)),
            dma((16,)),
            dma((16,)),
        ],
        compiler_params=params(1, 60),
    )(block_input, gain.reshape(1, -1), qkv_low, gate_weight, up_weight, down_weight)


GELU_A = 0.7978845608
GELU_B = 0.044715


def moe_kernel(
    send_ref,
    w_ref,
    down_ref,
    ret_ref,
    grad_ref,
    recv,
    own_part,
    sib_send,
    sib_recv,
    back,
    xs,
    cs,
    hid,
    gcs,
    ucs,
    down,
    here,
    x_send,
    x_recv,
    d_send,
    d_recv,
    f_send,
    f_recv,
    p_send,
    p_recv,
    r_send,
    r_recv,
):
    x, c, m, z, y = spot()
    barrier = pltpu.get_barrier_semaphore()

    def greet(k, carry):
        pl.semaphore_signal(barrier, inc=1, device_id={"mp": (m + k) % 16}, device_id_type=MESH)
        return carry

    lax.fori_loop(1, 16, greet, 0)
    pl.semaphore_signal(barrier, inc=1, device_id={"expert": 1 - c}, device_id_type=MESH)
    for d in range(1, 4):
        pl.semaphore_signal(barrier, inc=1, device_id={"dp": (x + d) % 4}, device_id_type=MESH)
    pl.semaphore_wait(barrier, 19)

    def fan(d, at):
        return push(
            down_ref, down.at[:, lanes(at, DB)], x_send.at[d], x_recv.at[d], {"dp": (x + d) % 4}
        )

    for d in (2, 1, 3):
        fan(d, x).start()
    stay = pltpu.make_async_copy(down_ref, down.at[:, lanes(x, DB)], here.at[0])
    stay.start()

    def expert_of(t):
        return ((t // 4) % 2) * 4 + t % 4

    def dispatch(k):
        t = (m + k) % 16
        return pltpu.make_async_remote_copy(
            src_ref=send_ref.at[expert_of(t)],
            dst_ref=recv.at[0, k],
            send_sem=d_send.at[k],
            recv_sem=d_recv.at[k],
            device_id={"mp": t},
            device_id_type=MESH,
        )

    def forward(k):
        return pltpu.make_async_remote_copy(
            src_ref=recv.at[0, k],
            dst_ref=recv.at[1, k],
            send_sem=f_send.at[k],
            recv_sem=f_recv.at[k],
            device_id={"expert": 1 - c},
            device_id_type=MESH,
        )

    def partials(j):
        return pltpu.make_async_remote_copy(
            src_ref=sib_send.at[j],
            dst_ref=sib_recv.at[j],
            send_sem=p_send.at[j],
            recv_sem=p_recv.at[j],
            device_id={"expert": 1 - c},
            device_id_type=MESH,
        )

    def giving(k):
        return pltpu.make_async_remote_copy(
            src_ref=back.at[k],
            dst_ref=ret_ref.at[m],
            send_sem=r_send.at[k],
            recv_sem=r_recv.at[k],
            device_id={"mp": (m + 16 - k) % 16},
            device_id_type=MESH,
        )

    def start_dispatch(k, carry):
        dispatch(k).start()
        return carry

    lax.fori_loop(1, 16, start_dispatch, 0)
    recv[0, 0] = send_ref[expert_of(m)]

    def finish(j):
        partials(j).wait_recv()
        back[pl.ds(4 * j, 4)] = (own_part[...] + sib_recv[j].astype(F32)).astype(BF16)
        for i in range(4):
            k = 4 * j + i

            @pl.when(k > 0)
            def _():
                giving(k).start()

            @pl.when(k == 0)
            def _():
                ret_ref[m] = back[0]

    def chunk(j, carry):
        for i in range(4):
            k = 4 * j + i

            @pl.when(k > 0)
            def _():
                dispatch(k).wait_recv()

            forward(k).start()

        @pl.when(j > 0)
        def _():
            finish(j - 1)

        for i in range(4):
            forward(4 * j + i).wait_recv()
        blk = recv[:, pl.ds(4 * j, 4)].astype(F32)
        span = pl.ds(pl.multiple_of(j * 8 * ROWS, 16), 8 * ROWS)
        xs[span] = blk[:, :, :ROWS].reshape(8 * ROWS, 4 * DB).astype(BF16)
        cs[span] = blk[:, :, ROWS:].reshape(8 * ROWS, 4 * DB).astype(BF16)
        gate = dot_nt(xs[span], w_ref[0])
        up = dot_nt(xs[span], w_ref[1])
        hid_cot = dot_nt(cs[span], down[...])
        sq = gate * gate
        th = jnp.tanh(GELU_A * (gate + GELU_B * (gate * sq)))
        half = 0.5 * (1.0 + th)
        act = gate * half
        slope = half + 0.5 * gate * (1.0 - th * th) * (GELU_A * (1.0 + 3.0 * GELU_B * sq))
        hid[span] = (act * up).astype(BF16)
        gcs[span] = (hid_cot * up * slope).astype(BF16)
        ucs[span] = (hid_cot * act).astype(BF16)
        out = dot(hid[span], down[...]).reshape(2, 4, ROWS, 4 * DB)
        rows = (dot(gcs[span], w_ref[0]) + dot(ucs[span], w_ref[1])).reshape(2, 4, ROWS, 4 * DB)
        own_part[:, :ROWS] = out[0]
        own_part[:, ROWS:] = rows[0]
        sib_send[j] = jnp.concatenate([out[1], rows[1]], axis=1).astype(BF16)
        partials(j).start()
        return carry

    stay.wait()
    for d in (1, 2, 3):
        fan(d, (x + 4 - d) % 4).wait_recv()
    lax.fori_loop(0, 4, chunk, 0)
    finish(3)
    for i, (a, b) in enumerate(((gcs, xs), (ucs, xs), (hid, cs))):
        g = dot_tn(a[...], b[...])
        for at in range(4):
            grad_ref[at, i] = g[:, at * DB : (at + 1) * DB].astype(BF16)

    def drain(k, carry):
        pltpu.make_async_remote_copy(
            src_ref=back.at[k],
            dst_ref=ret_ref.at[(m + k) % 16],
            send_sem=r_send.at[k],
            recv_sem=r_recv.at[k],
            device_id={"mp": (m + 16 - k) % 16},
            device_id_type=MESH,
        ).wait()
        dispatch(k).wait_send()
        forward(k).wait_send()
        return carry

    lax.fori_loop(1, 16, drain, 0)
    forward(0).wait_send()
    for d in (1, 2, 3):
        fan(d, x).wait_send()
    for j in range(4):
        partials(j).wait_send()


def moe(send, weights, down):
    dma = pltpu.SemaphoreType.DMA
    block = (2 * ROWS, 4 * DB)
    return pl.pallas_call(
        moe_kernel,
        out_shape=(
            jax.ShapeDtypeStruct((16, *block), BF16),
            jax.ShapeDtypeStruct((4, 3, FFQ, DB), BF16),
        ),
        in_specs=[pl.BlockSpec(memory_space=VMEM)] * 3,
        out_specs=(pl.BlockSpec(memory_space=VMEM),) * 2,
        scratch_shapes=[
            VMEM((2, 16, *block), BF16),
            VMEM((4, *block), F32),
            VMEM((4, 4, *block), BF16),
            VMEM((4, 4, *block), BF16),
            VMEM((16, *block), BF16),
            VMEM((32 * ROWS, 4 * DB), BF16),
            VMEM((32 * ROWS, 4 * DB), BF16),
            VMEM((32 * ROWS, FFQ), BF16),
            VMEM((32 * ROWS, FFQ), BF16),
            VMEM((32 * ROWS, FFQ), BF16),
            VMEM((FFQ, 4 * DB), BF16),
            dma((1,)),
            dma((4,)),
            dma((4,)),
            dma((16,)),
            dma((16,)),
            dma((16,)),
            dma((16,)),
            dma((4,)),
            dma((4,)),
            dma((16,)),
            dma((16,)),
        ],
        compiler_params=params(3, 62),
    )(send, weights, down)


def attend_back_kernel(
    dctx_ref,
    qkv_ref,
    ctx_ref,
    lse_ref,
    nall_ref,
    wq_ref,
    x_ref,
    gain_ref,
    mid_ref,
    o_ref,
    few_ref,
    g_ref,
    in_ref,
    gain_out_ref,
    full_ref,
    g_out_ref,
    o_out_ref,
    few_out_ref,
    o_sib,
    o_half,
    o_mp,
    o_quarter,
    o_dp,
    few_mp,
    few_sum,
    few_rest,
    cot,
    key_rows,
    value_rows,
    row_dot,
    dk,
    dv,
    pc_here,
    pc_tok,
    slices,
    parts,
    g_in,
    g_sum,
    gain_row,
    gain_mp,
    gain_rest,
    here,
    a_send,
    a_recv,
    b_send,
    b_recv,
    q_send,
    q_recv,
    f_send,
    f_recv,
    t_send,
    t_recv,
    x_send,
    x_recv,
    s_send,
    s_recv,
    u_send,
    u_recv,
    v_send,
    v_recv,
    o_send,
    o_recv,
    om_send,
    om_recv,
    og_send,
    og_recv,
    ox_send,
    ox_recv,
    fm_send,
    fm_recv,
    fr_send,
    fr_recv,
):
    x, c, m, z, y = spot()
    pc, pz = swapped(c, z)
    away = (pc - c) * (pc - c)
    barrier = pltpu.get_barrier_semaphore()

    def remote(el):
        return (away == 1) | (el != y)

    def partner(el):
        return {"expert": pc, "mp": pz * 4 + el}

    def rest(r):
        return {"dp": (x + r % 4) % 4, "expert": (c + r // 4) % 2}

    def each(lo, hi, f):
        def one(k, carry):
            f(k)
            return carry

        lax.fori_loop(lo, hi, one, 0)

    greet_mp(barrier, m)
    for el in range(4):

        @pl.when(remote(el))
        def _():
            pl.semaphore_signal(barrier, inc=1, device_id=partner(el), device_id_type=MESH)

    for r in range(1, 8):
        pl.semaphore_signal(barrier, inc=1, device_id=rest(r), device_id_type=MESH)
    pl.semaphore_wait(barrier, 15 + 3 + away + 7)

    def cot_out(k):
        t = (m + k) % 16
        return push(dctx_ref.at[t], cot.at[:, lanes(m, 128)], a_send.at[k], a_recv.at[k], {"mp": t})

    def cot_in(k):
        s = (m + 16 - k) % 16
        return push(dctx_ref.at[0], cot.at[:, lanes(s, 128)], a_send.at[k], a_recv.at[k], {"mp": s})

    each(1, 16, lambda k: cot_out(k).start())
    cot[:, lanes(m, 128)] = dctx_ref[m]

    def fan(d):
        t = (x + d) % 4
        return push(g_ref.at[t], g_in.at[d], x_send.at[d], x_recv.at[d], {"dp": t})

    for d in (2, 1, 3):
        fan(d).start()
    keep = pltpu.make_async_copy(g_ref.at[x], g_in.at[0], here.at[0])
    keep.start()

    def halves():
        return push(
            o_ref.at[1 - c], o_sib, o_send.at[0], o_recv.at[0], {"expert": 1 - c}
        )

    def thirty(k):
        t = (m + k) % 16
        return push(o_half.at[t], o_mp.at[k], om_send.at[k], om_recv.at[k], {"mp": t})

    def quarters(d):
        t = (x + d) % 4
        return push(
            o_quarter.at[:, lanes(t, DB)], o_dp.at[d], ox_send.at[0, d], ox_recv.at[0, d], {"dp": t}
        )

    def regain(d, at):
        return push(
            o_out_ref.at[c, m, :, lanes(x, DB)],
            o_out_ref.at[c, m, :, lanes(at, DB)],
            ox_send.at[1, d],
            ox_recv.at[1, d],
            {"dp": (x + d) % 4},
        )

    def regather(k, at):
        return push(
            o_out_ref.at[c, m], o_out_ref.at[c, at], og_send.at[k], og_recv.at[k], mp_at(m, k)
        )

    def retwin(core):
        return push(
            o_out_ref.at[core], o_out_ref.at[core], o_send.at[1], o_recv.at[1], {"expert": 1 - c}
        )

    def few_near(k):
        return push(few_ref, few_mp.at[k], fm_send.at[k], fm_recv.at[k], mp_at(m, k))

    def few_far(r):
        return push(few_sum, few_rest.at[r], fr_send.at[r], fr_recv.at[r], rest(r))

    halves().start()
    key_rows[...] = qkv_ref[1].astype(F32).T.astype(BF16)
    value_rows[...] = qkv_ref[2].astype(F32).T.astype(BF16)
    dk[...] = jnp.zeros_like(dk)
    dv[...] = jnp.zeros_like(dv)
    each(1, 16, lambda k: cot_in(k).wait_recv())
    row_dot[...] = jnp.sum(cot[...].astype(F32) * ctx_ref[...], axis=0, keepdims=True)

    def queries(b):
        cols = lanes(b, 256)
        q = (qkv_ref[0, :, cols].astype(F32) * 0.125).astype(BF16)
        p = jnp.exp(dot(key_rows[...], q) - lse_ref[:, cols])
        dp = dot(value_rows[...], cot[:, cols])
        ds = (p * (dp - row_dot[:, cols])).astype(BF16)
        pc_here[0, :, cols] = (dot(qkv_ref[1], ds) * 0.125).astype(BF16)
        dk[...] += dot_nt(ds, q)
        dv[...] += dot_nt(p.astype(BF16), cot[:, cols])

    def pair(i, carry):
        queries(2 * i)
        queries(2 * i + 1)
        return carry

    pair(0, 0)
    halves().wait_recv()
    o_half[...] = (o_ref[c].astype(F32) + o_sib[...].astype(F32)).astype(BF16)
    each(1, 16, lambda k: thirty(k).start())
    each(1, 16, lambda k: few_near(k).start())
    lax.fori_loop(1, 4, pair, 0)
    pc_here[1] = dk[...].T.astype(BF16)
    pc_here[2] = dv[...].T.astype(BF16)

    def pc_out(k):
        t = (m + k) % 16
        return push(
            pc_here.at[:, :, lanes(t, 128)], pc_tok.at[:, m], b_send.at[k], b_recv.at[k], {"mp": t}
        )

    def pc_in(k):
        s = (m + 16 - k) % 16
        return push(
            pc_here.at[:, :, pl.ds(0, 128)], pc_tok.at[:, s], b_send.at[k], b_recv.at[k], {"mp": s}
        )

    each(1, 16, lambda k: pc_out(k).start())
    pc_tok[:, m] = pc_here[:, :, lanes(m, 128)]

    each(1, 16, lambda k: thirty(k).wait_recv())
    o_sum = o_half[m].astype(F32)
    for k in range(1, 16):
        o_sum += o_mp[k].astype(F32)
    o_quarter[...] = o_sum.astype(BF16)
    for d in (2, 1, 3):
        quarters(d).start()
    each(1, 16, lambda k: few_near(k).wait_recv())
    few_all = few_ref[...].astype(F32)
    for k in range(1, 16):
        few_all += few_mp[k].astype(F32)
    few_sum[...] = few_all.astype(BF16)
    for r in range(1, 8):
        few_far(r).start()

    slices[...] = dot(pc_here[...].reshape(192, 2048), nall_ref[...]).astype(BF16)

    def share_out(r):
        t = 2 * ((x + r % 4) % 4) + (c + r // 4) % 2
        return push(slices.at[:, lanes(t, 128)], parts.at[r], q_send.at[r], q_recv.at[r], rest(r))

    for r in range(1, 8):
        share_out(r).start()
    for d in (1, 2, 3):
        quarters(d).wait_recv()
    o_fin = o_quarter[:, lanes(x, DB)].astype(F32)
    for d in (1, 2, 3):
        o_fin += o_dp[d].astype(F32)
    o_out_ref[c, m, :, lanes(x, DB)] = o_fin.astype(BF16)
    for d in (2, 1, 3):
        regain(d, x).start()
    total = slices[:, lanes(2 * x + c, 128)].astype(F32)
    for r in range(1, 8):
        share_out(r).wait_recv()
    for r in range(1, 8):
        total += parts[r].astype(F32)
    full_ref[:, c, x, z, y] = total.astype(BF16).reshape(3, 64, 128)

    def along(axis, d):
        if axis == 0:
            return {"dp": (x + d) % 4}
        return z_at(z, y, d) if axis == 1 else y_at(z, y, d)

    orders = ((0, 2, 1), (2, 1, 0), (1, 0, 2))

    def spread(p, s, d, back):
        at = [x, z, y]
        axis = orders[p][s]
        if back:
            at[axis] = (at[axis] + 4 - d) % 4
        for done in orders[p][:s]:
            at[done] = slice(None)
        src = [x, z, y]
        for done in orders[p][:s]:
            src[done] = slice(None)
        return push(
            full_ref.at[(p, c, *src)],
            full_ref.at[(p, c, *at)],
            f_send.at[p, s, d],
            f_recv.at[p, s, d],
            along(axis, d),
        )

    def twin(p, back):
        core = 1 - c if back else c
        return push(
            full_ref.at[p, core],
            full_ref.at[p, core],
            t_send.at[p],
            t_recv.at[p],
            {"expert": 1 - c},
        )

    for p in range(3):
        for d in (2, 1, 3):
            spread(p, 0, d, False).start()

    each(1, 16, lambda k: pc_in(k).wait_recv())
    dn = dot(wq_ref[...], pc_tok[...].reshape(3072, 128)).T
    xf = x_ref[...].astype(F32)
    scale = lax.rsqrt(jnp.mean(xf * xf, axis=-1, keepdims=True) + EPSILON)
    hat = xf * scale
    gained = dn * gain_ref[...]
    in_ref[...] = mid_ref[...] + scale * (
        gained - hat * jnp.mean(gained * hat, axis=-1, keepdims=True)
    )
    gain_row[...] = jnp.sum(dn * hat, axis=0, keepdims=True)

    def gain_out(k):
        return push(gain_row, gain_mp.at[k], u_send.at[k], u_recv.at[k], mp_at(m, k))

    def gain_far(r):
        return push(gain_mp.at[0], gain_rest.at[r], v_send.at[r], v_recv.at[r], rest(r))

    each(1, 16, lambda k: gain_out(k).start())
    for d in (1, 2, 3):
        regain(d, (x + 4 - d) % 4).wait_recv()
    each(1, 16, lambda k: regather(k, m).start())
    for r in range(1, 8):
        few_far(r).wait_recv()
        few_all += few_rest[r].astype(F32)
    few_out_ref[...] = few_all

    for p in range(3):
        for d in (1, 2, 3):
            spread(p, 0, d, True).wait_recv()
    for p in range(3):
        for d in (2, 1, 3):
            spread(p, 1, d, False).start()

    each(1, 16, lambda k: gain_out(k).wait_recv())
    got = gain_row[...]
    for k in range(1, 16):
        got += gain_mp[k]
    gain_mp[0] = got
    for r in range(1, 8):
        gain_far(r).start()

    for p in range(3):
        for d in (1, 2, 3):
            spread(p, 1, d, True).wait_recv()
    for p in range(3):
        for d in (2, 1, 3):
            spread(p, 2, d, False).start()

    keep.wait()
    for d in (1, 2, 3):
        fan(d).wait_recv()
    for i in range(3):
        g_sum[i] = (
            g_in[0, i].astype(F32)
            + g_in[1, i].astype(F32)
            + g_in[2, i].astype(F32)
            + g_in[3, i].astype(F32)
        ).astype(BF16)

    def home_out(at):
        return push(
            g_sum.at[:, pl.ds(at * FFB, FFB), :],
            g_out_ref.at[y],
            s_send.at[at],
            s_recv.at[y],
            partner(at),
        )

    def home_in(at):
        return push(
            g_sum.at[:, pl.ds(at * FFB, FFB), :],
            g_out_ref.at[at],
            s_send.at[at],
            s_recv.at[at],
            partner(at),
        )

    for at in range(4):

        @pl.when(remote(at))
        def _():
            home_out(at).start()

    @pl.when(away == 0)
    def _():
        kept = pltpu.make_async_copy(
            g_sum.at[:, pl.ds(pl.multiple_of(y * FFB, 16), FFB), :], g_out_ref.at[y], here.at[1]
        )
        kept.start()
        kept.wait()

    each(1, 16, lambda k: regather(k, (m + 16 - k) % 16).wait_recv())
    retwin(c).start()
    for r in range(1, 8):
        gain_far(r).wait_recv()
    for r in range(1, 8):
        got += gain_rest[r]
    gain_out_ref[...] = got

    for p in range(3):
        for d in (1, 2, 3):
            spread(p, 2, d, True).wait_recv()
        twin(p, False).start()
    for at in range(4):

        @pl.when(remote(at))
        def _():
            home_in(at).wait_recv()

    retwin(1 - c).wait_recv()
    for p in range(3):
        twin(p, True).wait_recv()
    for p in range(3):
        twin(p, False).wait_send()
        for s in range(3):
            for d in (1, 2, 3):
                spread(p, s, d, False).wait_send()
    halves().wait_send()
    retwin(c).wait_send()
    each(1, 16, lambda k: thirty(k).wait_send())
    each(1, 16, lambda k: regather(k, m).wait_send())
    each(1, 16, lambda k: few_near(k).wait_send())
    for d in (1, 2, 3):
        quarters(d).wait_send()
        regain(d, x).wait_send()
    for r in range(1, 8):
        few_far(r).wait_send()
    each(1, 16, lambda k: cot_out(k).wait_send())
    each(1, 16, lambda k: pc_out(k).wait_send())
    each(1, 16, lambda k: gain_out(k).wait_send())
    for d in (1, 2, 3):
        fan(d).wait_send()
    for r in range(1, 8):
        share_out(r).wait_send()
        gain_far(r).wait_send()
    for at in range(4):

        @pl.when(remote(at))
        def _():
            home_out(at).wait_send()


def attend_back(
    dctx, qkv, ctx, lse, nall, qkv_low, block_input, gain, middle_cot, out_term, few, grads
):
    dma = pltpu.SemaphoreType.DMA
    vm = pl.BlockSpec(memory_space=VMEM)
    hbm = pl.BlockSpec(memory_space=pl.ANY)
    shape = jax.ShapeDtypeStruct
    return pl.pallas_call(
        attend_back_kernel,
        out_shape=(
            shape((128, 1024), F32),
            shape((1, 1024), F32),
            shape((3, 2, 4, 4, 4, 64, 128), BF16),
            shape((4, 3, FFB, DB), BF16),
            shape((2, 16, 32, 1024), BF16),
            shape((16, 1024), F32),
        ),
        in_specs=[vm] * 11 + [hbm],
        out_specs=(vm,) * 6,
        scratch_shapes=[
            VMEM((16, 32, 1024), BF16),
            VMEM((16, 32, 1024), BF16),
            VMEM((16, 32, 1024), BF16),
            VMEM((32, 1024), BF16),
            VMEM((4, 32, DB), BF16),
            VMEM((16, 16, 1024), BF16),
            VMEM((16, 1024), BF16),
            VMEM((8, 16, 1024), BF16),
            VMEM((64, 2048), BF16),
            VMEM((2048, 64), BF16),
            VMEM((2048, 64), BF16),
            VMEM((1, 2048), F32),
            VMEM((2048, 64), F32),
            VMEM((2048, 64), F32),
            VMEM((3, 64, 2048), BF16),
            VMEM((3, 16, 64, 128), BF16),
            VMEM((192, 1024), BF16),
            VMEM((8, 192, 128), BF16),
            VMEM((4, 3, FFQ, DB), BF16),
            VMEM((3, FFQ, DB), BF16),
            VMEM((1, 1024), F32),
            VMEM((16, 1, 1024), F32),
            VMEM((8, 1, 1024), F32),
            dma((2,)),
            dma((16,)),
            dma((16,)),
            dma((16,)),
            dma((16,)),
            dma((8,)),
            dma((8,)),
            dma((3, 3, 4)),
            dma((3, 3, 4)),
            dma((3,)),
            dma((3,)),
            dma((4,)),
            dma((4,)),
            dma((4,)),
            dma((4,)),
            dma((16,)),
            dma((16,)),
            dma((8,)),
            dma((8,)),
            dma((2,)),
            dma((2,)),
            dma((16,)),
            dma((16,)),
            dma((16,)),
            dma((16,)),
            dma((2, 4)),
            dma((2, 4)),
            dma((16,)),
            dma((16,)),
            dma((8,)),
            dma((8,)),
        ],
        compiler_params=params(2, 60),
    )(
        dctx,
        qkv,
        ctx,
        lse,
        nall.reshape(2048, 1024),
        qkv_low,
        block_input,
        gain.reshape(1, -1),
        middle_cot,
        out_term,
        few,
        grads,
    )


def unfold_kernel(g_ref, o_ref):
    o_ref[...] = g_ref[...].reshape(3072, 128).astype(F32).T


def unfold(full):
    return pl.pallas_call(
        unfold_kernel,
        out_shape=jax.ShapeDtypeStruct((1024, 3072), F32),
        grid=(4, 2),
        in_specs=[
            pl.BlockSpec((3, None, None, 4, 4, 64, 128), lambda i, j: (0, j, i, 0, 0, 0, 0)),
        ],
        out_specs=pl.BlockSpec((128, 3072), lambda i, j: (2 * i + j, 0)),
        compiler_params=pltpu.CompilerParams(vmem_limit_bytes=32 * 1024 * 1024),
    )(full)


def rms_norm(values, gain):
    return values * lax.rsqrt(jnp.mean(values * values, axis=-1, keepdims=True) + EPSILON) * gain


def gating(moe_in, router_weight, routes):
    logits = jnp.dot(moe_in, router_weight, precision=HIGHEST, preferred_element_type=F32)
    probs = jax.nn.softmax(logits, axis=-1)
    onehot = (routes[:, :, None] == jnp.arange(8, dtype=routes.dtype)).astype(F32)
    chosen = jnp.sum(probs[:, None, :] * onehot, axis=2)
    return chosen / jnp.sum(chosen, axis=1, keepdims=True)


def body(
    block_input,
    attn_gain,
    qkv_weight,
    out_weight,
    moe_gain,
    router_weight,
    gate_weight,
    up_weight,
    down_weight,
    routes,
    slot_index,
    cotangent,
):
    tok_rows, width = block_input.shape
    inputs = block_input.astype(F32)
    qkv_low = qkv_weight.astype(BF16)
    out_low = out_weight.astype(BF16)
    ctx_tok, qkv, ctx_here, lse, nall, weights, down = attend(
        block_input, attn_gain, qkv_low, gate_weight, up_weight, down_weight
    )
    context = ctx_tok.T
    middle = inputs + dot(context, out_low)
    moe_in, moe_back = jax.vjp(rms_norm, middle, moe_gain)
    gates, gate_back = jax.vjp(partial(gating, routes=routes), moe_in, router_weight)
    valid = slot_index < ROWS
    place = routes * (2 * ROWS) + slot_index
    keep = valid.astype(F32)
    upstream = cotangent.astype(F32)
    pair_rows = jnp.repeat(moe_in.astype(BF16), 2, axis=0)
    pair_cots = (gates[:, :, None] * upstream[:, None, :]).astype(BF16).reshape(2 * tok_rows, width)
    target = jnp.where(valid, place, 16 * ROWS).reshape(-1)
    cot_target = jnp.where(valid, place + ROWS, 16 * ROWS).reshape(-1)
    send = jnp.zeros((16 * ROWS, width), BF16)
    send = send.at[target].set(pair_rows, mode="drop").at[cot_target].set(pair_cots, mode="drop")
    returned, grads = moe(send.reshape(8, 2 * ROWS, width), weights, down)
    returned = returned.reshape(2, 8 * 2 * ROWS, width).astype(F32)
    returned = (returned[0] + returned[1]).astype(BF16)
    fetch_at = jnp.where(valid, place, 0)
    fetched = jnp.take(returned, fetch_at, axis=0).astype(F32) * keep[:, :, None]
    block_output = (middle + jnp.sum(gates[:, :, None] * fetched, axis=1)).astype(BF16)
    gate_cot = jnp.sum(upstream[:, None, :] * fetched, axis=2)
    moe_cot = jnp.sum(
        jnp.take(returned, fetch_at + ROWS, axis=0).astype(F32) * keep[:, :, None], axis=1
    )
    router_in_cot, router_term = gate_back(gate_cot)
    middle_norm_cot, moe_gain_term = moe_back(moe_cot + router_in_cot)
    middle_cot = upstream + middle_norm_cot
    branch_cot = middle_cot.astype(BF16)
    out_term = dot(ctx_tok, branch_cot)
    context_cot = dot_nt(out_low, branch_cot).astype(BF16).reshape(HEADS, 64, tok_rows)
    few = jnp.concatenate([router_term.T, moe_gain_term[None], jnp.zeros((7, width), F32)], axis=0)
    input_grad, gain_grad, full, mine, out_grad, few = attend_back(
        context_cot,
        qkv,
        ctx_here,
        lse,
        nall,
        qkv_low,
        block_input,
        attn_gain,
        middle_cot,
        out_term.astype(BF16).reshape(2, 16, 32, width),
        few.astype(BF16),
        grads,
    )
    mine = mine.astype(F32)
    return (
        block_output,
        input_grad,
        gain_grad.reshape(-1),
        unfold(full),
        out_grad.reshape(width, width).astype(F32),
        few[8],
        few[:8].T,
        jnp.swapaxes(mine[:, 0], 1, 2),
        jnp.swapaxes(mine[:, 1], 1, 2),
        mine[:, 2],
    )


def solution(mesh):
    tokens = P(("dp", "expert", "mp"), None)
    cols = P("expert", "dp", "mp")
    rows = P("expert", "mp", "dp")
    return jax.shard_map(
        body,
        mesh=mesh,
        in_specs=(tokens, P(), P(), P(), P(), P(), cols, cols, rows, tokens, tokens, tokens),
        out_specs=(tokens, tokens, P(), P(), P(), P(), P(), cols, cols, rows),
        check_vma=False,
    )
```

```python
import jax
import jax.numpy as jnp
from jax import lax
from jax.experimental import pallas as pl
from jax.experimental.pallas import tpu as pltpu
from jax.sharding import PartitionSpec as P

EPSILON = 1e-06
HIGHEST = lax.Precision.HIGHEST
MESH = pl.DeviceIdType.MESH
F32 = jnp.float32
BF16 = jnp.bfloat16
VMEM = pltpu.VMEM
ROWS = 40
FFB = 176
FFQ = 704
DB = 256
NT = (((1,), (1,)), ((), ()))
TN = (((0,), (0,)), ((), ()))


def dot(a, b):
    return jnp.dot(a, b, preferred_element_type=F32)


def dot_nt(a, b):
    return lax.dot_general(a, b, NT, preferred_element_type=F32)


def dot_tn(a, b):
    return lax.dot_general(a, b, TN, preferred_element_type=F32)


def spot():
    m = lax.axis_index("mp")
    return lax.axis_index("dp"), lax.axis_index("expert"), m, m // 4, m % 4


def params(cid, mb=60):
    return pltpu.CompilerParams(
        collective_id=cid, has_side_effects=True, vmem_limit_bytes=mb * 1024 * 1024
    )


def swapped(c, z):
    return z % 2, 2 * (z // 2) + c


def mp_at(m, k):
    return {"mp": (m + k) % 16}


def y_at(z, y, d):
    return {"mp": z * 4 + (y + d) % 4}


def z_at(z, y, d):
    return {"mp": ((z + d) % 4) * 4 + y}


def push(src, dst, send, recv, device):
    return pltpu.make_async_remote_copy(
        src_ref=src, dst_ref=dst, send_sem=send, recv_sem=recv, device_id=device, device_id_type=MESH
    )


def lanes(at, size):
    return pl.ds(pl.multiple_of(at * size, size), size)


def greet_mp(barrier, m):
    def one(k, carry):
        pl.semaphore_signal(barrier, inc=1, device_id=mp_at(m, k), device_id_type=MESH)
        return carry

    lax.fori_loop(1, 16, one, 0)


def places(routes, slots):
    return jnp.where(slots < ROWS, routes * (2 * ROWS) + slots, -1.0)


def picks(columns):
    lane = lax.broadcasted_iota(jnp.int32, (128, 8), 1).astype(F32)
    return [(columns[:, j : j + 1] == lane).astype(F32) for j in range(2)]


def gates_of(probs, hot):
    chosen = [jnp.sum(probs * h, axis=1, keepdims=True) for h in hot]
    total = chosen[0] + chosen[1]
    return [v / total for v in chosen], total


def exact(a, b, dims):
    return lax.dot_general(a, b, dims, precision=HIGHEST, preferred_element_type=F32)


def unit(v):
    scale = lax.rsqrt(jnp.mean(v * v, axis=-1, keepdims=True) + EPSILON)
    return v * scale, scale


def attend_kernel(
    x_ref,
    gain_ref,
    gate_ref,
    up_ref,
    down_ref,
    moe_gain_ref,
    router_ref,
    pairs_ref,
    cot_ref,
    wq_hbm,
    wo_hbm,
    send_ref,
    mid_ref,
    probs_ref,
    ctx_ref,
    qkv_ref,
    ctx_here_ref,
    lse_ref,
    down_out_ref,
    nall_ref,
    w_out_ref,
    wq_out_ref,
    wo_out_ref,
    wq_wide,
    wo_wide,
    wq_ref,
    wo_ref,
    normed,
    heads,
    blocks,
    stage,
    key_rows,
    ctx_low,
    here,
    s_send,
    s_recv,
    x_send,
    x_recv,
    a_send,
    a_recv,
    n_send,
    n_recv,
    c_send,
    c_recv,
):
    x, c, m, z, y = spot()
    pc, pz = swapped(c, z)
    away = (pc - c) * (pc - c)
    barrier = pltpu.get_barrier_semaphore()

    def remote(el):
        return (away == 1) | (el != y)

    def partner(el):
        return {"expert": pc, "mp": pz * 4 + el}

    greet_mp(barrier, m)
    for el in range(4):

        @pl.when(remote(el))
        def _():
            pl.semaphore_signal(barrier, inc=1, device_id=partner(el), device_id_type=MESH)

    for d in range(1, 4):
        pl.semaphore_signal(barrier, inc=1, device_id={"dp": (x + d) % 4}, device_id_type=MESH)

    wide = 512

    def load(i):
        cols = pl.ds(i * wide, wide)
        return pltpu.make_async_copy(wq_hbm.at[:, cols], wq_wide.at[:, cols], here.at[4 + i])

    def save(i):
        cols = pl.ds(i * wide, wide)
        return pltpu.make_async_copy(wq_ref.at[:, cols], wq_out_ref.at[:, cols], here.at[4 + i])

    load_o = pltpu.make_async_copy(wo_hbm, wo_wide, here.at[10])
    save_o = pltpu.make_async_copy(wo_ref, wo_out_ref, here.at[10])
    for i in range(6):
        load(i).start()
    load_o.start()
    for el in range(4):
        blocks[el, 0] = gate_ref[el].astype(BF16)
        blocks[el, 1] = up_ref[el].astype(BF16)
        blocks[el, 2] = down_ref[el].astype(BF16)
    pl.semaphore_wait(barrier, 15 + 6 + away)

    def units(at):
        return stage.at[:, pl.ds(pl.multiple_of(at * FFB, 16), FFB), :]

    def block_out(el):
        return push(blocks.at[el], units(y), s_send.at[el], s_recv.at[y], partner(el))

    def block_in(el):
        return push(blocks.at[el], units(el), s_send.at[el], s_recv.at[el], partner(el))

    for el in range(4):

        @pl.when(remote(el))
        def _():
            block_out(el).start()

    normed[...] = (unit(x_ref[...].astype(F32))[0] * gain_ref[...]).astype(BF16)
    half = 512

    def near(part, d):
        cols = pl.ds(part * half, half)
        device = y_at(z, y, d) if part == 0 else z_at(z, y, d)
        return lambda at: push(
            normed.at[:, cols],
            nall_ref.at[at // 4, at % 4, :, cols],
            n_send.at[part, 0, d],
            n_recv.at[part, 0, d],
            device,
        )

    def far(part, d):
        cols = pl.ds(part * half, half)
        if part == 0:
            return lambda at: push(
                nall_ref.at[z, :, :, cols],
                nall_ref.at[at // 4, :, :, cols],
                n_send.at[part, 1, d],
                n_recv.at[part, 1, d],
                z_at(z, y, d),
            )
        return lambda at: push(
            nall_ref.at[:, y, :, cols],
            nall_ref.at[:, at % 4, :, cols],
            n_send.at[part, 1, d],
            n_recv.at[part, 1, d],
            y_at(z, y, d),
        )

    y_from = [z * 4 + (y + 4 - d) % 4 for d in range(4)]
    z_from = [((z + 4 - d) % 4) * 4 + y for d in range(4)]

    for i in range(6):
        load(i).wait()
        cols = slice(i * wide, (i + 1) * wide)
        wq_ref[:, cols] = wq_wide[:, cols].astype(BF16)
        save(i).start()
        part = dot(normed[...], wq_ref[:, cols])
        heads[i // 2, (i % 2) * 8 : (i % 2) * 8 + 8] = part.T.astype(BF16).reshape(8, 64, 128)

    def head_out(k):
        t = (m + k) % 16
        return push(
            heads.at[:, t],
            qkv_ref.at[:, :, lanes(m, 128)],
            a_send.at[k],
            a_recv.at[k],
            mp_at(m, k),
        )

    def head_in(k):
        return push(
            heads.at[:, 0],
            qkv_ref.at[:, :, lanes((m + 16 - k) % 16, 128)],
            a_send.at[k],
            a_recv.at[k],
            mp_at(m, k),
        )

    def each(lo, hi, f):
        def one(k, carry):
            f(k)
            return carry

        lax.fori_loop(lo, hi, one, 0)

    each(1, 16, lambda k: head_out(k).start())
    own = pltpu.make_async_copy(heads.at[:, m], qkv_ref.at[:, :, lanes(m, 128)], here.at[0])
    own.start()
    mine = pltpu.make_async_copy(normed, nall_ref.at[z, y], here.at[1])
    mine.start()
    for d in (2, 1, 3):
        near(0, d)(m).start()
        near(1, d)(m).start()

    @pl.when(away == 0)
    def _():
        kept = pltpu.make_async_copy(blocks.at[y], units(y), here.at[2])
        kept.start()
        kept.wait()

    for el in range(4):

        @pl.when(remote(el))
        def _():
            block_in(el).wait_recv()

    def fan(d, at):
        return push(
            stage.at[:2],
            w_out_ref.at[:, :, lanes(at, DB)],
            x_send.at[d],
            x_recv.at[d],
            {"dp": (x + d) % 4},
        )

    for d in (2, 1, 3):
        fan(d, x).start()
    stay = pltpu.make_async_copy(stage.at[:2], w_out_ref.at[:, :, lanes(x, DB)], here.at[3])
    stay.start()
    down_out_ref[...] = stage[2]
    load_o.wait()
    wo_ref[...] = wo_wide[...].astype(BF16)
    save_o.start()

    own.wait()
    each(1, 16, lambda k: head_in(k).wait_recv())
    for d in (2, 1, 3):
        near(0, d)(y_from[d]).wait_recv()
        near(1, d)(z_from[d]).wait_recv()
    mine.wait()
    for d in (2, 1, 3):
        far(0, d)(m).start()
        far(1, d)(m).start()

    key_rows[...] = qkv_ref[1].astype(F32).T.astype(BF16)

    def ctx_out(t):
        return push(
            ctx_low.at[:, lanes(t, 128)],
            ctx_ref.at[pl.ds(pl.multiple_of(m * 64, 64), 64), :],
            c_send.at[(t + 16 - m) % 16],
            c_recv.at[(t + 16 - m) % 16],
            {"mp": t},
        )

    def ctx_in(k):
        s = (m + 16 - k) % 16
        return push(
            ctx_low.at[:, pl.ds(0, 128)],
            ctx_ref.at[pl.ds(pl.multiple_of(s * 64, 64), 64), :],
            c_send.at[k],
            c_recv.at[k],
            {"mp": s},
        )

    def queries(i):
        b = (m // 2 + i) % 8
        cols = lanes(b, 256)
        q = (qkv_ref[0, :, cols].astype(F32) * 0.125).astype(BF16)
        s = dot(key_rows[...], q)
        top = jnp.max(s, axis=0, keepdims=True)
        p = jnp.exp(s - top)
        total = jnp.sum(p, axis=0, keepdims=True)
        ctx = dot(qkv_ref[2], p.astype(BF16)) / total
        lse_ref[:, cols] = top + jnp.log(total)
        ctx_here_ref[:, cols] = ctx
        ctx_low[:, cols] = ctx.astype(BF16)

    def pair(i, carry):
        queries(2 * i)
        queries(2 * i + 1)
        for u in range(2):
            b = (m // 2 + 2 * i + u) % 8
            for v in range(2):
                t = 2 * b + v

                @pl.when(t != m)
                def _():
                    ctx_out(t).start()

        return carry

    lax.fori_loop(0, 4, pair, 0)
    ctx_ref[pl.ds(pl.multiple_of(m * 64, 64), 64), :] = ctx_low[:, lanes(m, 128)]
    each(1, 16, lambda k: ctx_in(k).wait_recv())

    mid = x_ref[...].astype(F32) + dot_tn(ctx_ref[...], wo_ref[...])
    mid_ref[...] = mid
    moe_in = unit(mid)[0] * moe_gain_ref[...]
    logits = exact(moe_in, router_ref[...], NT)
    grown = jnp.exp(logits - jnp.max(logits, axis=1, keepdims=True))
    probs = grown / jnp.sum(grown, axis=1, keepdims=True)
    probs_ref[...] = probs
    gates, _ = gates_of(probs, picks(pairs_ref[...].T))
    upstream = cot_ref[...].astype(F32)
    rows = [moe_in.astype(BF16)] + [(g * upstream).astype(BF16) for g in gates]
    row = lax.broadcasted_iota(jnp.int32, (16 * ROWS, 128), 0).astype(F32)
    at = [places(pairs_ref[j : j + 1], pairs_ref[2 + j : 3 + j]) for j in range(2)]
    hot = [((row == at[0]) | (row == at[1]))] + [row == jnp.where(a < 0, a, a + ROWS) for a in at]
    hot = jnp.concatenate([h.astype(F32) for h in hot], axis=1).astype(BF16)
    sent = dot(hot, jnp.concatenate(rows, axis=0))
    send_ref[...] = sent.astype(BF16).reshape(8, 2 * ROWS, 1024)

    for i in range(6):
        save(i).wait()
    save_o.wait()
    for d in (1, 2, 3):
        far(0, d)(z_from[d]).wait_recv()
        far(1, d)(y_from[d]).wait_recv()
        fan(d, (x + 4 - d) % 4).wait_recv()
    for d in (1, 2, 3):
        near(0, d)(m).wait_send()
        near(1, d)(m).wait_send()
        far(0, d)(m).wait_send()
        far(1, d)(m).wait_send()
        fan(d, x).wait_send()
    stay.wait()
    each(1, 16, lambda k: head_out(k).wait_send())
    each(1, 16, lambda k: ctx_in(k).wait_send())
    for el in range(4):

        @pl.when(remote(el))
        def _():
            block_out(el).wait_send()


def attend(
    block_input,
    gain,
    gate_weight,
    up_weight,
    down_weight,
    moe_gain,
    router,
    pairs,
    cotangent,
    qkv_weight,
    out_weight,
):
    dma = pltpu.SemaphoreType.DMA
    vm = pl.BlockSpec(memory_space=VMEM)
    hbm = pl.BlockSpec(memory_space=pl.ANY)
    shape = jax.ShapeDtypeStruct
    return pl.pallas_call(
        attend_kernel,
        out_shape=(
            shape((8, 2 * ROWS, 1024), BF16),
            shape((128, 1024), F32),
            shape((128, 8), F32),
            shape((1024, 128), BF16),
            shape((3, 64, 2048), BF16),
            shape((64, 2048), F32),
            shape((1, 2048), F32),
            shape((FFQ, DB), BF16),
            shape((4, 4, 128, 1024), BF16),
            shape((2, FFQ, 4 * DB), BF16),
            shape((1024, 3072), BF16),
            shape((1024, 1024), BF16),
        ),
        in_specs=[vm] * 9 + [hbm] * 2,
        out_specs=(vm,) * 8 + (hbm,) * 4,
        scratch_shapes=[
            VMEM((1024, 3072), F32),
            VMEM((1024, 1024), F32),
            VMEM((1024, 3072), BF16),
            VMEM((1024, 1024), BF16),
            VMEM((128, 1024), BF16),
            VMEM((3, 16, 64, 128), BF16),
            VMEM((4, 3, FFB, DB), BF16),
            VMEM((3, FFQ, DB), BF16),
            VMEM((2048, 64), BF16),
            VMEM((64, 2048), BF16),
            dma((11,)),
            dma((4,)),
            dma((4,)),
            dma((4,)),
            dma((4,)),
            dma((16,)),
            dma((16,)),
            dma((2, 2, 4)),
            dma((2, 2, 4)),
            dma((16,)),
            dma((16,)),
        ],
        compiler_params=params(1, 62),
    )(
        block_input,
        gain.reshape(1, -1),
        jnp.swapaxes(gate_weight, 1, 2),
        jnp.swapaxes(up_weight, 1, 2),
        down_weight,
        moe_gain.reshape(1, -1),
        router.T,
        pairs,
        cotangent,
        qkv_weight,
        out_weight,
    )


GELU_A = 0.7978845608
GELU_B = 0.044715


def moe_kernel(
    send_ref,
    w_ref,
    down_ref,
    ret_ref,
    grad_ref,
    first_ref,
    recv,
    own_part,
    sib_send,
    sib_recv,
    back,
    xs,
    cs,
    hid,
    gcs,
    ucs,
    down,
    first,
    here,
    x_send,
    x_recv,
    g_send,
    g_recv,
    d_send,
    d_recv,
    f_send,
    f_recv,
    p_send,
    p_recv,
    r_send,
    r_recv,
):
    x, c, m, z, y = spot()
    barrier = pltpu.get_barrier_semaphore()

    def greet(k, carry):
        pl.semaphore_signal(barrier, inc=1, device_id={"mp": (m + k) % 16}, device_id_type=MESH)
        return carry

    lax.fori_loop(1, 16, greet, 0)
    pl.semaphore_signal(barrier, inc=1, device_id={"expert": 1 - c}, device_id_type=MESH)
    for d in range(1, 4):
        pl.semaphore_signal(barrier, inc=1, device_id={"dp": (x + d) % 4}, device_id_type=MESH)
    pl.semaphore_wait(barrier, 19)

    def fan(d, at):
        return push(
            down_ref, down.at[:, lanes(at, DB)], x_send.at[d], x_recv.at[d], {"dp": (x + d) % 4}
        )

    for d in (2, 1, 3):
        fan(d, x).start()
    stay = pltpu.make_async_copy(down_ref, down.at[:, lanes(x, DB)], here.at[0])
    stay.start()

    def expert_of(t):
        return ((t // 4) % 2) * 4 + t % 4

    def dispatch(k):
        t = (m + k) % 16
        return pltpu.make_async_remote_copy(
            src_ref=send_ref.at[expert_of(t)],
            dst_ref=recv.at[0, k],
            send_sem=d_send.at[k],
            recv_sem=d_recv.at[k],
            device_id={"mp": t},
            device_id_type=MESH,
        )

    def forward(k):
        return pltpu.make_async_remote_copy(
            src_ref=recv.at[0, k],
            dst_ref=recv.at[1, k],
            send_sem=f_send.at[k],
            recv_sem=f_recv.at[k],
            device_id={"expert": 1 - c},
            device_id_type=MESH,
        )

    def partials(j):
        return pltpu.make_async_remote_copy(
            src_ref=sib_send.at[j],
            dst_ref=sib_recv.at[j],
            send_sem=p_send.at[j],
            recv_sem=p_recv.at[j],
            device_id={"expert": 1 - c},
            device_id_type=MESH,
        )

    def giving(k):
        return pltpu.make_async_remote_copy(
            src_ref=back.at[k],
            dst_ref=ret_ref.at[m],
            send_sem=r_send.at[k],
            recv_sem=r_recv.at[k],
            device_id={"mp": (m + 16 - k) % 16},
            device_id_type=MESH,
        )

    def start_dispatch(k, carry):
        dispatch(k).start()
        return carry

    lax.fori_loop(1, 16, start_dispatch, 0)
    recv[0, 0] = send_ref[expert_of(m)]

    def finish(j):
        partials(j).wait_recv()
        back[pl.ds(4 * j, 4)] = (own_part[...] + sib_recv[j].astype(F32)).astype(BF16)
        for i in range(4):
            k = 4 * j + i

            @pl.when(k > 0)
            def _():
                giving(k).start()

            @pl.when(k == 0)
            def _():
                ret_ref[m] = back[0]

    def chunk(j, carry):
        for i in range(4):
            k = 4 * j + i

            @pl.when(k > 0)
            def _():
                dispatch(k).wait_recv()

            forward(k).start()

        @pl.when(j > 0)
        def _():
            finish(j - 1)

        for i in range(4):
            forward(4 * j + i).wait_recv()
        blk = recv[:, pl.ds(4 * j, 4)].astype(F32)
        span = pl.ds(pl.multiple_of(j * 8 * ROWS, 16), 8 * ROWS)
        xs[span] = blk[:, :, :ROWS].reshape(8 * ROWS, 4 * DB).astype(BF16)
        cs[span] = blk[:, :, ROWS:].reshape(8 * ROWS, 4 * DB).astype(BF16)
        gate = dot_nt(xs[span], w_ref[0])
        up = dot_nt(xs[span], w_ref[1])
        hid_cot = dot_nt(cs[span], down[...])
        sq = gate * gate
        th = jnp.tanh(GELU_A * (gate + GELU_B * (gate * sq)))
        half = 0.5 * (1.0 + th)
        act = gate * half
        slope = half + 0.5 * gate * (1.0 - th * th) * (GELU_A * (1.0 + 3.0 * GELU_B * sq))
        hid[span] = (act * up).astype(BF16)
        gcs[span] = (hid_cot * up * slope).astype(BF16)
        ucs[span] = (hid_cot * act).astype(BF16)
        out = dot(hid[span], down[...]).reshape(2, 4, ROWS, 4 * DB)
        rows = (dot(gcs[span], w_ref[0]) + dot(ucs[span], w_ref[1])).reshape(2, 4, ROWS, 4 * DB)
        own_part[:, :ROWS] = out[0]
        own_part[:, ROWS:] = rows[0]
        sib_send[j] = jnp.concatenate([out[1], rows[1]], axis=1).astype(BF16)
        partials(j).start()
        return carry

    stay.wait()
    for d in (1, 2, 3):
        fan(d, (x + 4 - d) % 4).wait_recv()
    lax.fori_loop(0, 4, chunk, 0)
    finish(3)

    def lead(d):
        t = (x + d) % 4
        return push(first.at[t], first_ref.at[d], g_send.at[d], g_recv.at[d], {"dp": t})

    g = dot_tn(gcs[...], xs[...])
    for at in range(4):
        first[at] = g[:, at * DB : (at + 1) * DB].astype(BF16)
    for d in (2, 1, 3):
        lead(d).start()
    first_ref[0] = first[x]
    for i, (a, b) in enumerate(((ucs, xs), (hid, cs))):
        g = dot_tn(a[...], b[...])
        for at in range(4):
            grad_ref[at, i] = g[:, at * DB : (at + 1) * DB].astype(BF16)

    def drain(k, carry):
        pltpu.make_async_remote_copy(
            src_ref=back.at[k],
            dst_ref=ret_ref.at[(m + k) % 16],
            send_sem=r_send.at[k],
            recv_sem=r_recv.at[k],
            device_id={"mp": (m + 16 - k) % 16},
            device_id_type=MESH,
        ).wait()
        dispatch(k).wait_send()
        forward(k).wait_send()
        return carry

    lax.fori_loop(1, 16, drain, 0)
    forward(0).wait_send()
    for d in (1, 2, 3):
        fan(d, x).wait_send()
        lead(d).wait_recv()
    for d in (1, 2, 3):
        lead(d).wait_send()
    for j in range(4):
        partials(j).wait_send()


def moe(send, weights, down):
    dma = pltpu.SemaphoreType.DMA
    block = (2 * ROWS, 4 * DB)
    return pl.pallas_call(
        moe_kernel,
        out_shape=(
            jax.ShapeDtypeStruct((16, *block), BF16),
            jax.ShapeDtypeStruct((4, 2, FFQ, DB), BF16),
            jax.ShapeDtypeStruct((4, FFQ, DB), BF16),
        ),
        in_specs=[pl.BlockSpec(memory_space=VMEM)] * 3,
        out_specs=(pl.BlockSpec(memory_space=VMEM),) * 3,
        scratch_shapes=[
            VMEM((2, 16, *block), BF16),
            VMEM((4, *block), F32),
            VMEM((4, 4, *block), BF16),
            VMEM((4, 4, *block), BF16),
            VMEM((16, *block), BF16),
            VMEM((32 * ROWS, 4 * DB), BF16),
            VMEM((32 * ROWS, 4 * DB), BF16),
            VMEM((32 * ROWS, FFQ), BF16),
            VMEM((32 * ROWS, FFQ), BF16),
            VMEM((32 * ROWS, FFQ), BF16),
            VMEM((FFQ, 4 * DB), BF16),
            VMEM((4, FFQ, DB), BF16),
            dma((1,)),
            dma((4,)),
            dma((4,)),
            dma((4,)),
            dma((4,)),
            dma((16,)),
            dma((16,)),
            dma((16,)),
            dma((16,)),
            dma((4,)),
            dma((4,)),
            dma((16,)),
            dma((16,)),
        ],
        compiler_params=params(3, 62),
    )(send, weights, down)


def attend_back_kernel(
    ret_ref,
    mid_ref,
    probs_ref,
    pairs_ref,
    cot_ref,
    moe_gain_ref,
    router_ref,
    wo_ref,
    tok_ref,
    qkv_ref,
    ctx_ref,
    lse_ref,
    x_ref,
    gain_ref,
    first_ref,
    g_ref,
    nall_hbm,
    wq_hbm,
    y_ref,
    in_ref,
    gain_out_ref,
    full_ref,
    g_out_ref,
    o_out_ref,
    few_out_ref,
    dctx_ref,
    nall_ref,
    wq_ref,
    mid_cot,
    o_ref,
    few_ref,
    o_sib,
    o_half,
    o_mp,
    o_quarter,
    o_dp,
    few_mp,
    few_sum,
    few_done,
    few_rest,
    cot,
    key_rows,
    value_rows,
    row_dot,
    dk,
    dv,
    pc_here,
    pc_tok,
    slices,
    parts,
    g_in,
    g_sum,
    gain_row,
    gain_mp,
    gain_rest,
    here,
    a_send,
    a_recv,
    b_send,
    b_recv,
    q_send,
    q_recv,
    f_send,
    f_recv,
    t_send,
    t_recv,
    x_send,
    x_recv,
    s_send,
    s_recv,
    u_send,
    u_recv,
    v_send,
    v_recv,
    o_send,
    o_recv,
    om_send,
    om_recv,
    og_send,
    og_recv,
    ox_send,
    ox_recv,
    fm_send,
    fm_recv,
    fr_send,
    fr_recv,
):
    x, c, m, z, y = spot()
    pc, pz = swapped(c, z)
    away = (pc - c) * (pc - c)
    barrier = pltpu.get_barrier_semaphore()

    def remote(el):
        return (away == 1) | (el != y)

    def partner(el):
        return {"expert": pc, "mp": pz * 4 + el}

    def rest(r):
        return {"dp": (x + r % 4) % 4, "expert": (c + r // 4) % 2}

    def each(lo, hi, f):
        def one(k, carry):
            f(k)
            return carry

        lax.fori_loop(lo, hi, one, 0)

    greet_mp(barrier, m)
    for el in range(4):

        @pl.when(remote(el))
        def _():
            pl.semaphore_signal(barrier, inc=1, device_id=partner(el), device_id_type=MESH)

    for r in range(1, 8):
        pl.semaphore_signal(barrier, inc=1, device_id=rest(r), device_id_type=MESH)
    pl.semaphore_wait(barrier, 15 + 3 + away + 7)

    def fan(d):
        t = (x + d) % 4
        return push(g_ref.at[t], g_in.at[d], x_send.at[d], x_recv.at[d], {"dp": t})

    for d in (2, 1, 3):
        fan(d).start()
    keep = pltpu.make_async_copy(g_ref.at[x], g_in.at[0], here.at[0])
    keep.start()
    load_n = pltpu.make_async_copy(nall_hbm, nall_ref, here.at[2])
    load_n.start()
    load_w = pltpu.make_async_copy(wq_hbm, wq_ref, here.at[3])
    load_w.start()

    columns = pairs_ref[...].T
    hot = picks(columns)
    probs = probs_ref[...]
    gates, total = gates_of(probs, hot)
    at = places(columns[:, 0:2], columns[:, 2:4])
    lane = lax.broadcasted_iota(jnp.int32, (128, 16 * ROWS), 1).astype(F32)
    at = [at[:, j : j + 1] for j in range(2)]
    given = (ret_ref[:8].astype(F32) + ret_ref[8:].astype(F32)).astype(BF16)
    given = given.reshape(16 * ROWS, 1024)
    fetched = [dot((lane == a).astype(F32).astype(BF16), given) for a in at]
    low = [lane == jnp.where(a < 0, a, a + ROWS) for a in at]
    moe_cot = dot((low[0] | low[1]).astype(F32).astype(BF16), given)
    mid = mid_ref[...]
    upstream = cot_ref[...].astype(F32)
    y_ref[...] = (mid + gates[0] * fetched[0] + gates[1] * fetched[1]).astype(BF16)
    gate_cot = [jnp.sum(upstream * f, axis=1, keepdims=True) for f in fetched]
    inner = gate_cot[0] * gates[0] + gate_cot[1] * gates[1]
    probs_cot = sum(h * ((g - inner) / total) for h, g in zip(hot, gate_cot))
    logit_cot = probs * (probs_cot - jnp.sum(probs * probs_cot, axis=1, keepdims=True))
    hat, scale = unit(mid)
    moe_cot += exact(logit_cot, router_ref[...], (((1,), (0,)), ((), ())))
    few_ref[:8] = exact(logit_cot, hat * moe_gain_ref[...], TN)
    few_ref[8:] = jnp.concatenate(
        [jnp.sum(moe_cot * hat, axis=0, keepdims=True), jnp.zeros((7, 1024), F32)], axis=0
    )
    gained = moe_cot * moe_gain_ref[...]
    mid_cot[...] = upstream + scale * (gained - hat * jnp.mean(gained * hat, axis=-1, keepdims=True))
    branch_cot = mid_cot[...].astype(BF16)
    dctx_ref[...] = dot_nt(wo_ref[...], branch_cot).astype(BF16).reshape(16, 64, 128)

    def cot_out(k):
        t = (m + k) % 16
        return push(dctx_ref.at[t], cot.at[:, lanes(m, 128)], a_send.at[k], a_recv.at[k], {"mp": t})

    def cot_in(k):
        s = (m + 16 - k) % 16
        return push(dctx_ref.at[0], cot.at[:, lanes(s, 128)], a_send.at[k], a_recv.at[k], {"mp": s})

    each(1, 16, lambda k: cot_out(k).start())
    cot[:, lanes(m, 128)] = dctx_ref[m]

    o_ref[...] = dot(tok_ref[...], branch_cot).astype(BF16).reshape(2, 16, 32, 1024)

    def halves():
        return push(
            o_ref.at[1 - c], o_sib, o_send.at[0], o_recv.at[0], {"expert": 1 - c}
        )

    def thirty(k):
        t = (m + k) % 16
        return push(o_half.at[t], o_mp.at[k], om_send.at[k], om_recv.at[k], {"mp": t})

    def quarters(d):
        t = (x + d) % 4
        return push(
            o_quarter.at[:, lanes(t, DB)], o_dp.at[d], ox_send.at[0, d], ox_recv.at[0, d], {"dp": t}
        )

    def regain(d, at):
        return push(
            o_out_ref.at[c, m, :, lanes(x, DB)],
            o_out_ref.at[c, m, :, lanes(at, DB)],
            ox_send.at[1, d],
            ox_recv.at[1, d],
            {"dp": (x + d) % 4},
        )

    def regather(k, at):
        return push(
            o_out_ref.at[c, m], o_out_ref.at[c, at], og_send.at[k], og_recv.at[k], mp_at(m, k)
        )

    def retwin(core):
        return push(
            o_out_ref.at[core], o_out_ref.at[core], o_send.at[1], o_recv.at[1], {"expert": 1 - c}
        )

    def few_share(r):
        t = 2 * ((x + r % 4) % 4) + (c + r // 4) % 2
        return push(
            few_ref.at[:, lanes(t, 128)], few_rest.at[r], fr_send.at[0, r], fr_recv.at[0, r], rest(r)
        )

    def few_near(k):
        return push(few_sum, few_mp.at[k], fm_send.at[k], fm_recv.at[k], mp_at(m, k))

    def few_back(r, back):
        t = 2 * ((x + 4 - r % 4) % 4) + (c + r // 4) % 2 if back else 2 * x + c
        return push(
            few_done, few_out_ref.at[:, lanes(t, 128)], fr_send.at[1, r], fr_recv.at[1, r], rest(r)
        )

    for r in range(1, 8):
        few_share(r).start()
    halves().start()
    key_rows[...] = qkv_ref[1].astype(F32).T.astype(BF16)
    value_rows[...] = qkv_ref[2].astype(F32).T.astype(BF16)
    dk[...] = jnp.zeros_like(dk)
    dv[...] = jnp.zeros_like(dv)
    each(1, 16, lambda k: cot_in(k).wait_recv())
    row_dot[...] = jnp.sum(cot[...].astype(F32) * ctx_ref[...], axis=0, keepdims=True)

    def queries(b):
        cols = lanes(b, 256)
        q = (qkv_ref[0, :, cols].astype(F32) * 0.125).astype(BF16)
        p = jnp.exp(dot(key_rows[...], q) - lse_ref[:, cols])
        dp = dot(value_rows[...], cot[:, cols])
        ds = (p * (dp - row_dot[:, cols])).astype(BF16)
        pc_here[0, :, cols] = (dot(qkv_ref[1], ds) * 0.125).astype(BF16)
        dk[...] += dot_nt(ds, q)
        dv[...] += dot_nt(p.astype(BF16), cot[:, cols])

    def pair(i, carry):
        queries(2 * i)
        queries(2 * i + 1)
        return carry

    pair(0, 0)
    halves().wait_recv()
    o_half[...] = (o_ref[c].astype(F32) + o_sib[...].astype(F32)).astype(BF16)
    each(1, 16, lambda k: thirty(k).start())
    few_all = few_ref[:, lanes(2 * x + c, 128)]
    for r in range(1, 8):
        few_share(r).wait_recv()
        few_all += few_rest[r]
    few_sum[...] = few_all
    each(1, 16, lambda k: few_near(k).start())
    lax.fori_loop(1, 4, pair, 0)
    pc_here[1] = dk[...].T.astype(BF16)
    pc_here[2] = dv[...].T.astype(BF16)

    def pc_out(k):
        t = (m + k) % 16
        return push(
            pc_here.at[:, :, lanes(t, 128)], pc_tok.at[:, m], b_send.at[k], b_recv.at[k], {"mp": t}
        )

    def pc_in(k):
        s = (m + 16 - k) % 16
        return push(
            pc_here.at[:, :, pl.ds(0, 128)], pc_tok.at[:, s], b_send.at[k], b_recv.at[k], {"mp": s}
        )

    each(1, 16, lambda k: pc_out(k).start())
    pc_tok[:, m] = pc_here[:, :, lanes(m, 128)]

    each(1, 16, lambda k: thirty(k).wait_recv())
    o_sum = o_half[m].astype(F32)
    for k in range(1, 16):
        o_sum += o_mp[k].astype(F32)
    o_quarter[...] = o_sum.astype(BF16)
    for d in (2, 1, 3):
        quarters(d).start()
    each(1, 16, lambda k: few_near(k).wait_recv())
    few_all = few_sum[...]
    for k in range(1, 16):
        few_all += few_mp[k]
    few_done[...] = few_all
    few_out_ref[:, lanes(2 * x + c, 128)] = few_all
    for r in range(1, 8):
        few_back(r, False).start()

    load_n.wait()
    slices[...] = dot(pc_here[...].reshape(192, 2048), nall_ref[...]).astype(BF16)

    def share_out(r):
        t = 2 * ((x + r % 4) % 4) + (c + r // 4) % 2
        return push(slices.at[:, lanes(t, 128)], parts.at[r], q_send.at[r], q_recv.at[r], rest(r))

    for r in range(1, 8):
        share_out(r).start()
    for d in (1, 2, 3):
        quarters(d).wait_recv()
    o_fin = o_quarter[:, lanes(x, DB)].astype(F32)
    for d in (1, 2, 3):
        o_fin += o_dp[d].astype(F32)
    o_out_ref[c, m, :, lanes(x, DB)] = o_fin.astype(BF16)
    for d in (2, 1, 3):
        regain(d, x).start()
    total = slices[:, lanes(2 * x + c, 128)].astype(F32)
    for r in range(1, 8):
        share_out(r).wait_recv()
    for r in range(1, 8):
        total += parts[r].astype(F32)
    full_ref[:, c, x, z, y] = total.astype(BF16).reshape(3, 64, 128)

    def along(axis, d):
        if axis == 0:
            return {"dp": (x + d) % 4}
        return z_at(z, y, d) if axis == 1 else y_at(z, y, d)

    orders = ((0, 2, 1), (2, 1, 0), (1, 0, 2))

    def spread(p, s, d, back):
        at = [x, z, y]
        axis = orders[p][s]
        if back:
            at[axis] = (at[axis] + 4 - d) % 4
        for done in orders[p][:s]:
            at[done] = slice(None)
        src = [x, z, y]
        for done in orders[p][:s]:
            src[done] = slice(None)
        return push(
            full_ref.at[(p, c, *src)],
            full_ref.at[(p, c, *at)],
            f_send.at[p, s, d],
            f_recv.at[p, s, d],
            along(axis, d),
        )

    def twin(p, back):
        core = 1 - c if back else c
        return push(
            full_ref.at[p, core],
            full_ref.at[p, core],
            t_send.at[p],
            t_recv.at[p],
            {"expert": 1 - c},
        )

    for p in range(3):
        for d in (2, 1, 3):
            spread(p, 0, d, False).start()

    each(1, 16, lambda k: pc_in(k).wait_recv())
    load_w.wait()
    dn = dot(wq_ref[...], pc_tok[...].reshape(3072, 128)).T
    hat, scale = unit(x_ref[...].astype(F32))
    gained = dn * gain_ref[...]
    in_ref[...] = mid_cot[...] + scale * (
        gained - hat * jnp.mean(gained * hat, axis=-1, keepdims=True)
    )
    gain_row[...] = jnp.sum(dn * hat, axis=0, keepdims=True)

    def gain_out(k):
        return push(gain_row, gain_mp.at[k], u_send.at[k], u_recv.at[k], mp_at(m, k))

    def gain_far(r):
        return push(gain_mp.at[0], gain_rest.at[r], v_send.at[r], v_recv.at[r], rest(r))

    each(1, 16, lambda k: gain_out(k).start())
    for d in (1, 2, 3):
        regain(d, (x + 4 - d) % 4).wait_recv()
    each(1, 16, lambda k: regather(k, m).start())
    for p in range(3):
        for d in (1, 2, 3):
            spread(p, 0, d, True).wait_recv()
    for p in range(3):
        for d in (2, 1, 3):
            spread(p, 1, d, False).start()

    each(1, 16, lambda k: gain_out(k).wait_recv())
    got = gain_row[...]
    for k in range(1, 16):
        got += gain_mp[k]
    gain_mp[0] = got
    for r in range(1, 8):
        gain_far(r).start()

    for p in range(3):
        for d in (1, 2, 3):
            spread(p, 1, d, True).wait_recv()
    for p in range(3):
        for d in (2, 1, 3):
            spread(p, 2, d, False).start()

    keep.wait()
    for d in (1, 2, 3):
        fan(d).wait_recv()
    for i in range(2):
        g_sum[i + 1] = (
            g_in[0, i].astype(F32)
            + g_in[1, i].astype(F32)
            + g_in[2, i].astype(F32)
            + g_in[3, i].astype(F32)
        ).astype(BF16)
    g_sum[0] = (
        first_ref[0].astype(F32)
        + first_ref[1].astype(F32)
        + first_ref[2].astype(F32)
        + first_ref[3].astype(F32)
    ).astype(BF16)

    def home_out(at):
        return push(
            g_sum.at[:, pl.ds(at * FFB, FFB), :],
            g_out_ref.at[y],
            s_send.at[at],
            s_recv.at[y],
            partner(at),
        )

    def home_in(at):
        return push(
            g_sum.at[:, pl.ds(at * FFB, FFB), :],
            g_out_ref.at[at],
            s_send.at[at],
            s_recv.at[at],
            partner(at),
        )

    for at in range(4):

        @pl.when(remote(at))
        def _():
            home_out(at).start()

    @pl.when(away == 0)
    def _():
        kept = pltpu.make_async_copy(
            g_sum.at[:, pl.ds(pl.multiple_of(y * FFB, 16), FFB), :], g_out_ref.at[y], here.at[1]
        )
        kept.start()
        kept.wait()

    each(1, 16, lambda k: regather(k, (m + 16 - k) % 16).wait_recv())
    retwin(c).start()
    for r in range(1, 8):
        gain_far(r).wait_recv()
    for r in range(1, 8):
        got += gain_rest[r]
    gain_out_ref[...] = got

    for p in range(3):
        for d in (1, 2, 3):
            spread(p, 2, d, True).wait_recv()
        twin(p, False).start()
    for at in range(4):

        @pl.when(remote(at))
        def _():
            home_in(at).wait_recv()

    retwin(1 - c).wait_recv()
    for r in range(1, 8):
        few_back(r, True).wait_recv()
    for p in range(3):
        twin(p, True).wait_recv()
    for p in range(3):
        twin(p, False).wait_send()
        for s in range(3):
            for d in (1, 2, 3):
                spread(p, s, d, False).wait_send()
    halves().wait_send()
    retwin(c).wait_send()
    each(1, 16, lambda k: thirty(k).wait_send())
    each(1, 16, lambda k: regather(k, m).wait_send())
    each(1, 16, lambda k: few_near(k).wait_send())
    for d in (1, 2, 3):
        quarters(d).wait_send()
        regain(d, x).wait_send()
    for r in range(1, 8):
        few_share(r).wait_send()
        few_back(r, False).wait_send()
    each(1, 16, lambda k: cot_out(k).wait_send())
    each(1, 16, lambda k: pc_out(k).wait_send())
    each(1, 16, lambda k: gain_out(k).wait_send())
    for d in (1, 2, 3):
        fan(d).wait_send()
    for r in range(1, 8):
        share_out(r).wait_send()
        gain_far(r).wait_send()
    for at in range(4):

        @pl.when(remote(at))
        def _():
            home_out(at).wait_send()


def attend_back(*operands):
    dma = pltpu.SemaphoreType.DMA
    vm = pl.BlockSpec(memory_space=VMEM)
    hbm = pl.BlockSpec(memory_space=pl.ANY)
    shape = jax.ShapeDtypeStruct
    return pl.pallas_call(
        attend_back_kernel,
        out_shape=(
            shape((128, 1024), BF16),
            shape((128, 1024), F32),
            shape((1, 1024), F32),
            shape((3, 2, 4, 4, 4, 64, 128), BF16),
            shape((4, 3, FFB, DB), BF16),
            shape((2, 16, 32, 1024), BF16),
            shape((16, 1024), F32),
        ),
        in_specs=[vm] * 15 + [hbm] * 3,
        out_specs=(vm,) * 7,
        scratch_shapes=[
            VMEM((16, 64, 128), BF16),
            VMEM((2048, 1024), BF16),
            VMEM((1024, 3072), BF16),
            VMEM((128, 1024), F32),
            VMEM((2, 16, 32, 1024), BF16),
            VMEM((16, 1024), F32),
            VMEM((16, 32, 1024), BF16),
            VMEM((16, 32, 1024), BF16),
            VMEM((16, 32, 1024), BF16),
            VMEM((32, 1024), BF16),
            VMEM((4, 32, DB), BF16),
            VMEM((16, 16, 128), F32),
            VMEM((16, 128), F32),
            VMEM((16, 128), F32),
            VMEM((8, 16, 128), F32),
            VMEM((64, 2048), BF16),
            VMEM((2048, 64), BF16),
            VMEM((2048, 64), BF16),
            VMEM((1, 2048), F32),
            VMEM((2048, 64), F32),
            VMEM((2048, 64), F32),
            VMEM((3, 64, 2048), BF16),
            VMEM((3, 16, 64, 128), BF16),
            VMEM((192, 1024), BF16),
            VMEM((8, 192, 128), BF16),
            VMEM((4, 2, FFQ, DB), BF16),
            VMEM((3, FFQ, DB), BF16),
            VMEM((1, 1024), F32),
            VMEM((16, 1, 1024), F32),
            VMEM((8, 1, 1024), F32),
            dma((4,)),
            dma((16,)),
            dma((16,)),
            dma((16,)),
            dma((16,)),
            dma((8,)),
            dma((8,)),
            dma((3, 3, 4)),
            dma((3, 3, 4)),
            dma((3,)),
            dma((3,)),
            dma((4,)),
            dma((4,)),
            dma((4,)),
            dma((4,)),
            dma((16,)),
            dma((16,)),
            dma((8,)),
            dma((8,)),
            dma((2,)),
            dma((2,)),
            dma((16,)),
            dma((16,)),
            dma((16,)),
            dma((16,)),
            dma((2, 4)),
            dma((2, 4)),
            dma((16,)),
            dma((16,)),
            dma((2, 8)),
            dma((2, 8)),
        ],
        compiler_params=params(2, 62),
    )(*operands)


def unfold_kernel(g_ref, o_ref):
    o_ref[...] = g_ref[...].reshape(3072, 128).astype(F32).T


def unfold(full):
    return pl.pallas_call(
        unfold_kernel,
        out_shape=jax.ShapeDtypeStruct((1024, 3072), F32),
        grid=(4, 2),
        in_specs=[
            pl.BlockSpec((3, None, None, 4, 4, 64, 128), lambda i, j: (0, j, i, 0, 0, 0, 0)),
        ],
        out_specs=pl.BlockSpec((128, 3072), lambda i, j: (2 * i + j, 0)),
        compiler_params=pltpu.CompilerParams(vmem_limit_bytes=32 * 1024 * 1024),
    )(full)


def body(
    block_input,
    attn_gain,
    qkv_weight,
    out_weight,
    moe_gain,
    router_weight,
    gate_weight,
    up_weight,
    down_weight,
    routes,
    slot_index,
    cotangent,
):
    width = block_input.shape[1]
    pairs = jnp.concatenate([routes.T, slot_index.T, jnp.zeros((4, 128), jnp.int32)]).astype(F32)
    send, middle, probs, ctx_tok, qkv, ctx_here, lse, down, nall, weights, qkv_low, out_low = attend(
        block_input,
        attn_gain,
        gate_weight,
        up_weight,
        down_weight,
        moe_gain,
        router_weight,
        pairs,
        cotangent,
        qkv_weight,
        out_weight,
    )
    returned, grads, first = moe(send, weights, down)
    block_output, input_grad, gain_grad, full, mine, out_grad, few = attend_back(
        returned,
        middle,
        probs,
        pairs,
        cotangent,
        moe_gain.reshape(1, -1),
        router_weight.T,
        out_low,
        ctx_tok,
        qkv,
        ctx_here,
        lse,
        block_input,
        attn_gain.reshape(1, -1),
        first,
        grads,
        nall.reshape(2048, 1024),
        qkv_low,
    )
    mine = mine.astype(F32)
    return (
        block_output,
        input_grad,
        gain_grad.reshape(-1),
        unfold(full),
        out_grad.reshape(width, width).astype(F32),
        few[8],
        few[:8].T,
        jnp.swapaxes(mine[:, 0], 1, 2),
        jnp.swapaxes(mine[:, 1], 1, 2),
        mine[:, 2],
    )


def solution(mesh):
    tokens = P(("dp", "expert", "mp"), None)
    cols = P("expert", "dp", "mp")
    rows = P("expert", "mp", "dp")
    return jax.shard_map(
        body,
        mesh=mesh,
        in_specs=(tokens, P(), P(), P(), P(), P(), cols, cols, rows, tokens, tokens, tokens),
        out_specs=(tokens, tokens, P(), P(), P(), P(), P(), cols, cols, rows),
        check_vma=False,
    )
```

```python
import jax
import jax.numpy as jnp
from jax import lax
from jax.experimental import pallas as pl
from jax.experimental.pallas import tpu as pltpu
from jax.sharding import PartitionSpec as P

EPSILON = 1e-06
HIGHEST = lax.Precision.HIGHEST
MESH = pl.DeviceIdType.MESH
F32 = jnp.float32
BF16 = jnp.bfloat16
VMEM = pltpu.VMEM
ROWS = 40
FFB = 176
FFQ = 704
DB = 256
NT = (((1,), (1,)), ((), ()))
TN = (((0,), (0,)), ((), ()))


def dot(a, b):
    return jnp.dot(a, b, preferred_element_type=F32)


def dot_nt(a, b):
    return lax.dot_general(a, b, NT, preferred_element_type=F32)


def dot_tn(a, b):
    return lax.dot_general(a, b, TN, preferred_element_type=F32)


def spot():
    m = lax.axis_index("mp")
    return lax.axis_index("dp"), lax.axis_index("expert"), m, m // 4, m % 4


def params(cid, mb=60):
    return pltpu.CompilerParams(
        collective_id=cid, has_side_effects=True, vmem_limit_bytes=mb * 1024 * 1024
    )


def swapped(c, z):
    return z % 2, 2 * (z // 2) + c


def mp_at(m, k):
    return {"mp": (m + k) % 16}


def y_at(z, y, d):
    return {"mp": z * 4 + (y + d) % 4}


def z_at(z, y, d):
    return {"mp": ((z + d) % 4) * 4 + y}


def push(src, dst, send, recv, device):
    return pltpu.make_async_remote_copy(
        src_ref=src, dst_ref=dst, send_sem=send, recv_sem=recv, device_id=device, device_id_type=MESH
    )


def lanes(at, size):
    return pl.ds(pl.multiple_of(at * size, size), size)


def greet_mp(barrier, m):
    def one(k, carry):
        pl.semaphore_signal(barrier, inc=1, device_id=mp_at(m, k), device_id_type=MESH)
        return carry

    lax.fori_loop(1, 16, one, 0)


def places(routes, slots):
    return jnp.where(slots < ROWS, routes * (2 * ROWS) + slots, -1.0)


def picks(columns):
    lane = lax.broadcasted_iota(jnp.int32, (128, 8), 1).astype(F32)
    return [(columns[:, j : j + 1] == lane).astype(F32) for j in range(2)]


def gates_of(probs, hot):
    chosen = [jnp.sum(probs * h, axis=1, keepdims=True) for h in hot]
    total = chosen[0] + chosen[1]
    return [v / total for v in chosen], total


def exact(a, b, dims):
    return lax.dot_general(a, b, dims, precision=HIGHEST, preferred_element_type=F32)


def unit(v):
    scale = lax.rsqrt(jnp.mean(v * v, axis=-1, keepdims=True) + EPSILON)
    return v * scale, scale


def attend_kernel(
    x_ref,
    gain_ref,
    gate_ref,
    up_ref,
    downs_ref,
    moe_gain_ref,
    router_ref,
    pairs_ref,
    cot_ref,
    wq_hbm,
    wo_hbm,
    send_ref,
    mid_ref,
    probs_ref,
    ctx_ref,
    qkv_ref,
    ctx_here_ref,
    lse_ref,
    down_ref,
    nall_ref,
    w_out_ref,
    wq_out_ref,
    wo_out_ref,
    wq_wide,
    wo_wide,
    wq_ref,
    wo_ref,
    normed,
    heads,
    blocks,
    stage,
    key_rows,
    ctx_low,
    here,
    s_send,
    s_recv,
    x_send,
    x_recv,
    a_send,
    a_recv,
    n_send,
    n_recv,
    c_send,
    c_recv,
):
    x, c, m, z, y = spot()
    pc, pz = swapped(c, z)
    away = (pc - c) * (pc - c)
    barrier = pltpu.get_barrier_semaphore()

    def remote(el):
        return (away == 1) | (el != y)

    def partner(el):
        return {"expert": pc, "mp": pz * 4 + el}

    greet_mp(barrier, m)
    for el in range(4):

        @pl.when(remote(el))
        def _():
            pl.semaphore_signal(barrier, inc=1, device_id=partner(el), device_id_type=MESH)

    for d in range(1, 4):
        pl.semaphore_signal(barrier, inc=1, device_id={"dp": (x + d) % 4}, device_id_type=MESH)

    wide = 512

    def load(i):
        cols = pl.ds(i * wide, wide)
        return pltpu.make_async_copy(wq_hbm.at[:, cols], wq_wide.at[:, cols], here.at[4 + i])

    def save(i):
        cols = pl.ds(i * wide, wide)
        return pltpu.make_async_copy(wq_ref.at[:, cols], wq_out_ref.at[:, cols], here.at[4 + i])

    load_o = pltpu.make_async_copy(wo_hbm, wo_wide, here.at[10])
    save_o = pltpu.make_async_copy(wo_ref, wo_out_ref, here.at[10])
    for i in range(6):
        load(i).start()
    load_o.start()
    for el in range(4):
        blocks[el, 0] = gate_ref[el].astype(BF16)
        blocks[el, 1] = up_ref[el].astype(BF16)
        blocks[el, 2] = downs_ref[el].astype(BF16)
    pl.semaphore_wait(barrier, 15 + 6 + away)

    def units(at):
        return stage.at[:, pl.ds(pl.multiple_of(at * FFB, 16), FFB), :]

    def block(i, el, at):
        return push(
            blocks.at[el, i],
            stage.at[i, pl.ds(pl.multiple_of(at * FFB, 16), FFB), :],
            s_send.at[i, el],
            s_recv.at[i, at],
            partner(el),
        )

    def each_block(f):
        for el in range(4):

            @pl.when(remote(el))
            def _(el=el):
                f(el)

    def blocks_out(i):
        each_block(lambda el: block(i, el, y).start())

    def blocks_in(i):
        each_block(lambda el: block(i, el, el).wait_recv())

    blocks_out(0)

    @pl.when(away == 0)
    def _():
        kept = pltpu.make_async_copy(blocks.at[y], units(y), here.at[2])
        kept.start()
        kept.wait()

    normed[...] = (unit(x_ref[...].astype(F32))[0] * gain_ref[...]).astype(BF16)
    half = 512

    def near(part, d):
        cols = pl.ds(part * half, half)
        device = y_at(z, y, d) if part == 0 else z_at(z, y, d)
        return lambda at: push(
            normed.at[:, cols],
            nall_ref.at[at // 4, at % 4, :, cols],
            n_send.at[part, 0, d],
            n_recv.at[part, 0, d],
            device,
        )

    y_from = [z * 4 + (y + 4 - d) % 4 for d in range(4)]
    z_from = [((z + 4 - d) % 4) * 4 + y for d in range(4)]

    for i in range(6):
        load(i).wait()
        cols = slice(i * wide, (i + 1) * wide)
        wq_ref[:, cols] = wq_wide[:, cols].astype(BF16)
        save(i).start()
        part = dot(normed[...], wq_ref[:, cols])
        heads[i // 2, (i % 2) * 8 : (i % 2) * 8 + 8] = part.T.astype(BF16).reshape(8, 64, 128)

    def head_out(k):
        t = (m + k) % 16
        return push(
            heads.at[:, t],
            qkv_ref.at[:, :, lanes(m, 128)],
            a_send.at[k],
            a_recv.at[k],
            mp_at(m, k),
        )

    def head_in(k):
        return push(
            heads.at[:, 0],
            qkv_ref.at[:, :, lanes((m + 16 - k) % 16, 128)],
            a_send.at[k],
            a_recv.at[k],
            mp_at(m, k),
        )

    def each(lo, hi, f):
        def one(k, carry):
            f(k)
            return carry

        lax.fori_loop(lo, hi, one, 0)

    each(1, 16, lambda k: head_out(k).start())
    own = pltpu.make_async_copy(heads.at[:, m], qkv_ref.at[:, :, lanes(m, 128)], here.at[0])
    own.start()
    mine = pltpu.make_async_copy(normed, nall_ref.at[z, y], here.at[1])
    mine.start()


    def fan(i, d, step, at):
        rows = pl.ds(0, FFQ) if step == 0 else pl.ds(0 if d == 1 else FFQ // 2, FFQ // 2)
        cols = w_out_ref.at[i, rows, lanes(at, DB)]
        return push(
            stage.at[i] if step == 0 else cols,
            cols,
            x_send.at[i, step, d],
            x_recv.at[i, step, d],
            {"dp": (x + d) % 4},
        )

    def fan_wait(i, step):
        for d in (1, 3):
            fan(i, d, step, (x + 8 - d * (1 + step)) % 4).wait_recv()

    def fan_start(i, step):
        for d in (1, 3):
            fan(i, d, step, x if step == 0 else (x + 4 - d) % 4).start()

    def fan_own(i):
        return pltpu.make_async_copy(stage.at[i], w_out_ref.at[i, :, lanes(x, DB)], here.at[2 + i])

    blocks_in(0)
    fan_start(0, 0)
    fan_own(0).start()
    load_o.wait()
    wo_ref[...] = wo_wide[...].astype(BF16)
    save_o.start()

    own.wait()
    each(1, 16, lambda k: head_in(k).wait_recv())
    blocks_out(1)
    blocks_out(2)
    for d in (2, 1, 3):
        near(0, d)(m).start()
        near(1, d)(m).start()

    key_rows[...] = qkv_ref[1].astype(F32).T.astype(BF16)

    def ctx_out(t):
        return push(
            ctx_low.at[:, lanes(t, 128)],
            ctx_ref.at[pl.ds(pl.multiple_of(m * 64, 64), 64), :],
            c_send.at[(t + 16 - m) % 16],
            c_recv.at[(t + 16 - m) % 16],
            {"mp": t},
        )

    def ctx_in(k):
        s = (m + 16 - k) % 16
        return push(
            ctx_low.at[:, pl.ds(0, 128)],
            ctx_ref.at[pl.ds(pl.multiple_of(s * 64, 64), 64), :],
            c_send.at[k],
            c_recv.at[k],
            {"mp": s},
        )

    def queries(i):
        b = (m // 2 + i) % 8
        cols = lanes(b, 256)
        q = (qkv_ref[0, :, cols].astype(F32) * 0.125).astype(BF16)
        s = dot(key_rows[...], q)
        top = jnp.max(s, axis=0, keepdims=True)
        p = jnp.exp(s - top)
        total = jnp.sum(p, axis=0, keepdims=True)
        ctx = dot(qkv_ref[2], p.astype(BF16)) / total
        lse_ref[:, cols] = top + jnp.log(total)
        ctx_here_ref[:, cols] = ctx
        ctx_low[:, cols] = ctx.astype(BF16)

    def pair(i, carry):
        queries(2 * i)
        queries(2 * i + 1)
        for u in range(2):
            b = (m // 2 + 2 * i + u) % 8
            for v in range(2):
                t = 2 * b + v

                @pl.when(t != m)
                def _():
                    ctx_out(t).start()

        @pl.when(i == 0)
        def _():
            blocks_in(1)
            fan_start(1, 0)
            fan_own(1).start()

        @pl.when(i == 1)
        def _():
            fan_wait(0, 0)
            fan_start(0, 1)
            blocks_in(2)

        return carry

    lax.fori_loop(0, 4, pair, 0)
    ctx_ref[pl.ds(pl.multiple_of(m * 64, 64), 64), :] = ctx_low[:, lanes(m, 128)]
    each(1, 16, lambda k: ctx_in(k).wait_recv())

    fan_wait(1, 0)
    fan_start(1, 1)
    down_ref[...] = stage[2]

    mid = x_ref[...].astype(F32) + dot_tn(ctx_ref[...], wo_ref[...])
    mid_ref[...] = mid
    moe_in = unit(mid)[0] * moe_gain_ref[...]
    logits = exact(moe_in, router_ref[...], NT)
    grown = jnp.exp(logits - jnp.max(logits, axis=1, keepdims=True))
    probs = grown / jnp.sum(grown, axis=1, keepdims=True)
    probs_ref[...] = probs
    gates, _ = gates_of(probs, picks(pairs_ref[...].T))
    upstream = cot_ref[...].astype(F32)
    rows = [moe_in.astype(BF16)] + [(g * upstream).astype(BF16) for g in gates]
    row = lax.broadcasted_iota(jnp.int32, (16 * ROWS, 128), 0).astype(F32)
    at = [places(pairs_ref[j : j + 1], pairs_ref[2 + j : 3 + j]) for j in range(2)]
    hot = [((row == at[0]) | (row == at[1]))] + [row == jnp.where(a < 0, a, a + ROWS) for a in at]
    hot = jnp.concatenate([h.astype(F32) for h in hot], axis=1).astype(BF16)
    sent = dot(hot, jnp.concatenate(rows, axis=0))
    send_ref[...] = sent.astype(BF16).reshape(8, 2 * ROWS, 1024)

    for i in range(6):
        save(i).wait()
    save_o.wait()
    fan_wait(0, 1)
    fan_wait(1, 1)
    for d in (1, 2, 3):
        near(0, d)(y_from[d]).wait_recv()
        near(1, d)(z_from[d]).wait_recv()
    for d in (1, 2, 3):
        near(0, d)(m).wait_send()
        near(1, d)(m).wait_send()
    mine.wait()
    for i in range(2):
        fan_own(i).wait()
        for d in (1, 3):
            for step in range(2):
                fan(i, d, step, x).wait_send()
    each(1, 16, lambda k: head_out(k).wait_send())
    each(1, 16, lambda k: ctx_in(k).wait_send())
    for i in range(3):
        each_block(lambda el, i=i: block(i, el, y).wait_send())


def attend(
    block_input,
    gain,
    gate_weight,
    up_weight,
    down_weight,
    moe_gain,
    router,
    pairs,
    cotangent,
    qkv_weight,
    out_weight,
):
    dma = pltpu.SemaphoreType.DMA
    vm = pl.BlockSpec(memory_space=VMEM)
    hbm = pl.BlockSpec(memory_space=pl.ANY)
    shape = jax.ShapeDtypeStruct
    return pl.pallas_call(
        attend_kernel,
        out_shape=(
            shape((8, 2 * ROWS, 1024), BF16),
            shape((128, 1024), F32),
            shape((128, 8), F32),
            shape((1024, 128), BF16),
            shape((3, 64, 2048), BF16),
            shape((64, 2048), F32),
            shape((1, 2048), F32),
            shape((FFQ, DB), BF16),
            shape((4, 4, 128, 1024), BF16),
            shape((2, FFQ, 4 * DB), BF16),
            shape((1024, 3072), BF16),
            shape((1024, 1024), BF16),
        ),
        in_specs=[vm] * 9 + [hbm] * 2,
        out_specs=(vm,) * 8 + (hbm,) * 4,
        scratch_shapes=[
            VMEM((1024, 3072), F32),
            VMEM((1024, 1024), F32),
            VMEM((1024, 3072), BF16),
            VMEM((1024, 1024), BF16),
            VMEM((128, 1024), BF16),
            VMEM((3, 16, 64, 128), BF16),
            VMEM((4, 3, FFB, DB), BF16),
            VMEM((3, FFQ, DB), BF16),
            VMEM((2048, 64), BF16),
            VMEM((64, 2048), BF16),
            dma((11,)),
            dma((3, 4)),
            dma((3, 4)),
            dma((2, 2, 4)),
            dma((2, 2, 4)),
            dma((16,)),
            dma((16,)),
            dma((2, 1, 4)),
            dma((2, 1, 4)),
            dma((16,)),
            dma((16,)),
        ],
        compiler_params=params(1, 62),
    )(
        block_input,
        gain.reshape(1, -1),
        jnp.swapaxes(gate_weight, 1, 2),
        jnp.swapaxes(up_weight, 1, 2),
        down_weight,
        moe_gain.reshape(1, -1),
        router.T,
        pairs,
        cotangent,
        qkv_weight,
        out_weight,
    )


GELU_A = 0.7978845608
GELU_B = 0.044715


def experts_back_kernel(
    mid_ref,
    probs_ref,
    pairs_ref,
    cot_ref,
    moe_gain_ref,
    router_ref,
    tok_ref,
    qkv_ref,
    ctx_ref,
    lse_ref,
    x_ref,
    gain_ref,
    down_ref,
    send_hbm,
    w_hbm,
    near_hbm,
    wq_hbm,
    wo_hbm,
    y_ref,
    in_ref,
    gain_out_ref,
    g_out_ref,
    few_out_ref,
    full_ref,
    ret_ref,
    nall_ref,
    weights,
    recv,
    rows,
    back,
    sib_recv,
    sib_send,
    own_part,
    hid,
    gcs,
    ucs,
    g_relay,
    g_near,
    dctx,
    mid_cot,
    few,
    o_sib,
    o_x,
    o_q,
    o_mp,
    o_fin,
    few_mp,
    few_sum,
    few_done,
    few_rest,
    cot,
    key_rows,
    value_rows,
    row_dot,
    dk,
    dv,
    pc_here,
    pc_tok,
    slices,
    own_share,
    parts,
    gain_row,
    gain_mp,
    gain_rest,
    here,
    d_send,
    d_recv,
    f_send,
    f_recv,
    p_send,
    p_recv,
    r_send,
    r_recv,
    w_send,
    w_recv,
    x_send,
    x_recv,
    s_send,
    s_recv,
    n_send,
    n_recv,
    a_send,
    a_recv,
    b_send,
    b_recv,
    q_send,
    q_recv,
    g_send,
    g_recv,
    t_send,
    t_recv,
    u_send,
    u_recv,
    v_send,
    v_recv,
    o_send,
    o_recv,
    ox_send,
    ox_recv,
    om_send,
    om_recv,
    fm_send,
    fm_recv,
    fr_send,
    fr_recv,
):
    x, c, m, z, y = spot()
    pc, pz = swapped(c, z)
    away = (pc - c) * (pc - c)
    barrier = pltpu.get_barrier_semaphore()

    def remote(el):
        return (away == 1) | (el != y)

    def partner(el):
        return {"expert": pc, "mp": pz * 4 + el}

    def rest(r):
        return {"dp": (x + r % 4) % 4, "expert": (c + r // 4) % 2}

    def each(lo, hi, f):
        def one(k, carry):
            f(k)
            return carry

        lax.fori_loop(lo, hi, one, 0)

    def local(src, dst, i):
        return pltpu.make_async_copy(src, dst, here.at[i])

    twin = {"expert": 1 - c}
    size = 2 * ROWS

    greet_mp(barrier, m)
    for el in range(4):

        @pl.when(remote(el))
        def _():
            pl.semaphore_signal(barrier, inc=1, device_id=partner(el), device_id_type=MESH)

    for r in range(1, 8):
        pl.semaphore_signal(barrier, inc=1, device_id=rest(r), device_id_type=MESH)
    load_w = [local(w_hbm.at[i], weights.at[pl.ds(i * FFQ, FFQ)], i) for i in range(2)]
    for copy in load_w:
        copy.start()
    near = [
        local(near_hbm.at[z, :, :, pl.ds(0, 512)], nall_ref.at[z, :, :, pl.ds(0, 512)], 2),
        local(near_hbm.at[:, y, :, pl.ds(512, 512)], nall_ref.at[:, y, :, pl.ds(512, 512)], 3),
    ]
    for copy in near:
        copy.start()
    pl.semaphore_wait(barrier, 15 + 3 + away + 7)

    def expert_of(t):
        return ((t // 4) % 2) * 4 + t % 4

    def slot(core, k, n=1):
        return pl.ds(pl.multiple_of((core * 16 + k) * size, size), n * size)

    def dispatch(k):
        t = (m + k) % 16
        return push(
            send_hbm.at[expert_of(t)],
            recv.at[slot(0, k)],
            d_send.at[k],
            d_recv.at[k],
            {"mp": t},
        )

    def forward(k):
        return push(recv.at[slot(0, k)], recv.at[slot(1, k)], f_send.at[k], f_recv.at[k], twin)

    def partials(j):
        return push(
            sib_send.at[j % 2],
            sib_recv.at[pl.ds(pl.multiple_of(j * 4 * size, size), 4 * size)],
            p_send.at[j],
            p_recv.at[j],
            twin,
        )

    def spot_of(k, n=1):
        return pl.ds(pl.multiple_of(k * size, size), n * size)

    def giving(k, at):
        return push(
            back.at[spot_of(k)], ret_ref.at[at], r_send.at[k], r_recv.at[k], mp_at(m, 16 - k)
        )

    def down_fan(d, at):
        return push(
            down_ref,
            weights.at[pl.ds(2 * FFQ, FFQ), lanes(at, DB)],
            w_send.at[d],
            w_recv.at[d],
            {"dp": (x + d) % 4},
        )

    each(1, 16, lambda k: dispatch(k).start())
    own = local(send_hbm.at[expert_of(m)], recv.at[slot(0, 0)], 4)
    own.start()
    for d in (2, 1, 3):
        down_fan(d, x).start()
    weights[2 * FFQ :, lanes(x, DB)] = down_ref[...]
    own.wait()

    def finish(j):
        partials(j).wait_recv()
        span = spot_of(4 * j, 4)
        back[span] = (own_part[...] + sib_recv[span].astype(F32)).astype(BF16)
        for i in range(4):
            k = 4 * j + i

            @pl.when(k > 0)
            def _():
                giving(k, m).start()

            @pl.when(k == 0)
            def _():
                local(back.at[spot_of(0)], ret_ref.at[m], 4).start()

    gate_w, up_w, down_w = (slice(i * FFQ, (i + 1) * FFQ) for i in range(3))
    cot_rows = 32 * ROWS

    def chunk(j, carry):
        for i in range(4):
            k = 4 * j + i

            @pl.when(k > 0)
            def _():
                dispatch(k).wait_recv()

            forward(k).start()

        @pl.when(j > 0)
        def _():
            finish(j - 1)

        @pl.when(j == 0)
        def _():
            for copy in load_w:
                copy.wait()
            for d in (1, 2, 3):
                down_fan(d, (x + 4 - d) % 4).wait_recv()

        for i in range(4):
            forward(4 * j + i).wait_recv()
        xs = pl.ds(pl.multiple_of(j * 8 * ROWS, 16), 8 * ROWS)
        cs = pl.ds(pl.multiple_of(cot_rows + j * 8 * ROWS, 16), 8 * ROWS)
        for r in range(2):
            blk = recv[slot(r, 4 * j, 4)].astype(F32).reshape(4, size, 4 * DB)
            for at, part in ((0, blk[:, :ROWS]), (cot_rows, blk[:, ROWS:])):
                span = pl.ds(pl.multiple_of(at + (2 * j + r) * 4 * ROWS, 16), 4 * ROWS)
                rows[span] = part.reshape(4 * ROWS, 4 * DB).astype(BF16)
        gate = dot_nt(rows[xs], weights[gate_w])
        up = dot_nt(rows[xs], weights[up_w])
        hid_cot = dot_nt(rows[cs], weights[down_w])
        sq = gate * gate
        th = jnp.tanh(GELU_A * (gate + GELU_B * (gate * sq)))
        half = 0.5 * (1.0 + th)
        act = gate * half
        slope = half + 0.5 * gate * (1.0 - th * th) * (GELU_A * (1.0 + 3.0 * GELU_B * sq))
        hid[xs] = (act * up).astype(BF16)
        gcs[xs] = (hid_cot * up * slope).astype(BF16)
        ucs[xs] = (hid_cot * act).astype(BF16)
        out = dot(hid[xs], weights[down_w]).reshape(2, 4, ROWS, 4 * DB)
        low = dot(gcs[xs], weights[gate_w]) + dot(ucs[xs], weights[up_w])
        low = low.reshape(2, 4, ROWS, 4 * DB)
        own_part[...] = jnp.concatenate([out[0], low[0]], axis=1).reshape(4 * size, 4 * DB)

        @pl.when(j > 1)
        def _():
            partials(j - 2).wait_send()

        sib_send[j % 2] = (
            jnp.concatenate([out[1], low[1]], axis=1).reshape(4 * size, 4 * DB).astype(BF16)
        )
        partials(j).start()
        return carry

    lax.fori_loop(0, 4, chunk, 0)
    finish(3)
    each(0, 16, lambda k: forward(k).wait_send())
    load_o = local(wo_hbm, weights.at[pl.ds(0, 1024)], 0)
    load_o.start()

    unit_half = FFQ // 2

    def unit_rows(i, d):
        return pl.ds(i * FFQ + (0 if d == 1 else unit_half), unit_half)

    def relay(i, d):
        return push(
            recv.at[unit_rows(i, d), lanes((x + 2) % 4, DB)],
            g_relay.at[d // 2, i],
            x_send.at[0, i, d],
            x_recv.at[0, i, d],
            {"dp": (x + d) % 4},
        )

    def settle(i, d):
        return push(
            recv.at[pl.ds(i * FFQ, FFQ), lanes((x + d) % 4, DB)],
            g_near.at[d // 2, i],
            x_send.at[1, i, d],
            x_recv.at[1, i, d],
            {"dp": (x + d) % 4},
        )

    for i, (a, at) in enumerate(((gcs, 0), (ucs, 0), (hid, cot_rows))):
        g = dot_tn(a[...], rows[at : at + cot_rows])
        recv[i * FFQ : (i + 1) * FFQ] = g.astype(BF16)
        for d in (1, 3):
            relay(i, d).start()
    load_q = [
        local(wq_hbm.at[:, pl.ds(i * 1024, 1024)], rows.at[pl.ds(i * 1024, 1024)], 5 + i)
        for i in range(3)
    ]
    for copy in load_q:
        copy.start()
    for i in range(3):
        for d in (1, 3):
            relay(i, d).wait_recv()
            span, cols = unit_rows(i, d), lanes((x + d) % 4, DB)
            recv[span, cols] = (
                recv[span, cols].astype(F32) + g_relay[d // 2, i].astype(F32)
            ).astype(BF16)
            settle(i, d).start()

    def home(i, at, to):
        return push(
            recv.at[pl.ds(i * FFQ + at * FFB, FFB), lanes(x, DB)],
            g_out_ref.at[to, i],
            s_send.at[i, at],
            s_recv.at[i, to],
            partner(at),
        )

    def each_home(f):
        for at in range(4):

            @pl.when(remote(at))
            def _(at=at):
                f(at)

    def go_home(i):
        for d in (1, 3):
            settle(i, d).wait_recv()
        span, cols = pl.ds(i * FFQ, FFQ), lanes(x, DB)
        recv[span, cols] = (
            recv[span, cols].astype(F32) + g_near[0, i].astype(F32) + g_near[1, i].astype(F32)
        ).astype(BF16)
        each_home(lambda at: home(i, at, y).start())

        @pl.when(away == 0)
        def _():
            kept = local(
                recv.at[pl.ds(pl.multiple_of(i * FFQ + y * FFB, 16), FFB), cols], g_out_ref.at[y, i], 1
            )
            kept.start()
            kept.wait()

    local(back.at[spot_of(0)], ret_ref.at[m], 4).wait()
    each(1, 16, lambda k: giving(k, (m + k) % 16).wait())
    load_r = local(ret_ref, back.reshape(16, size, 4 * DB), 4)
    load_r.start()
    load_r.wait()

    for copy in near:
        copy.wait()
    y_from = [z * 4 + (y + 4 - d) % 4 for d in range(4)]
    z_from = [((z + 4 - d) % 4) * 4 + y for d in range(4)]

    def far(part, d, step, origin):
        cols = pl.ds(part * 512, 512)
        some = pl.ds(0, 4) if step == 0 else pl.ds(0 if d == 1 else 2, 2)
        if part == 0:
            ref, device = nall_ref.at[origin // 4, some, :, cols], z_at(z, y, d)
        else:
            ref, device = nall_ref.at[some, origin % 4, :, cols], y_at(z, y, d)
        return push(ref, ref, n_send.at[part, step, d], n_recv.at[part, step, d], device)

    def far_wait(step):
        for part, origins in enumerate((z_from, y_from)):
            for d in (1, 3):
                far(part, d, step, origins[(d * (1 + step)) % 4]).wait_recv()

    def far_start(step):
        for part, origins in enumerate((z_from, y_from)):
            for d in (1, 3):
                far(part, d, step, origins[d * step]).start()

    columns = pairs_ref[...].T
    hot = picks(columns)
    probs = probs_ref[...]
    gates, total = gates_of(probs, hot)
    at = places(columns[:, 0:2], columns[:, 2:4])
    lane = lax.broadcasted_iota(jnp.int32, (128, 16 * ROWS), 1).astype(F32)
    at = [at[:, j : j + 1] for j in range(2)]
    given = (back[: 8 * size].astype(F32) + back[8 * size :].astype(F32)).astype(BF16)
    fetched = [dot((lane == a).astype(F32).astype(BF16), given) for a in at]
    low = [lane == jnp.where(a < 0, a, a + ROWS) for a in at]
    moe_cot = dot((low[0] | low[1]).astype(F32).astype(BF16), given)
    mid = mid_ref[...]
    upstream = cot_ref[...].astype(F32)
    y_ref[...] = (mid + gates[0] * fetched[0] + gates[1] * fetched[1]).astype(BF16)
    gate_cot = [jnp.sum(upstream * f, axis=1, keepdims=True) for f in fetched]
    inner = gate_cot[0] * gates[0] + gate_cot[1] * gates[1]
    probs_cot = sum(h * ((g - inner) / total) for h, g in zip(hot, gate_cot))
    logit_cot = probs * (probs_cot - jnp.sum(probs * probs_cot, axis=1, keepdims=True))
    hat, scale = unit(mid)
    moe_cot += exact(logit_cot, router_ref[...], (((1,), (0,)), ((), ())))
    few[:8] = exact(logit_cot, hat * moe_gain_ref[...], TN)
    few[8:] = jnp.concatenate(
        [jnp.sum(moe_cot * hat, axis=0, keepdims=True), jnp.zeros((7, 1024), F32)], axis=0
    )
    gained = moe_cot * moe_gain_ref[...]
    mid_cot[...] = upstream + scale * (gained - hat * jnp.mean(gained * hat, axis=-1, keepdims=True))
    branch_cot = mid_cot[...].astype(BF16)
    load_o.wait()
    dctx[...] = dot_nt(weights[:1024], branch_cot).astype(BF16).reshape(16, 64, 128)

    def cot_out(k):
        t = (m + k) % 16
        return push(dctx.at[t], cot.at[:, lanes(m, 128)], a_send.at[k], a_recv.at[k], {"mp": t})

    def cot_in(k):
        s = (m + 16 - k) % 16
        return push(dctx.at[0], cot.at[:, lanes(s, 128)], a_send.at[k], a_recv.at[k], {"mp": s})

    each(1, 16, lambda k: cot_out(k).start())
    far_start(0)
    cot[:, lanes(m, 128)] = dctx[m]

    weights[1024:2048] = dot(tok_ref[...], branch_cot).astype(BF16)

    def halves():
        rows_at = pl.ds(pl.multiple_of(1024 + (1 - c) * 512, 512), 512)
        return push(weights.at[rows_at], o_sib, o_send.at[0], o_recv.at[0], twin)

    def quarters(d):
        t = (x + d) % 4
        return push(
            weights.at[pl.ds(0, 512), lanes(t, DB)], o_x.at[d], ox_send.at[d], ox_recv.at[d], {"dp": t}
        )

    def thirty(k):
        t = (m + k) % 16
        return push(
            o_q.at[pl.ds(pl.multiple_of(t * 32, 32), 32)],
            o_mp.at[k],
            om_send.at[k],
            om_recv.at[k],
            {"mp": t},
        )

    def few_share(r):
        t = 2 * ((x + r % 4) % 4) + (c + r // 4) % 2
        return push(
            few.at[:, lanes(t, 128)], few_rest.at[r], fr_send.at[0, r], fr_recv.at[0, r], rest(r)
        )

    def few_near(k):
        return push(few_sum, few_mp.at[k], fm_send.at[k], fm_recv.at[k], mp_at(m, k))

    def few_back(r, back_from):
        t = 2 * ((x + 4 - r % 4) % 4) + (c + r // 4) % 2 if back_from else 2 * x + c
        return push(
            few_done, few_out_ref.at[:, lanes(t, 128)], fr_send.at[1, r], fr_recv.at[1, r], rest(r)
        )

    halves().start()
    for r in range(1, 8):
        few_share(r).start()

    def along(axis, d):
        if axis == 0:
            return {"dp": (x + d) % 4}
        return z_at(z, y, d) if axis == 1 else y_at(z, y, d)

    orders = ((0, 2, 1), (2, 1, 0), (1, 0, 2), (1, 2, 0))

    def spread(p, s, d, incoming):
        at = [x, z, y]
        axis = orders[p][s]
        if incoming:
            at[axis] = (at[axis] + 4 - d) % 4
        src = [x, z, y]
        for done in orders[p][:s]:
            at[done] = slice(None)
            src[done] = slice(None)
        return push(
            full_ref.at[(p, c, *src)],
            full_ref.at[(p, c, *at)],
            g_send.at[p, s, d],
            g_recv.at[p, s, d],
            along(axis, d),
        )

    def spread_start(p, s):
        for d in (2, 1, 3):
            spread(p, s, d, False).start()

    def spread_wait(p, s):
        for d in (1, 2, 3):
            spread(p, s, d, True).wait_recv()

    def share_twin(p, core):
        return push(full_ref.at[p, core], full_ref.at[p, core], t_send.at[p], t_recv.at[p], twin)

    key_rows[...] = qkv_ref[1].astype(F32).T.astype(BF16)
    value_rows[...] = qkv_ref[2].astype(F32).T.astype(BF16)
    dk[...] = jnp.zeros_like(dk)
    dv[...] = jnp.zeros_like(dv)
    halves().wait_recv()
    weights[:512] = (
        weights[pl.ds(pl.multiple_of(1024 + c * 512, 512), 512)].astype(F32) + o_sib[...].astype(F32)
    ).astype(BF16)
    for d in (2, 1, 3):
        quarters(d).start()
    go_home(0)
    each(1, 16, lambda k: cot_in(k).wait_recv())
    row_dot[...] = jnp.sum(cot[...].astype(F32) * ctx_ref[...], axis=0, keepdims=True)

    def queries(b):
        cols = lanes(b, 256)
        q = (qkv_ref[0, :, cols].astype(F32) * 0.125).astype(BF16)
        p = jnp.exp(dot(key_rows[...], q) - lse_ref[:, cols])
        dp = dot(value_rows[...], cot[:, cols])
        ds = (p * (dp - row_dot[:, cols])).astype(BF16)
        pc_here[0, :, cols] = (dot(qkv_ref[1], ds) * 0.125).astype(BF16)
        dk[...] += dot_nt(ds, q)
        dv[...] += dot_nt(p.astype(BF16), cot[:, cols])

    def pair(i, carry):
        queries(2 * i)
        queries(2 * i + 1)

        @pl.when(i == 0)
        def _():
            for d in (1, 2, 3):
                quarters(d).wait_recv()
            o_sum = weights[:512, lanes(x, DB)].astype(F32)
            for d in (1, 2, 3):
                o_sum += o_x[d].astype(F32)
            o_q[...] = o_sum.astype(BF16)
            each(1, 16, lambda k: thirty(k).start())
            few_all = few[:, lanes(2 * x + c, 128)]
            for r in range(1, 8):
                few_share(r).wait_recv()
                few_all += few_rest[r]
            few_sum[...] = few_all
            each(1, 16, lambda k: few_near(k).start())

        @pl.when(i == 1)
        def _():
            far_wait(0)
            far_start(1)

        @pl.when(i == 2)
        def _():
            each(1, 16, lambda k: thirty(k).wait_recv())
            o_sum = o_q[pl.ds(pl.multiple_of(m * 32, 32), 32)].astype(F32)
            for k in range(1, 16):
                o_sum += o_mp[k].astype(F32)
            o_low = o_sum.astype(BF16)
            o_fin[:32] = o_low[:, :128]
            o_fin[32:] = o_low[:, 128:]
            lay = local(o_fin, full_ref.at[3, c, x, z, y], 2)
            lay.start()
            lay.wait()
            spread_start(3, 0)

        return carry

    lax.fori_loop(0, 4, pair, 0)
    pc_here[1] = dk[...].T.astype(BF16)
    pc_here[2] = dv[...].T.astype(BF16)

    def pc_out(k):
        t = (m + k) % 16
        return push(
            pc_here.at[:, :, lanes(t, 128)], pc_tok.at[:, m], b_send.at[k], b_recv.at[k], {"mp": t}
        )

    def pc_in(k):
        s = (m + 16 - k) % 16
        return push(
            pc_here.at[:, :, pl.ds(0, 128)], pc_tok.at[:, s], b_send.at[k], b_recv.at[k], {"mp": s}
        )

    each(1, 16, lambda k: pc_out(k).start())
    pc_tok[:, m] = pc_here[:, :, lanes(m, 128)]

    far_wait(1)
    load_n = [
        local(nall_ref.at[pl.ds(2 * i, 2)], ref.at[pl.ds(0, 1024)].reshape(2, 4, 128, 1024), 2 + i)
        for i, ref in enumerate((back, sib_recv))
    ]
    for copy in load_n:
        copy.start()
    for copy in load_n:
        copy.wait()
    long = pc_here[...].reshape(192, 2048)
    slices[...] = (dot(long[:, :1024], back[:1024]) + dot(long[:, 1024:], sib_recv[:1024])).astype(BF16)

    def share_out(r):
        t = 2 * ((x + r % 4) % 4) + (c + r // 4) % 2
        return push(slices.at[:, lanes(t, 128)], parts.at[r], q_send.at[r], q_recv.at[r], rest(r))

    for r in range(1, 8):
        share_out(r).start()
    spread_wait(3, 0)
    spread_start(3, 1)
    whole = slices[:, lanes(2 * x + c, 128)].astype(F32)
    for r in range(1, 8):
        share_out(r).wait_recv()
    for r in range(1, 8):
        whole += parts[r].astype(F32)
    own_share[...] = whole.astype(BF16).reshape(3, 64, 128)
    lay = local(own_share, full_ref.at[pl.ds(0, 3), c, x, z, y], 2)
    lay.start()
    lay.wait()
    for p in range(3):
        spread_start(p, 0)
    go_home(1)

    each(1, 16, lambda k: pc_in(k).wait_recv())
    for copy in load_q:
        copy.wait()
    dn = sum(dot(rows[i * 1024 : (i + 1) * 1024], pc_tok[i].reshape(1024, 128)) for i in range(3)).T
    hat, scale = unit(x_ref[...].astype(F32))
    gained = dn * gain_ref[...]
    in_ref[...] = mid_cot[...] + scale * (
        gained - hat * jnp.mean(gained * hat, axis=-1, keepdims=True)
    )
    gain_row[...] = jnp.sum(dn * hat, axis=0, keepdims=True)

    def gain_out(k):
        return push(gain_row, gain_mp.at[k], u_send.at[k], u_recv.at[k], mp_at(m, k))

    def gain_far(r):
        return push(gain_mp.at[0], gain_rest.at[r], v_send.at[r], v_recv.at[r], rest(r))

    each(1, 16, lambda k: gain_out(k).start())
    for p in range(3):
        spread_wait(p, 0)
        spread_start(p, 1)
    spread_wait(3, 1)
    spread_start(3, 2)
    go_home(2)

    each(1, 16, lambda k: few_near(k).wait_recv())
    few_all = few_sum[...]
    for k in range(1, 16):
        few_all += few_mp[k]
    few_done[...] = few_all
    few_out_ref[:, lanes(2 * x + c, 128)] = few_all
    for r in range(1, 8):
        few_back(r, False).start()
    for p in range(3):
        spread_wait(p, 1)
        spread_start(p, 2)
    each(1, 16, lambda k: gain_out(k).wait_recv())
    got = gain_row[...]
    for k in range(1, 16):
        got += gain_mp[k]
    gain_mp[0] = got
    for r in range(1, 8):
        gain_far(r).start()
    for r in range(1, 8):
        gain_far(r).wait_recv()
    for r in range(1, 8):
        got += gain_rest[r]
    gain_out_ref[...] = got

    for p in (3, 0, 1, 2):
        spread_wait(p, 2)
        share_twin(p, c).start()
    for i in range(3):
        each_home(lambda at, i=i: home(i, at, at).wait_recv())
    for r in range(1, 8):
        few_back(r, True).wait_recv()
    for p in range(4):
        share_twin(p, 1 - c).wait_recv()

    for p in range(4):
        share_twin(p, c).wait_send()
        for s in range(3):
            for d in (1, 2, 3):
                spread(p, s, d, False).wait_send()
    each(1, 16, lambda k: dispatch(k).wait_send())
    each(1, 16, lambda k: cot_out(k).wait_send())
    each(1, 16, lambda k: pc_out(k).wait_send())
    each(1, 16, lambda k: gain_out(k).wait_send())
    each(1, 16, lambda k: thirty(k).wait_send())
    each(1, 16, lambda k: few_near(k).wait_send())
    for j in (2, 3):
        partials(j).wait_send()
    halves().wait_send()
    for d in (1, 2, 3):
        down_fan(d, x).wait_send()
        quarters(d).wait_send()
    for d in (1, 3):
        for i in range(3):
            relay(i, d).wait_send()
            settle(i, d).wait_send()
        for step in range(2):
            far(0, d, step, m).wait_send()
            far(1, d, step, m).wait_send()
    for r in range(1, 8):
        few_share(r).wait_send()
        few_back(r, False).wait_send()
        share_out(r).wait_send()
        gain_far(r).wait_send()
    for i in range(3):
        each_home(lambda at, i=i: home(i, at, y).wait_send())


def experts_back(*operands):
    dma = pltpu.SemaphoreType.DMA
    vm = pl.BlockSpec(memory_space=VMEM)
    hbm = pl.BlockSpec(memory_space=pl.ANY)
    shape = jax.ShapeDtypeStruct
    width = 4 * DB
    pairs_of = lambda *dims: [dma(dims), dma(dims)]
    return pl.pallas_call(
        experts_back_kernel,
        out_shape=(
            shape((128, 1024), BF16),
            shape((128, 1024), F32),
            shape((1, 1024), F32),
            shape((4, 3, FFB, DB), BF16),
            shape((16, 1024), F32),
            shape((4, 2, 4, 4, 4, 64, 128), BF16),
            shape((16, 2 * ROWS, width), BF16),
            shape((4, 4, 128, 1024), BF16),
        ),
        in_specs=[vm] * 13 + [hbm] * 5,
        out_specs=(vm,) * 5 + (hbm,) * 3,
        scratch_shapes=[
            VMEM((3 * FFQ, width), BF16),
            VMEM((64 * ROWS, width), BF16),
            VMEM((3072, width), BF16),
            VMEM((32 * ROWS, width), BF16),
            VMEM((32 * ROWS, width), BF16),
            VMEM((2, 8 * ROWS, width), BF16),
            VMEM((8 * ROWS, width), F32),
            VMEM((32 * ROWS, FFQ), BF16),
            VMEM((32 * ROWS, FFQ), BF16),
            VMEM((32 * ROWS, FFQ), BF16),
            VMEM((2, 3, FFQ // 2, DB), BF16),
            VMEM((2, 3, FFQ, DB), BF16),
            VMEM((16, 64, 128), BF16),
            VMEM((128, 1024), F32),
            VMEM((16, 1024), F32),
            VMEM((512, 1024), BF16),
            VMEM((4, 512, DB), BF16),
            VMEM((512, DB), BF16),
            VMEM((16, 32, DB), BF16),
            VMEM((64, 128), BF16),
            VMEM((16, 16, 128), F32),
            VMEM((16, 128), F32),
            VMEM((16, 128), F32),
            VMEM((8, 16, 128), F32),
            VMEM((64, 2048), BF16),
            VMEM((2048, 64), BF16),
            VMEM((2048, 64), BF16),
            VMEM((1, 2048), F32),
            VMEM((2048, 64), F32),
            VMEM((2048, 64), F32),
            VMEM((3, 64, 2048), BF16),
            VMEM((3, 16, 64, 128), BF16),
            VMEM((192, 1024), BF16),
            VMEM((3, 64, 128), BF16),
            VMEM((8, 192, 128), BF16),
            VMEM((1, 1024), F32),
            VMEM((16, 1, 1024), F32),
            VMEM((8, 1, 1024), F32),
            dma((8,)),
            *pairs_of(16),
            *pairs_of(16),
            *pairs_of(4),
            *pairs_of(16),
            *pairs_of(4),
            *pairs_of(2, 3, 4),
            *pairs_of(3, 4),
            *pairs_of(2, 2, 4),
            *pairs_of(16),
            *pairs_of(16),
            *pairs_of(8),
            *pairs_of(4, 3, 4),
            *pairs_of(4),
            *pairs_of(16),
            *pairs_of(8),
            *pairs_of(1),
            *pairs_of(4),
            *pairs_of(16),
            *pairs_of(16),
            *pairs_of(2, 8),
        ],
        compiler_params=params(2, 63),
    )(*operands)


def unfold_kernel(f_ref, o_ref, g_ref, qkv_ref, out_ref, gate_ref, up_ref, down_ref):
    qkv_ref[...] = f_ref[...].reshape(3072, 128).astype(F32).T
    for i in range(4):
        for h in range(2):
            part = o_ref[i, :, 32 * h : 32 * (h + 1)].reshape(128, 128)
            out_ref[:, (2 * i + h) * 128 : (2 * i + h + 1) * 128] = part.astype(F32)
    gate_ref[...] = g_ref[0].astype(F32)
    up_ref[...] = g_ref[1].astype(F32)
    down_ref[...] = g_ref[2].astype(F32)


def unfold(full, blocks):
    shape = jax.ShapeDtypeStruct
    share = pl.BlockSpec((None, FFB, 128), lambda i, j: (i, 0, j))
    return pl.pallas_call(
        unfold_kernel,
        out_shape=(
            shape((1024, 3072), F32),
            shape((1024, 1024), F32),
            *[shape((4, FFB, DB), F32)] * 3,
        ),
        grid=(4, 2),
        in_specs=[
            pl.BlockSpec((3, None, None, 4, 4, 64, 128), lambda i, j: (0, j, i, 0, 0, 0, 0)),
            pl.BlockSpec((None, None, 4, None, 4, 64, 128), lambda i, j: (3, j, 0, i, 0, 0, 0)),
            pl.BlockSpec((None, 3, FFB, 128), lambda i, j: (i, 0, 0, j)),
        ],
        out_specs=(
            pl.BlockSpec((128, 3072), lambda i, j: (2 * i + j, 0)),
            pl.BlockSpec((128, 1024), lambda i, j: (4 * j + i, 0)),
            *[share] * 3,
        ),
        compiler_params=pltpu.CompilerParams(vmem_limit_bytes=48 * 1024 * 1024),
    )(full, full, blocks)


def body(
    block_input,
    attn_gain,
    qkv_weight,
    out_weight,
    moe_gain,
    router_weight,
    gate_weight,
    up_weight,
    down_weight,
    routes,
    slot_index,
    cotangent,
):
    pairs = jnp.concatenate([routes.T, slot_index.T, jnp.zeros((4, 128), jnp.int32)]).astype(F32)
    (
        send,
        middle,
        probs,
        ctx_tok,
        qkv,
        ctx_here,
        lse,
        down,
        near,
        weights,
        qkv_low,
        out_low,
    ) = attend(
        block_input,
        attn_gain,
        gate_weight,
        up_weight,
        down_weight,
        moe_gain,
        router_weight,
        pairs,
        cotangent,
        qkv_weight,
        out_weight,
    )
    block_output, input_grad, gain_grad, mine, few, full, _, _ = experts_back(
        middle,
        probs,
        pairs,
        cotangent,
        moe_gain.reshape(1, -1),
        router_weight.T,
        ctx_tok,
        qkv,
        ctx_here,
        lse,
        block_input,
        attn_gain.reshape(1, -1),
        down,
        send,
        weights,
        near,
        qkv_low,
        out_low,
    )
    qkv_grad, out_grad, gate_grad, up_grad, down_grad = unfold(full, mine)
    return (
        block_output,
        input_grad,
        gain_grad.reshape(-1),
        qkv_grad,
        out_grad,
        few[8],
        few[:8].T,
        jnp.swapaxes(gate_grad, 1, 2),
        jnp.swapaxes(up_grad, 1, 2),
        down_grad,
    )


def solution(mesh):
    tokens = P(("dp", "expert", "mp"), None)
    cols = P("expert", "dp", "mp")
    rows = P("expert", "mp", "dp")
    return jax.shard_map(
        body,
        mesh=mesh,
        in_specs=(tokens, P(), P(), P(), P(), P(), cols, cols, rows, tokens, tokens, tokens),
        out_specs=(tokens, tokens, P(), P(), P(), P(), P(), cols, cols, rows),
        check_vma=False,
    )
```

```python
import jax
import jax.numpy as jnp
from jax import lax
from jax.experimental import pallas as pl
from jax.experimental.pallas import tpu as pltpu
from jax.sharding import PartitionSpec as P

EPSILON = 1e-06
HIGHEST = lax.Precision.HIGHEST
MESH = pl.DeviceIdType.MESH
F32 = jnp.float32
BF16 = jnp.bfloat16
VMEM = pltpu.VMEM
ROWS = 40
FFB = 176
FFQ = 704
DB = 256
NT = (((1,), (1,)), ((), ()))
TN = (((0,), (0,)), ((), ()))


def dot(a, b):
    return jnp.dot(a, b, preferred_element_type=F32)


def dot_nt(a, b):
    return lax.dot_general(a, b, NT, preferred_element_type=F32)


def dot_tn(a, b):
    return lax.dot_general(a, b, TN, preferred_element_type=F32)


def spot():
    m = lax.axis_index("mp")
    return lax.axis_index("dp"), lax.axis_index("expert"), m, m // 4, m % 4


def params(cid, mb=60):
    return pltpu.CompilerParams(
        collective_id=cid, has_side_effects=True, vmem_limit_bytes=mb * 1024 * 1024
    )


def swapped(c, z):
    return z % 2, 2 * (z // 2) + c


def mp_at(m, k):
    return {"mp": (m + k) % 16}


def y_at(z, y, d):
    return {"mp": z * 4 + (y + d) % 4}


def z_at(z, y, d):
    return {"mp": ((z + d) % 4) * 4 + y}


def push(src, dst, send, recv, device):
    return pltpu.make_async_remote_copy(
        src_ref=src, dst_ref=dst, send_sem=send, recv_sem=recv, device_id=device, device_id_type=MESH
    )


def lanes(at, size):
    return pl.ds(pl.multiple_of(at * size, size), size)


def greet_mp(barrier, m):
    def one(k, carry):
        pl.semaphore_signal(barrier, inc=1, device_id=mp_at(m, k), device_id_type=MESH)
        return carry

    lax.fori_loop(1, 16, one, 0)


def places(routes, slots):
    return jnp.where(slots < ROWS, routes * (2 * ROWS) + slots, -1.0)


def picks(columns):
    lane = lax.broadcasted_iota(jnp.int32, (128, 8), 1).astype(F32)
    return [(columns[:, j : j + 1] == lane).astype(F32) for j in range(2)]


def gates_of(probs, hot):
    chosen = [jnp.sum(probs * h, axis=1, keepdims=True) for h in hot]
    total = chosen[0] + chosen[1]
    return [v / total for v in chosen], total


def exact(a, b, dims):
    return lax.dot_general(a, b, dims, precision=HIGHEST, preferred_element_type=F32)


def unit(v):
    scale = lax.rsqrt(jnp.mean(v * v, axis=-1, keepdims=True) + EPSILON)
    return v * scale, scale


def attend_kernel(
    x_ref,
    gain_ref,
    gate_ref,
    up_ref,
    downs_ref,
    moe_gain_ref,
    router_ref,
    pairs_ref,
    cot_ref,
    wq_hbm,
    wo_hbm,
    send_ref,
    mid_ref,
    probs_ref,
    ctx_ref,
    qkv_ref,
    ctx_here_ref,
    lse_ref,
    nall_ref,
    w_out_ref,
    wq_out_ref,
    wo_out_ref,
    wq_wide,
    wo_wide,
    wq_ref,
    wo_ref,
    normed,
    heads,
    blocks,
    stage,
    key_rows,
    ctx_low,
    here,
    s_send,
    s_recv,
    x_send,
    x_recv,
    a_send,
    a_recv,
    n_send,
    n_recv,
    c_send,
    c_recv,
):
    x, c, m, z, y = spot()
    pc, pz = swapped(c, z)
    away = (pc - c) * (pc - c)
    barrier = pltpu.get_barrier_semaphore()

    def remote(el):
        return (away == 1) | (el != y)

    def partner(el):
        return {"expert": pc, "mp": pz * 4 + el}

    greet_mp(barrier, m)
    for el in range(4):

        @pl.when(remote(el))
        def _():
            pl.semaphore_signal(barrier, inc=1, device_id=partner(el), device_id_type=MESH)

    for d in range(1, 4):
        pl.semaphore_signal(barrier, inc=1, device_id={"dp": (x + d) % 4}, device_id_type=MESH)

    wide = 512

    def load(i):
        cols = pl.ds(i * wide, wide)
        return pltpu.make_async_copy(wq_hbm.at[:, cols], wq_wide.at[:, cols], here.at[4 + i])

    def save(i):
        cols = pl.ds(i * wide, wide)
        return pltpu.make_async_copy(wq_ref.at[:, cols], wq_out_ref.at[:, cols], here.at[4 + i])

    load_o = pltpu.make_async_copy(wo_hbm, wo_wide, here.at[10])
    save_o = pltpu.make_async_copy(wo_ref, wo_out_ref, here.at[10])
    for i in range(6):
        load(i).start()
    load_o.start()
    for el in range(4):
        blocks[el, 0] = gate_ref[el].astype(BF16)
        blocks[el, 1] = up_ref[el].astype(BF16)
        blocks[el, 2] = downs_ref[el].astype(BF16)
    pl.semaphore_wait(barrier, 15 + 6 + away)

    def units(at):
        return stage.at[:, pl.ds(pl.multiple_of(at * FFB, 16), FFB), :]

    def block(i, el, at):
        return push(
            blocks.at[el, i],
            stage.at[i, pl.ds(pl.multiple_of(at * FFB, 16), FFB), :],
            s_send.at[i, el],
            s_recv.at[i, at],
            partner(el),
        )

    def each_block(f):
        for el in range(4):

            @pl.when(remote(el))
            def _(el=el):
                f(el)

    def blocks_out(i):
        each_block(lambda el: block(i, el, y).start())

    def blocks_in(i):
        each_block(lambda el: block(i, el, el).wait_recv())

    blocks_out(0)

    @pl.when(away == 0)
    def _():
        kept = pltpu.make_async_copy(blocks.at[y], units(y), here.at[2])
        kept.start()
        kept.wait()

    normed[...] = (unit(x_ref[...].astype(F32))[0] * gain_ref[...]).astype(BF16)
    half = 512

    def near(part, d):
        cols = pl.ds(part * half, half)
        device = y_at(z, y, d) if part == 0 else z_at(z, y, d)
        return lambda at: push(
            normed.at[:, cols],
            nall_ref.at[at // 4, at % 4, :, cols],
            n_send.at[part, 0, d],
            n_recv.at[part, 0, d],
            device,
        )

    y_from = [z * 4 + (y + 4 - d) % 4 for d in range(4)]
    z_from = [((z + 4 - d) % 4) * 4 + y for d in range(4)]

    def far(part, d, origin):
        cols = pl.ds(part * half, half)
        if part == 0:
            ref, device = nall_ref.at[origin // 4, :, :, cols], z_at(z, y, d)
        else:
            ref, device = nall_ref.at[:, origin % 4, :, cols], y_at(z, y, d)
        return push(ref, ref, n_send.at[part, 1, d], n_recv.at[part, 1, d], device)

    for i in range(6):
        load(i).wait()
        cols = slice(i * wide, (i + 1) * wide)
        wq_ref[:, cols] = wq_wide[:, cols].astype(BF16)
        save(i).start()
        part = dot(normed[...], wq_ref[:, cols])
        heads[i // 2, (i % 2) * 8 : (i % 2) * 8 + 8] = part.T.astype(BF16).reshape(8, 64, 128)

    def head_out(k):
        t = (m + k) % 16
        return push(
            heads.at[:, t],
            qkv_ref.at[:, :, lanes(m, 128)],
            a_send.at[k],
            a_recv.at[k],
            mp_at(m, k),
        )

    def head_in(k):
        return push(
            heads.at[:, 0],
            qkv_ref.at[:, :, lanes((m + 16 - k) % 16, 128)],
            a_send.at[k],
            a_recv.at[k],
            mp_at(m, k),
        )

    def each(lo, hi, f):
        def one(k, carry):
            f(k)
            return carry

        lax.fori_loop(lo, hi, one, 0)

    each(1, 16, lambda k: head_out(k).start())
    own = pltpu.make_async_copy(heads.at[:, m], qkv_ref.at[:, :, lanes(m, 128)], here.at[0])
    own.start()
    mine = pltpu.make_async_copy(normed, nall_ref.at[z, y], here.at[1])
    mine.start()
    blocks_out(1)
    blocks_out(2)
    for d in (2, 1, 3):
        near(0, d)(m).start()
        near(1, d)(m).start()


    def fan(i, d, step, at):
        rows = pl.ds(0, FFQ) if step == 0 else pl.ds(0 if d == 1 else FFQ // 2, FFQ // 2)
        cols = w_out_ref.at[i, rows, lanes(at, DB)]
        return push(
            stage.at[i] if step == 0 else cols,
            cols,
            x_send.at[i, step, d],
            x_recv.at[i, step, d],
            {"dp": (x + d) % 4},
        )

    def fan_wait(i, step):
        for d in (1, 3):
            fan(i, d, step, (x + 8 - d * (1 + step)) % 4).wait_recv()

    def fan_start(i, step):
        for d in (1, 3):
            fan(i, d, step, x if step == 0 else (x + 4 - d) % 4).start()

    def fan_own(i):
        return pltpu.make_async_copy(stage.at[i], w_out_ref.at[i, :, lanes(x, DB)], here.at[2 + i])

    blocks_in(0)
    fan_start(0, 0)
    fan_own(0).start()
    load_o.wait()
    wo_ref[...] = wo_wide[...].astype(BF16)
    save_o.start()

    own.wait()
    each(1, 16, lambda k: head_in(k).wait_recv())

    key_rows[...] = qkv_ref[1].astype(F32).T.astype(BF16)

    def ctx_out(t):
        return push(
            ctx_low.at[:, lanes(t, 128)],
            ctx_ref.at[pl.ds(pl.multiple_of(m * 64, 64), 64), :],
            c_send.at[(t + 16 - m) % 16],
            c_recv.at[(t + 16 - m) % 16],
            {"mp": t},
        )

    def ctx_in(k):
        s = (m + 16 - k) % 16
        return push(
            ctx_low.at[:, pl.ds(0, 128)],
            ctx_ref.at[pl.ds(pl.multiple_of(s * 64, 64), 64), :],
            c_send.at[k],
            c_recv.at[k],
            {"mp": s},
        )

    def queries(i):
        b = (m // 2 + i) % 8
        cols = lanes(b, 256)
        q = (qkv_ref[0, :, cols].astype(F32) * 0.125).astype(BF16)
        s = dot(key_rows[...], q)
        top = jnp.max(s, axis=0, keepdims=True)
        p = jnp.exp(s - top)
        total = jnp.sum(p, axis=0, keepdims=True)
        ctx = dot(qkv_ref[2], p.astype(BF16)) / total
        lse_ref[:, cols] = top + jnp.log(total)
        ctx_here_ref[:, cols] = ctx
        ctx_low[:, cols] = ctx.astype(BF16)

    def pair(i, carry):
        queries(2 * i)
        queries(2 * i + 1)
        for u in range(2):
            b = (m // 2 + 2 * i + u) % 8
            for v in range(2):
                t = 2 * b + v

                @pl.when(t != m)
                def _():
                    ctx_out(t).start()

        @pl.when(i == 0)
        def _():
            blocks_in(1)
            fan_start(1, 0)
            fan_own(1).start()

        @pl.when(i == 1)
        def _():
            fan_wait(0, 0)
            fan_start(0, 1)
            blocks_in(2)
            fan_start(2, 0)
            fan_own(2).start()

        return carry

    lax.fori_loop(0, 4, pair, 0)
    for d in (1, 2, 3):
        near(0, d)(y_from[d]).wait_recv()
        near(1, d)(z_from[d]).wait_recv()
    mine.wait()
    for d in (1, 3):
        far(0, d, m).start()
        far(1, d, m).start()
    ctx_ref[pl.ds(pl.multiple_of(m * 64, 64), 64), :] = ctx_low[:, lanes(m, 128)]
    each(1, 16, lambda k: ctx_in(k).wait_recv())

    fan_wait(1, 0)
    fan_start(1, 1)

    mid = x_ref[...].astype(F32) + dot_tn(ctx_ref[...], wo_ref[...])
    mid_ref[...] = mid
    moe_in = unit(mid)[0] * moe_gain_ref[...]
    logits = exact(moe_in, router_ref[...], NT)
    grown = jnp.exp(logits - jnp.max(logits, axis=1, keepdims=True))
    probs = grown / jnp.sum(grown, axis=1, keepdims=True)
    probs_ref[...] = probs
    gates, _ = gates_of(probs, picks(pairs_ref[...].T))
    upstream = cot_ref[...].astype(F32)
    rows = [moe_in.astype(BF16)] + [(g * upstream).astype(BF16) for g in gates]
    row = lax.broadcasted_iota(jnp.int32, (16 * ROWS, 128), 0).astype(F32)
    at = [places(pairs_ref[j : j + 1], pairs_ref[2 + j : 3 + j]) for j in range(2)]
    hot = [((row == at[0]) | (row == at[1]))] + [row == jnp.where(a < 0, a, a + ROWS) for a in at]
    hot = jnp.concatenate([h.astype(F32) for h in hot], axis=1).astype(BF16)
    sent = dot(hot, jnp.concatenate(rows, axis=0))
    send_ref[...] = sent.astype(BF16).reshape(8, 2 * ROWS, 1024)

    for i in range(6):
        save(i).wait()
    save_o.wait()
    fan_wait(0, 1)
    fan_wait(2, 0)
    fan_start(2, 1)
    fan_wait(1, 1)
    fan_wait(2, 1)
    for d in (1, 3):
        far(0, d, z_from[d]).wait_recv()
        far(1, d, y_from[d]).wait_recv()
    for d in (1, 2, 3):
        near(0, d)(m).wait_send()
        near(1, d)(m).wait_send()
    for d in (1, 3):
        far(0, d, m).wait_send()
        far(1, d, m).wait_send()
    for i in range(3):
        fan_own(i).wait()
        for d in (1, 3):
            for step in range(2):
                fan(i, d, step, x).wait_send()
    each(1, 16, lambda k: head_out(k).wait_send())
    each(1, 16, lambda k: ctx_in(k).wait_send())
    for i in range(3):
        each_block(lambda el, i=i: block(i, el, y).wait_send())


def attend(
    block_input,
    gain,
    gate_weight,
    up_weight,
    down_weight,
    moe_gain,
    router,
    pairs,
    cotangent,
    qkv_weight,
    out_weight,
):
    dma = pltpu.SemaphoreType.DMA
    vm = pl.BlockSpec(memory_space=VMEM)
    hbm = pl.BlockSpec(memory_space=pl.ANY)
    shape = jax.ShapeDtypeStruct
    return pl.pallas_call(
        attend_kernel,
        out_shape=(
            shape((8, 2 * ROWS, 1024), BF16),
            shape((128, 1024), F32),
            shape((128, 8), F32),
            shape((1024, 128), BF16),
            shape((3, 64, 2048), BF16),
            shape((64, 2048), F32),
            shape((1, 2048), F32),
            shape((4, 4, 128, 1024), BF16),
            shape((3, FFQ, 4 * DB), BF16),
            shape((1024, 3072), BF16),
            shape((1024, 1024), BF16),
        ),
        in_specs=[vm] * 9 + [hbm] * 2,
        out_specs=(vm,) * 7 + (hbm,) * 4,
        scratch_shapes=[
            VMEM((1024, 3072), F32),
            VMEM((1024, 1024), F32),
            VMEM((1024, 3072), BF16),
            VMEM((1024, 1024), BF16),
            VMEM((128, 1024), BF16),
            VMEM((3, 16, 64, 128), BF16),
            VMEM((4, 3, FFB, DB), BF16),
            VMEM((3, FFQ, DB), BF16),
            VMEM((2048, 64), BF16),
            VMEM((64, 2048), BF16),
            dma((11,)),
            dma((3, 4)),
            dma((3, 4)),
            dma((3, 2, 4)),
            dma((3, 2, 4)),
            dma((16,)),
            dma((16,)),
            dma((2, 2, 4)),
            dma((2, 2, 4)),
            dma((16,)),
            dma((16,)),
        ],
        compiler_params=params(1, 62),
    )(
        block_input,
        gain.reshape(1, -1),
        jnp.swapaxes(gate_weight, 1, 2),
        jnp.swapaxes(up_weight, 1, 2),
        down_weight,
        moe_gain.reshape(1, -1),
        router.T,
        pairs,
        cotangent,
        qkv_weight,
        out_weight,
    )


GELU_A = 0.7978845608
GELU_B = 0.044715


def experts_back_kernel(
    mid_ref,
    probs_ref,
    pairs_ref,
    cot_ref,
    moe_gain_ref,
    router_ref,
    tok_ref,
    qkv_ref,
    ctx_ref,
    lse_ref,
    x_ref,
    gain_ref,
    send_hbm,
    w_hbm,
    near_hbm,
    wq_hbm,
    wo_hbm,
    y_ref,
    in_ref,
    gain_out_ref,
    g_out_ref,
    few_out_ref,
    full_ref,
    ret_ref,
    nall_ref,
    weights,
    recv,
    rows,
    back,
    sib_recv,
    sib_send,
    own_part,
    hid,
    gcs,
    ucs,
    g_relay,
    g_near,
    dctx,
    few,
    o_sib,
    o_x,
    o_q,
    o_mp,
    few_mp,
    few_sum,
    few_done,
    few_rest,
    cot,
    key_values,
    row_dot,
    dkv,
    pc_here,
    pc_tok,
    slices,
    share,
    parts,
    gain_row,
    gain_mp,
    gain_rest,
    here,
    d_send,
    d_recv,
    f_send,
    f_recv,
    p_send,
    p_recv,
    r_send,
    r_recv,
    x_send,
    x_recv,
    s_send,
    s_recv,
    n_send,
    n_recv,
    a_send,
    a_recv,
    b_send,
    b_recv,
    q_send,
    q_recv,
    g_send,
    g_recv,
    t_send,
    t_recv,
    u_send,
    u_recv,
    v_send,
    v_recv,
    o_send,
    o_recv,
    ox_send,
    ox_recv,
    om_send,
    om_recv,
    fm_send,
    fm_recv,
    fr_send,
    fr_recv,
):
    x, c, m, z, y = spot()
    pc, pz = swapped(c, z)
    away = (pc - c) * (pc - c)
    barrier = pltpu.get_barrier_semaphore()

    def remote(el):
        return (away == 1) | (el != y)

    def partner(el):
        return {"expert": pc, "mp": pz * 4 + el}

    def rest(r):
        return {"dp": (x + r % 4) % 4, "expert": (c + r // 4) % 2}

    def each(lo, hi, f):
        def one(k, carry):
            f(k)
            return carry

        lax.fori_loop(lo, hi, one, 0)

    def local(src, dst, i):
        return pltpu.make_async_copy(src, dst, here.at[i])

    twin = {"expert": 1 - c}
    size = 2 * ROWS

    greet_mp(barrier, m)
    for el in range(4):

        @pl.when(remote(el))
        def _():
            pl.semaphore_signal(barrier, inc=1, device_id=partner(el), device_id_type=MESH)

    for r in range(1, 8):
        pl.semaphore_signal(barrier, inc=1, device_id=rest(r), device_id_type=MESH)
    load_w = [local(w_hbm.at[i], weights.at[pl.ds(i * FFQ, FFQ)], i) for i in range(3)]
    for copy in load_w:
        copy.start()
    near = []
    for i, d in enumerate((0, 1, 3)):
        at = (z + d) % 4, slice(None), slice(None), pl.ds(0, 512)
        near.append(local(near_hbm.at[at], nall_ref.at[at], 8 + i))
        at = slice(None), (y + d) % 4, slice(None), pl.ds(512, 512)
        near.append(local(near_hbm.at[at], nall_ref.at[at], 11 + i))
    for copy in near:
        copy.start()
    pl.semaphore_wait(barrier, 15 + 3 + away + 7)

    def expert_of(t):
        return ((t // 4) % 2) * 4 + t % 4

    def slot(core, k, n=1):
        return pl.ds(pl.multiple_of((core * 16 + k) * size, size), n * size)

    def dispatch(k):
        t = (m + k) % 16
        return push(
            send_hbm.at[expert_of(t)],
            recv.at[slot(0, k)],
            d_send.at[k],
            d_recv.at[k],
            {"mp": t},
        )

    def forward(k):
        return push(recv.at[slot(0, k)], recv.at[slot(1, k)], f_send.at[k], f_recv.at[k], twin)

    def partials(j):
        return push(
            sib_send.at[j % 2],
            sib_recv.at[pl.ds(pl.multiple_of(j * 4 * size, size), 4 * size)],
            p_send.at[j],
            p_recv.at[j],
            twin,
        )

    def spot_of(k, n=1):
        return pl.ds(pl.multiple_of(k * size, size), n * size)

    def giving(k, at):
        return push(
            back.at[spot_of(k)], ret_ref.at[at], r_send.at[k], r_recv.at[k], mp_at(m, 16 - k)
        )

    each(1, 16, lambda k: dispatch(k).start())
    own = local(send_hbm.at[expert_of(m)], recv.at[slot(0, 0)], 4)
    own.start()
    own.wait()

    def finish(j):
        partials(j).wait_recv()
        span = spot_of(4 * j, 4)
        back[span] = (own_part[...] + sib_recv[span].astype(F32)).astype(BF16)
        for i in range(4):
            k = 4 * j + i

            @pl.when(k > 0)
            def _():
                giving(k, m).start()

            @pl.when(k == 0)
            def _():
                local(back.at[spot_of(0)], ret_ref.at[m], 4).start()

    gate_w, up_w, down_w = (slice(i * FFQ, (i + 1) * FFQ) for i in range(3))
    cot_rows = 32 * ROWS

    def chunk(j, carry):
        for i in range(4):
            k = 4 * j + i

            @pl.when(k > 0)
            def _():
                dispatch(k).wait_recv()

            forward(k).start()

        @pl.when(j > 0)
        def _():
            finish(j - 1)

        @pl.when(j == 0)
        def _():
            for copy in load_w:
                copy.wait()

        for i in range(4):
            forward(4 * j + i).wait_recv()
        xs = pl.ds(pl.multiple_of(j * 8 * ROWS, 16), 8 * ROWS)
        cs = pl.ds(pl.multiple_of(cot_rows + j * 8 * ROWS, 16), 8 * ROWS)
        for r in range(2):
            blk = recv[slot(r, 4 * j, 4)].astype(F32).reshape(4, size, 4 * DB)
            for at, part in ((0, blk[:, :ROWS]), (cot_rows, blk[:, ROWS:])):
                span = pl.ds(pl.multiple_of(at + (2 * j + r) * 4 * ROWS, 16), 4 * ROWS)
                rows[span] = part.reshape(4 * ROWS, 4 * DB).astype(BF16)
        gate = dot_nt(rows[xs], weights[gate_w])
        up = dot_nt(rows[xs], weights[up_w])
        hid_cot = dot_nt(rows[cs], weights[down_w])
        sq = gate * gate
        th = jnp.tanh(GELU_A * (gate + GELU_B * (gate * sq)))
        half = 0.5 * (1.0 + th)
        act = gate * half
        slope = half + 0.5 * gate * (1.0 - th * th) * (GELU_A * (1.0 + 3.0 * GELU_B * sq))
        hid[xs] = (act * up).astype(BF16)
        gcs[xs] = (hid_cot * up * slope).astype(BF16)
        ucs[xs] = (hid_cot * act).astype(BF16)
        out = dot(hid[xs], weights[down_w]).reshape(2, 4, ROWS, 4 * DB)
        low = dot(gcs[xs], weights[gate_w]) + dot(ucs[xs], weights[up_w])
        low = low.reshape(2, 4, ROWS, 4 * DB)
        own_part[...] = jnp.concatenate([out[0], low[0]], axis=1).reshape(4 * size, 4 * DB)

        @pl.when(j > 1)
        def _():
            partials(j - 2).wait_send()

        sib_send[j % 2] = (
            jnp.concatenate([out[1], low[1]], axis=1).reshape(4 * size, 4 * DB).astype(BF16)
        )
        partials(j).start()
        return carry

    lax.fori_loop(0, 4, chunk, 0)
    finish(3)
    each(0, 16, lambda k: forward(k).wait_send())
    load_o = local(wo_hbm, weights.at[pl.ds(0, 1024)], 0)
    load_o.start()

    unit_half = FFQ // 2

    def unit_rows(i, d):
        return pl.ds(i * FFQ + (0 if d == 1 else unit_half), unit_half)

    def relay(i, d):
        return push(
            recv.at[unit_rows(i, d), lanes((x + 2) % 4, DB)],
            g_relay.at[d // 2, i],
            x_send.at[0, i, d],
            x_recv.at[0, i, d],
            {"dp": (x + d) % 4},
        )

    def settle(i, d):
        return push(
            recv.at[pl.ds(i * FFQ, FFQ), lanes((x + d) % 4, DB)],
            g_near.at[d // 2, i],
            x_send.at[1, i, d],
            x_recv.at[1, i, d],
            {"dp": (x + d) % 4},
        )

    for i, (a, at) in enumerate(((gcs, 0), (ucs, 0), (hid, cot_rows))):
        g = dot_tn(a[...], rows[at : at + cot_rows])
        recv[i * FFQ : (i + 1) * FFQ] = g.astype(BF16)
        for d in (1, 3):
            relay(i, d).start()
    load_q = [
        local(wq_hbm.at[:, pl.ds(i * 1024, 1024)], rows.at[pl.ds(i * 1024, 1024)], 5 + i)
        for i in range(3)
    ]
    for copy in load_q:
        copy.start()
    for i in range(3):
        for d in (1, 3):
            relay(i, d).wait_recv()
            span, cols = unit_rows(i, d), lanes((x + d) % 4, DB)
            recv[span, cols] = (
                recv[span, cols].astype(F32) + g_relay[d // 2, i].astype(F32)
            ).astype(BF16)
            settle(i, d).start()

    def home(i, at, to):
        return push(
            recv.at[pl.ds(i * FFQ + at * FFB, FFB), lanes(x, DB)],
            g_out_ref.at[to, i],
            s_send.at[i, at],
            s_recv.at[i, to],
            partner(at),
        )

    def each_home(f):
        for at in range(4):

            @pl.when(remote(at))
            def _(at=at):
                f(at)

    def go_home(i):
        for d in (1, 3):
            settle(i, d).wait_recv()
        span, cols = pl.ds(i * FFQ, FFQ), lanes(x, DB)
        recv[span, cols] = (
            recv[span, cols].astype(F32) + g_near[0, i].astype(F32) + g_near[1, i].astype(F32)
        ).astype(BF16)
        each_home(lambda at: home(i, at, y).start())

        @pl.when(away == 0)
        def _():
            kept = local(
                recv.at[pl.ds(pl.multiple_of(i * FFQ + y * FFB, 16), FFB), cols], g_out_ref.at[y, i], 1
            )
            kept.start()
            kept.wait()

    local(back.at[spot_of(0)], ret_ref.at[m], 4).wait()
    each(1, 16, lambda k: giving(k, (m + k) % 16).wait())
    load_r = local(ret_ref, back.reshape(16, size, 4 * DB), 4)
    load_r.start()
    load_r.wait()

    for copy in near:
        copy.wait()

    def far(part, d, hops):
        cols, some = pl.ds(part * 512, 512), pl.ds(0 if d == 1 else 2, 2)
        if part == 0:
            ref, device = nall_ref.at[(z + 8 - hops * d) % 4, some, :, cols], z_at(z, y, d)
        else:
            ref, device = nall_ref.at[some, (y + 8 - hops * d) % 4, :, cols], y_at(z, y, d)
        return push(ref, ref, n_send.at[part, d], n_recv.at[part, d], device)

    columns = pairs_ref[...].T
    hot = picks(columns)
    probs = probs_ref[...]
    gates, total = gates_of(probs, hot)
    at = places(columns[:, 0:2], columns[:, 2:4])
    lane = lax.broadcasted_iota(jnp.int32, (128, 16 * ROWS), 1).astype(F32)
    at = [at[:, j : j + 1] for j in range(2)]
    given = (back[: 8 * size].astype(F32) + back[8 * size :].astype(F32)).astype(BF16)
    fetched = [dot((lane == a).astype(F32).astype(BF16), given) for a in at]
    low = [lane == jnp.where(a < 0, a, a + ROWS) for a in at]
    moe_cot = dot((low[0] | low[1]).astype(F32).astype(BF16), given)
    mid = mid_ref[...]
    upstream = cot_ref[...].astype(F32)
    y_ref[...] = (mid + gates[0] * fetched[0] + gates[1] * fetched[1]).astype(BF16)
    gate_cot = [jnp.sum(upstream * f, axis=1, keepdims=True) for f in fetched]
    inner = gate_cot[0] * gates[0] + gate_cot[1] * gates[1]
    probs_cot = sum(h * ((g - inner) / total) for h, g in zip(hot, gate_cot))
    logit_cot = probs * (probs_cot - jnp.sum(probs * probs_cot, axis=1, keepdims=True))
    hat, scale = unit(mid)
    moe_cot += exact(logit_cot, router_ref[...], (((1,), (0,)), ((), ())))
    few[:8] = exact(logit_cot, hat * moe_gain_ref[...], TN)
    few[8:] = jnp.concatenate(
        [jnp.sum(moe_cot * hat, axis=0, keepdims=True), jnp.zeros((7, 1024), F32)], axis=0
    )
    gained = moe_cot * moe_gain_ref[...]
    in_ref[...] = upstream + scale * (gained - hat * jnp.mean(gained * hat, axis=-1, keepdims=True))
    branch_cot = in_ref[...].astype(BF16)
    load_o.wait()
    dctx[...] = dot_nt(weights[:1024], branch_cot).astype(BF16).reshape(16, 64, 128)

    def cot_out(k):
        t = (m + k) % 16
        return push(dctx.at[t], cot.at[:, lanes(m, 128)], a_send.at[k], a_recv.at[k], {"mp": t})

    def cot_in(k):
        s = (m + 16 - k) % 16
        return push(dctx.at[0], cot.at[:, lanes(s, 128)], a_send.at[k], a_recv.at[k], {"mp": s})

    each(1, 16, lambda k: cot_out(k).start())
    for d in (1, 3):
        far(0, d, 1).start()
        far(1, d, 1).start()
    cot[:, lanes(m, 128)] = dctx[m]

    weights[1024:2048] = dot(tok_ref[...], branch_cot).astype(BF16)

    def halves():
        rows_at = pl.ds(pl.multiple_of(1024 + (1 - c) * 512, 512), 512)
        return push(weights.at[rows_at], o_sib, o_send.at[0], o_recv.at[0], twin)

    def quarters(d):
        t = (x + d) % 4
        return push(
            weights.at[pl.ds(0, 512), lanes(t, DB)], o_x.at[d - 1], ox_send.at[d], ox_recv.at[d], {"dp": t}
        )

    def thirty(k):
        t = (m + k) % 16
        return push(
            o_q.at[pl.ds(pl.multiple_of(t * 32, 32), 32)],
            o_mp.at[k],
            om_send.at[k],
            om_recv.at[k],
            {"mp": t},
        )

    def few_share(r):
        t = 2 * ((x + r % 4) % 4) + (c + r // 4) % 2
        return push(
            few.at[:, lanes(t, 128)], few_rest.at[r], fr_send.at[0, r], fr_recv.at[0, r], rest(r)
        )

    def few_near(k):
        return push(few_sum, few_mp.at[k], fm_send.at[k], fm_recv.at[k], mp_at(m, k))

    def few_back(r, back_from):
        t = 2 * ((x + 4 - r % 4) % 4) + (c + r // 4) % 2 if back_from else 2 * x + c
        return push(
            few_done, few_out_ref.at[:, lanes(t, 128)], fr_send.at[1, r], fr_recv.at[1, r], rest(r)
        )

    halves().start()
    for r in range(1, 8):
        few_share(r).start()

    def along(axis, d):
        if axis == 0:
            return {"dp": (x + d) % 4}
        return z_at(z, y, d) if axis == 1 else y_at(z, y, d)

    orders = ((0, 2, 1), (1, 0, 2), (2, 1, 0), (0, 2, 1), (0, 1, 2))
    spans = [pl.ds(0, 64), pl.ds(64, 64), pl.ds(128, 64), pl.ds(192, 32), pl.ds(224, 32)]

    def spread(p, s, d, incoming):
        at = [x, z, y]
        axis = orders[p][s]
        if incoming:
            at[axis] = (at[axis] + 4 - d) % 4
        src = [x, z, y]
        for done in orders[p][:s]:
            at[done] = slice(None)
            src[done] = slice(None)
        return push(
            full_ref.at[(c, *src, spans[p])],
            full_ref.at[(c, *at, spans[p])],
            g_send.at[p, s, d],
            g_recv.at[p, s, d],
            along(axis, d),
        )

    def spread_start(p, s):
        for d in (2, 1, 3):
            spread(p, s, d, False).start()

    def last(p, d, hops):
        at = [slice(None)] * 3
        axis = orders[p][2]
        at[axis] = ((x, z, y)[axis] + 8 - hops * d) % 4
        return at

    def circle(p, d, step, incoming):
        at = last(p, d, step + incoming)
        if step:
            at[orders[p][0]] = pl.ds(0 if d == 1 else 2, 2)
        ref = full_ref.at[(c, *at, spans[p])]
        return push(ref, ref, g_send.at[p, 2 + step, d], g_recv.at[p, 2 + step, d], along(orders[p][2], d))

    def spread_wait(p, s):
        for d in (1, 2, 3):
            spread(p, s, d, True).wait_recv()

    def share_twin(p, i, core):
        d, hops = ((1, 0), (1, 1), (3, 1), (1, 2), (3, 2))[i]
        at = last(p, d, hops)
        if hops == 2:
            at[orders[p][0]] = pl.ds(0 if d == 1 else 2, 2)
        ref = full_ref.at[(core, *at, spans[p])]
        return push(ref, ref, t_send.at[p, i], t_recv.at[p, i], twin)

    key_values[...] = qkv_ref[1:].reshape(128, 2048).astype(F32).T.astype(BF16)
    dkv[...] = jnp.zeros_like(dkv)
    halves().wait_recv()
    weights[:512] = (
        weights[pl.ds(pl.multiple_of(1024 + c * 512, 512), 512)].astype(F32) + o_sib[...].astype(F32)
    ).astype(BF16)
    for d in (2, 1, 3):
        quarters(d).start()
    go_home(0)
    each(1, 16, lambda k: cot_in(k).wait_recv())
    row_dot[...] = jnp.sum(cot[...].astype(F32) * ctx_ref[...], axis=0, keepdims=True)

    def queries(b):
        cols = lanes(b, 256)
        q = (qkv_ref[0, :, cols].astype(F32) * 0.125).astype(BF16)
        none = jnp.zeros((64, 256), BF16)
        q = jnp.concatenate([q, none], axis=0)
        g = jnp.concatenate([none, cot[:, cols]], axis=0)
        p = jnp.exp(dot(key_values[...], q) - lse_ref[:, cols])
        dp = dot(key_values[...], g)
        ds = (p * (dp - row_dot[:, cols])).astype(BF16)
        pc_here[0, :, cols] = (dot(qkv_ref[1], ds) * 0.125).astype(BF16)
        dkv[...] += dot_nt(ds, q) + dot_nt(p.astype(BF16), g)

    def pair(i, carry):
        queries(2 * i)
        queries(2 * i + 1)

        @pl.when(i == 1)
        def _():
            go_home(1)

        @pl.when(i == 2)
        def _():
            for d in (1, 2, 3):
                quarters(d).wait_recv()
            o_sum = weights[:512, lanes(x, DB)].astype(F32)
            for d in (1, 2, 3):
                o_sum += o_x[d - 1].astype(F32)
            o_q[...] = o_sum.astype(BF16)
            each(1, 16, lambda k: thirty(k).start())
            few_all = few[:, lanes(2 * x + c, 128)]
            for r in range(1, 8):
                few_share(r).wait_recv()
                few_all += few_rest[r]
            few_sum[...] = few_all
            each(1, 16, lambda k: few_near(k).start())
            go_home(2)

        return carry

    lax.fori_loop(0, 4, pair, 0)
    pc_here[1:] = dkv[...].T.astype(BF16).reshape(2, 64, 2048)

    def pc_out(k):
        t = (m + k) % 16
        return push(
            pc_here.at[:, :, lanes(t, 128)], pc_tok.at[:, m], b_send.at[k], b_recv.at[k], {"mp": t}
        )

    def pc_in(k):
        s = (m + 16 - k) % 16
        return push(
            pc_here.at[:, :, pl.ds(0, 128)], pc_tok.at[:, s], b_send.at[k], b_recv.at[k], {"mp": s}
        )

    each(1, 16, lambda k: pc_out(k).start())
    pc_tok[:, m] = pc_here[:, :, lanes(m, 128)]

    for d in (1, 3):
        far(0, d, 2).wait_recv()
        far(1, d, 2).wait_recv()
    long = pc_here[...].reshape(192, 2048)
    slices[...] = dot(long, nall_ref[...].reshape(2048, 1024)).astype(BF16)

    def share_out(r):
        t = 2 * ((x + r % 4) % 4) + (c + r // 4) % 2
        return push(slices.at[:, lanes(t, 128)], parts.at[r], q_send.at[r], q_recv.at[r], rest(r))

    for r in range(1, 8):
        share_out(r).start()
    whole = slices[:, lanes(2 * x + c, 128)].astype(F32)
    for r in range(1, 8):
        share_out(r).wait_recv()
    for r in range(1, 8):
        whole += parts[r].astype(F32)
    share[:192] = whole.astype(BF16)
    lay = local(share.at[pl.ds(0, 192)], full_ref.at[c, x, z, y, pl.ds(0, 192)], 2)
    lay.start()
    lay.wait()
    for p in range(3):
        spread_start(p, 0)
    each(1, 16, lambda k: thirty(k).wait_recv())
    o_sum = o_q[pl.ds(pl.multiple_of(m * 32, 32), 32)].astype(F32)
    for k in range(1, 16):
        o_sum += o_mp[k].astype(F32)
    o_low = o_sum.astype(BF16)
    share[192:224] = o_low[:, :128]
    share[224:] = o_low[:, 128:]
    lay = local(share.at[pl.ds(192, 64)], full_ref.at[c, x, z, y, pl.ds(192, 64)], 2)
    lay.start()
    lay.wait()
    for p in (3, 4):
        spread_start(p, 0)

    def circles(p):
        spread_wait(p, 1)
        for d in (1, 3):
            circle(p, d, 0, 0).start()
        share_twin(p, 0, c).start()

    for p in range(3):
        spread_wait(p, 0)
        spread_start(p, 1)
    for p in range(3):
        circles(p)
    for p in (3, 4):
        spread_wait(p, 0)
        spread_start(p, 1)

    each(1, 16, lambda k: pc_in(k).wait_recv())
    for copy in load_q:
        copy.wait()
    dn = sum(dot(rows[i * 1024 : (i + 1) * 1024], pc_tok[i].reshape(1024, 128)) for i in range(3)).T
    hat, scale = unit(x_ref[...].astype(F32))
    gained = dn * gain_ref[...]
    in_ref[...] = in_ref[...] + scale * (
        gained - hat * jnp.mean(gained * hat, axis=-1, keepdims=True)
    )
    gain_row[...] = jnp.sum(dn * hat, axis=0, keepdims=True)

    def gain_out(k):
        return push(gain_row, gain_mp.at[k], u_send.at[k], u_recv.at[k], mp_at(m, k))

    def gain_far(r):
        return push(gain_mp.at[0], gain_rest.at[r], v_send.at[r], v_recv.at[r], rest(r))

    each(1, 16, lambda k: gain_out(k).start())
    for p in (3, 4):
        circles(p)

    def onward(p):
        for i, d in ((1, 1), (2, 3)):
            circle(p, d, 0, 1).wait_recv()
            circle(p, d, 1, 0).start()
            share_twin(p, i, c).start()

    for p in range(3):
        onward(p)
    each(1, 16, lambda k: gain_out(k).wait_recv())
    got = gain_row[...]
    for k in range(1, 16):
        got += gain_mp[k]
    gain_mp[0] = got
    for r in range(1, 8):
        gain_far(r).start()
    for p in (3, 4):
        onward(p)
    each(1, 16, lambda k: few_near(k).wait_recv())
    few_all = few_sum[...]
    for k in range(1, 16):
        few_all += few_mp[k]
    few_done[...] = few_all
    few_out_ref[:, lanes(2 * x + c, 128)] = few_all
    for r in range(1, 8):
        few_back(r, False).start()
    for p in range(5):
        for i, d in ((3, 1), (4, 3)):
            circle(p, d, 1, 1).wait_recv()
            share_twin(p, i, c).start()
    for r in range(1, 8):
        gain_far(r).wait_recv()
    for r in range(1, 8):
        got += gain_rest[r]
    gain_out_ref[...] = got
    for i in range(3):
        each_home(lambda at, i=i: home(i, at, at).wait_recv())
    for r in range(1, 8):
        few_back(r, True).wait_recv()
    for p in range(5):
        for i in range(5):
            share_twin(p, i, 1 - c).wait_recv()

    for p in range(5):
        for i in range(5):
            share_twin(p, i, c).wait_send()
        for d in (1, 2, 3):
            spread(p, 0, d, False).wait_send()
            spread(p, 1, d, False).wait_send()
        for d in (1, 3):
            circle(p, d, 0, 0).wait_send()
            circle(p, d, 1, 0).wait_send()
    each(1, 16, lambda k: dispatch(k).wait_send())
    each(1, 16, lambda k: cot_out(k).wait_send())
    each(1, 16, lambda k: pc_out(k).wait_send())
    each(1, 16, lambda k: gain_out(k).wait_send())
    each(1, 16, lambda k: thirty(k).wait_send())
    each(1, 16, lambda k: few_near(k).wait_send())
    for j in (2, 3):
        partials(j).wait_send()
    halves().wait_send()
    for d in (1, 2, 3):
        quarters(d).wait_send()
    for d in (1, 3):
        for i in range(3):
            relay(i, d).wait_send()
            settle(i, d).wait_send()
        far(0, d, 1).wait_send()
        far(1, d, 1).wait_send()
    for r in range(1, 8):
        few_share(r).wait_send()
        few_back(r, False).wait_send()
        share_out(r).wait_send()
        gain_far(r).wait_send()
    for i in range(3):
        each_home(lambda at, i=i: home(i, at, y).wait_send())


def experts_back(*operands):
    dma = pltpu.SemaphoreType.DMA
    vm = pl.BlockSpec(memory_space=VMEM)
    hbm = pl.BlockSpec(memory_space=pl.ANY)
    shape = jax.ShapeDtypeStruct
    width = 4 * DB
    pairs_of = lambda *dims: [dma(dims), dma(dims)]
    return pl.pallas_call(
        experts_back_kernel,
        out_shape=(
            shape((128, 1024), BF16),
            shape((128, 1024), F32),
            shape((1, 1024), F32),
            shape((4, 3, FFB, DB), BF16),
            shape((16, 1024), F32),
            shape((2, 4, 4, 4, 256, 128), BF16),
            shape((16, 2 * ROWS, width), BF16),
        ),
        in_specs=[vm] * 12 + [hbm] * 5,
        out_specs=(vm,) * 3 + (hbm, vm, vm, hbm),
        scratch_shapes=[
            VMEM((4, 4, 128, 1024), BF16),
            VMEM((3 * FFQ, width), BF16),
            VMEM((64 * ROWS, width), BF16),
            VMEM((3072, width), BF16),
            VMEM((32 * ROWS, width), BF16),
            VMEM((32 * ROWS, width), BF16),
            VMEM((2, 8 * ROWS, width), BF16),
            VMEM((8 * ROWS, width), F32),
            VMEM((32 * ROWS, FFQ), BF16),
            VMEM((32 * ROWS, FFQ), BF16),
            VMEM((32 * ROWS, FFQ), BF16),
            VMEM((2, 3, FFQ // 2, DB), BF16),
            VMEM((2, 3, FFQ, DB), BF16),
            VMEM((16, 64, 128), BF16),
            VMEM((16, 1024), F32),
            VMEM((512, 1024), BF16),
            VMEM((3, 512, DB), BF16),
            VMEM((512, DB), BF16),
            VMEM((16, 32, DB), BF16),
            VMEM((16, 16, 128), F32),
            VMEM((16, 128), F32),
            VMEM((16, 128), F32),
            VMEM((8, 16, 128), F32),
            VMEM((64, 2048), BF16),
            VMEM((2048, 128), BF16),
            VMEM((1, 2048), F32),
            VMEM((2048, 128), F32),
            VMEM((3, 64, 2048), BF16),
            VMEM((3, 16, 64, 128), BF16),
            VMEM((192, 1024), BF16),
            VMEM((256, 128), BF16),
            VMEM((8, 192, 128), BF16),
            VMEM((1, 1024), F32),
            VMEM((16, 1, 1024), F32),
            VMEM((8, 1, 1024), F32),
            dma((14,)),
            *pairs_of(16),
            *pairs_of(16),
            *pairs_of(4),
            *pairs_of(16),
            *pairs_of(2, 3, 4),
            *pairs_of(3, 4),
            *pairs_of(2, 4),
            *pairs_of(16),
            *pairs_of(16),
            *pairs_of(8),
            *pairs_of(5, 4, 4),
            *pairs_of(5, 5),
            *pairs_of(16),
            *pairs_of(8),
            *pairs_of(1),
            *pairs_of(4),
            *pairs_of(16),
            *pairs_of(16),
            *pairs_of(2, 8),
        ],
        compiler_params=params(2, 63),
    )(*operands)


def unfold_kernel(
    f_ref, o_ref, g_ref, few_ref, qkv_ref, out_ref, gate_ref, up_ref, down_ref, router_ref, gain_ref
):
    router_ref[...] = few_ref[:8]
    gain_ref[...] = few_ref[8:9]
    for i in range(3):
        part = f_ref[:, :, 64 * i : 64 * (i + 1)].reshape(1024, 128)
        qkv_ref[:, 1024 * i : 1024 * (i + 1)] = part.T.astype(F32)
    for i in range(4):
        for h in range(2):
            part = o_ref[i, :, 32 * h : 32 * (h + 1)].reshape(128, 128)
            out_ref[:, (2 * i + h) * 128 : (2 * i + h + 1) * 128] = part.astype(F32)
    gate_ref[...] = g_ref[0].astype(F32)
    up_ref[...] = g_ref[1].astype(F32)
    down_ref[...] = g_ref[2].astype(F32)


def unfold(full, blocks, few):
    shape = jax.ShapeDtypeStruct
    share = pl.BlockSpec((None, FFB, 128), lambda i, j: (i, 0, j))
    return pl.pallas_call(
        unfold_kernel,
        out_shape=(
            shape((1024, 3072), F32),
            shape((1024, 1024), F32),
            *[shape((4, FFB, DB), F32)] * 3,
            shape((8, 1024), F32),
            shape((1, 1024), F32),
        ),
        grid=(4, 2),
        in_specs=[
            pl.BlockSpec((None, None, 4, 4, 192, 128), lambda i, j: (j, i, 0, 0, 0, 0)),
            pl.BlockSpec((None, 4, None, 4, 64, 128), lambda i, j: (j, 0, i, 0, 3, 0)),
            pl.BlockSpec((None, 3, FFB, 128), lambda i, j: (i, 0, 0, j)),
            pl.BlockSpec((16, 1024), lambda i, j: (0, 0)),
        ],
        out_specs=(
            pl.BlockSpec((128, 3072), lambda i, j: (2 * i + j, 0)),
            pl.BlockSpec((128, 1024), lambda i, j: (4 * j + i, 0)),
            *[share] * 3,
            pl.BlockSpec((8, 1024), lambda i, j: (0, 0)),
            pl.BlockSpec((1, 1024), lambda i, j: (0, 0)),
        ),
        compiler_params=pltpu.CompilerParams(vmem_limit_bytes=48 * 1024 * 1024),
    )(full, full, blocks, few)


def body(
    block_input,
    attn_gain,
    qkv_weight,
    out_weight,
    moe_gain,
    router_weight,
    gate_weight,
    up_weight,
    down_weight,
    routes,
    slot_index,
    cotangent,
):
    pairs = jnp.concatenate([routes.T, slot_index.T, jnp.zeros((4, 128), jnp.int32)]).astype(F32)
    (
        send,
        middle,
        probs,
        ctx_tok,
        qkv,
        ctx_here,
        lse,
        near,
        weights,
        qkv_low,
        out_low,
    ) = attend(
        block_input,
        attn_gain,
        gate_weight,
        up_weight,
        down_weight,
        moe_gain,
        router_weight,
        pairs,
        cotangent,
        qkv_weight,
        out_weight,
    )
    block_output, input_grad, gain_grad, mine, few, full, _ = experts_back(
        middle,
        probs,
        pairs,
        cotangent,
        moe_gain.reshape(1, -1),
        router_weight.T,
        ctx_tok,
        qkv,
        ctx_here,
        lse,
        block_input,
        attn_gain.reshape(1, -1),
        send,
        weights,
        near,
        qkv_low,
        out_low,
    )
    qkv_grad, out_grad, gate_grad, up_grad, down_grad, router_grad, moe_gain_grad = unfold(
        full, mine, few
    )
    return (
        block_output,
        input_grad,
        gain_grad.reshape(-1),
        qkv_grad,
        out_grad,
        moe_gain_grad.reshape(-1),
        router_grad.T,
        jnp.swapaxes(gate_grad, 1, 2),
        jnp.swapaxes(up_grad, 1, 2),
        down_grad,
    )


def solution(mesh):
    tokens = P(("dp", "expert", "mp"), None)
    cols = P("expert", "dp", "mp")
    rows = P("expert", "mp", "dp")
    return jax.shard_map(
        body,
        mesh=mesh,
        in_specs=(tokens, P(), P(), P(), P(), P(), cols, cols, rows, tokens, tokens, tokens),
        out_specs=(tokens, tokens, P(), P(), P(), P(), P(), cols, cols, rows),
        check_vma=False,
    )
```

```python
import jax
import jax.numpy as jnp
from jax import lax
from jax.experimental import pallas as pl
from jax.experimental.pallas import tpu as pltpu
from jax.sharding import PartitionSpec as P

EPSILON = 1e-06
HIGHEST = lax.Precision.HIGHEST
MESH = pl.DeviceIdType.MESH
F32 = jnp.float32
BF16 = jnp.bfloat16
VMEM = pltpu.VMEM
ROWS = 40
FFB = 176
FFQ = 704
DB = 256
NT = (((1,), (1,)), ((), ()))
TN = (((0,), (0,)), ((), ()))


def dot(a, b):
    return jnp.dot(a, b, preferred_element_type=F32)


def dot_nt(a, b):
    return lax.dot_general(a, b, NT, preferred_element_type=F32)


def dot_tn(a, b):
    return lax.dot_general(a, b, TN, preferred_element_type=F32)


def spot():
    m = lax.axis_index("mp")
    return lax.axis_index("dp"), lax.axis_index("expert"), m, m // 4, m % 4


def params(cid, mb=60):
    return pltpu.CompilerParams(
        collective_id=cid, has_side_effects=True, vmem_limit_bytes=mb * 1024 * 1024
    )


def swapped(c, z):
    return z % 2, 2 * (z // 2) + c


def mp_at(m, k):
    return {"mp": (m + k) % 16}


def y_at(z, y, d):
    return {"mp": z * 4 + (y + d) % 4}


def z_at(z, y, d):
    return {"mp": ((z + d) % 4) * 4 + y}


def push(src, dst, send, recv, device):
    return pltpu.make_async_remote_copy(
        src_ref=src, dst_ref=dst, send_sem=send, recv_sem=recv, device_id=device, device_id_type=MESH
    )


def tally(ref, send, recv):
    return push(ref, ref, send, recv, {"expert": 1 - lax.axis_index("expert")})


def lanes(at, size):
    return pl.ds(pl.multiple_of(at * size, size), size)


def greet_mp(barrier, m):
    def one(k, carry):
        pl.semaphore_signal(barrier, inc=1, device_id=mp_at(m, k), device_id_type=MESH)
        return carry

    lax.fori_loop(1, 16, one, 0)


def places(routes, slots):
    return jnp.where(slots < ROWS, routes * (2 * ROWS) + slots, -1.0)


def picks(columns):
    lane = lax.broadcasted_iota(jnp.int32, (128, 8), 1).astype(F32)
    return [(columns[:, j : j + 1] == lane).astype(F32) for j in range(2)]


def gates_of(probs, hot):
    chosen = [jnp.sum(probs * h, axis=1, keepdims=True) for h in hot]
    total = chosen[0] + chosen[1]
    return [v / total for v in chosen], total


def exact(a, b, dims):
    return lax.dot_general(a, b, dims, precision=HIGHEST, preferred_element_type=F32)


def unit(v):
    scale = lax.rsqrt(jnp.mean(v * v, axis=-1, keepdims=True) + EPSILON)
    return v * scale, scale


def attend_kernel(
    x_ref,
    gain_ref,
    gate_ref,
    up_ref,
    downs_ref,
    moe_gain_ref,
    router_ref,
    pairs_ref,
    cot_ref,
    wq_hbm,
    wo_hbm,
    send_out,
    mid_out,
    probs_out,
    ctx_out_ref,
    qkv_out,
    ctx_here_out,
    lse_out,
    down_out,
    nall_ref,
    w_out_ref,
    wq_out_ref,
    wo_out_ref,
    send_ref,
    mid_ref,
    probs_ref,
    ctx_ref,
    qkv_ref,
    ctx_here_ref,
    lse_ref,
    down_ref,
    wq_wide,
    wo_wide,
    wq_ref,
    wo_ref,
    normed,
    heads,
    blocks,
    stage,
    key_rows,
    ctx_low,
    here,
    s_send,
    s_recv,
    x_send,
    x_recv,
    a_send,
    a_recv,
    n_send,
    n_recv,
    c_send,
    c_recv,
):
    x, c, m, z, y = spot()
    pc, pz = swapped(c, z)
    away = (pc - c) * (pc - c)
    barrier = pltpu.get_barrier_semaphore()

    def remote(el):
        return (away == 1) | (el != y)

    def partner(el):
        return {"expert": pc, "mp": pz * 4 + el}

    greet_mp(barrier, m)
    for el in range(4):

        @pl.when(remote(el))
        def _():
            pl.semaphore_signal(barrier, inc=1, device_id=partner(el), device_id_type=MESH)

    for d in range(1, 4):
        pl.semaphore_signal(barrier, inc=1, device_id={"dp": (x + d) % 4}, device_id_type=MESH)

    wide = 512

    def load(i):
        cols = pl.ds(i * wide, wide)
        return pltpu.make_async_copy(wq_hbm.at[:, cols], wq_wide.at[:, cols], here.at[4 + i])

    def save(i):
        cols = pl.ds(i * wide, wide)
        return pltpu.make_async_copy(wq_ref.at[:, cols], wq_out_ref.at[:, cols], here.at[4 + i])

    load_o = pltpu.make_async_copy(wo_hbm, wo_wide, here.at[10])
    save_o = pltpu.make_async_copy(wo_ref, wo_out_ref, here.at[10])
    for i in range(6):
        load(i).start()
    load_o.start()
    for el in range(4):
        blocks[el, 0] = gate_ref[el].astype(BF16)
        blocks[el, 1] = up_ref[el].astype(BF16)
        blocks[el, 2] = downs_ref[el].astype(BF16)
    pl.semaphore_wait(barrier, 15 + 6 + away)

    def units(at):
        return stage.at[:, pl.ds(pl.multiple_of(at * FFB, 16), FFB), :]

    def block(i, el, at):
        return push(
            blocks.at[el, i],
            stage.at[i, pl.ds(pl.multiple_of(at * FFB, 16), FFB), :],
            s_send.at[i, el],
            s_recv.at[i, at],
            partner(el),
        )

    def each_block(f):
        for el in range(4):

            @pl.when(remote(el))
            def _(el=el):
                f(el)

    def blocks_out(i):
        each_block(lambda el: block(i, el, y).start())

    def blocks_in(i):
        each_block(lambda el: block(i, el, el).wait_recv())

    blocks_out(0)

    @pl.when(away == 0)
    def _():
        kept = pltpu.make_async_copy(blocks.at[y], units(y), here.at[2])
        kept.start()
        kept.wait()

    normed[...] = (unit(x_ref[...].astype(F32))[0] * gain_ref[...]).astype(BF16)
    half = 512

    def near(part, d):
        cols = pl.ds(part * half, half)
        device = y_at(z, y, d) if part == 0 else z_at(z, y, d)
        return lambda at: push(
            normed.at[:, cols],
            nall_ref.at[at // 4, at % 4, :, cols],
            n_send.at[part, 0, d],
            n_recv.at[part, 0, d],
            device,
        )

    y_from = [z * 4 + (y + 4 - d) % 4 for d in range(4)]
    z_from = [((z + 4 - d) % 4) * 4 + y for d in range(4)]

    def far(part, d, origin):
        cols = pl.ds(part * half, half)
        if part == 0:
            ref, device = nall_ref.at[origin // 4, :, :, cols], z_at(z, y, d)
        else:
            ref, device = nall_ref.at[:, origin % 4, :, cols], y_at(z, y, d)
        return push(ref, ref, n_send.at[part, 1, d], n_recv.at[part, 1, d], device)

    for i in range(6):
        load(i).wait()
        cols = slice(i * wide, (i + 1) * wide)
        wq_ref[:, cols] = wq_wide[:, cols].astype(BF16)
        save(i).start()
        part = dot(normed[...], wq_ref[:, cols])
        heads[i // 2, (i % 2) * 8 : (i % 2) * 8 + 8] = part.T.astype(BF16).reshape(8, 64, 128)

    def head_out(k):
        t = (m + k) % 16
        return push(
            heads.at[:, t],
            qkv_ref.at[:, :, lanes(m, 128)],
            a_send.at[0],
            a_recv.at[0],
            mp_at(m, k),
        )

    def each(lo, hi, f):
        def one(k, carry):
            f(k)
            return carry

        lax.fori_loop(lo, hi, one, 0)

    each(1, 16, lambda k: head_out(k).start())
    own = pltpu.make_async_copy(heads.at[:, m], qkv_ref.at[:, :, lanes(m, 128)], here.at[0])
    own.start()
    mine = pltpu.make_async_copy(normed, nall_ref.at[z, y], here.at[1])
    mine.start()
    blocks_out(1)
    blocks_out(2)
    for d in (2, 1, 3):
        near(0, d)(m).start()
        near(1, d)(m).start()


    def fan(i, d, step, at):
        rows = pl.ds(0, FFQ) if step == 0 else pl.ds(0 if d == 1 else FFQ // 2, FFQ // 2)
        cols = w_out_ref.at[i, rows, lanes(at, DB)]
        return push(
            stage.at[i] if step == 0 else cols,
            cols,
            x_send.at[i, step, d],
            x_recv.at[i, step, d],
            {"dp": (x + d) % 4},
        )

    def fan_wait(i, step):
        for d in (1, 3):
            fan(i, d, step, (x + 8 - d * (1 + step)) % 4).wait_recv()

    def fan_start(i, step):
        for d in (1, 3):
            fan(i, d, step, x if step == 0 else (x + 4 - d) % 4).start()

    def fan_own(i):
        return pltpu.make_async_copy(stage.at[i], w_out_ref.at[i, :, lanes(x, DB)], here.at[2 + i])

    blocks_in(0)
    fan_start(0, 0)
    fan_own(0).start()
    load_o.wait()
    wo_ref[...] = wo_wide[...].astype(BF16)
    save_o.start()

    own.wait()
    some = qkv_ref.at[:, :, pl.ds(0, 15 * 128)]
    tally(some, a_send.at[0], a_recv.at[0]).wait_recv()

    key_rows[...] = qkv_ref[1].astype(F32).T.astype(BF16)

    def ctx_out(t):
        return push(
            ctx_low.at[:, lanes(t, 128)],
            ctx_ref.at[pl.ds(pl.multiple_of(m * 64, 64), 64), :],
            c_send.at[0],
            c_recv.at[0],
            {"mp": t},
        )

    def queries(i):
        b = (m // 2 + i) % 8
        cols = lanes(b, 256)
        q = (qkv_ref[0, :, cols].astype(F32) * 0.125).astype(BF16)
        s = dot(key_rows[...], q)
        top = jnp.max(s, axis=0, keepdims=True)
        p = jnp.exp(s - top)
        total = jnp.sum(p, axis=0, keepdims=True)
        ctx = dot(qkv_ref[2], p.astype(BF16)) / total
        lse_ref[:, cols] = top + jnp.log(total)
        ctx_here_ref[:, cols] = ctx
        ctx_low[:, cols] = ctx.astype(BF16)

    def pair(i, carry):
        queries(2 * i)
        queries(2 * i + 1)
        for u in range(2):
            b = (m // 2 + 2 * i + u) % 8
            for v in range(2):
                t = 2 * b + v

                @pl.when(t != m)
                def _():
                    ctx_out(t).start()

        @pl.when(i == 0)
        def _():
            blocks_in(1)
            fan_start(1, 0)
            fan_own(1).start()

        @pl.when(i == 1)
        def _():
            fan_wait(0, 0)
            fan_start(0, 1)
            blocks_in(2)
            down_ref[...] = stage[2]

        return carry

    lax.fori_loop(0, 4, pair, 0)
    for d in (1, 2, 3):
        near(0, d)(y_from[d]).wait_recv()
        near(1, d)(z_from[d]).wait_recv()
    mine.wait()
    for d in (1, 3):
        far(0, d, m).start()
        far(1, d, m).start()
    ctx_ref[pl.ds(pl.multiple_of(m * 64, 64), 64), :] = ctx_low[:, lanes(m, 128)]
    lot = ctx_ref.at[pl.ds(0, 15 * 64)]
    tally(lot, c_send.at[0], c_recv.at[0]).wait_recv()

    fan_wait(1, 0)
    fan_start(1, 1)

    mid = x_ref[...].astype(F32) + dot_tn(ctx_ref[...], wo_ref[...])
    mid_ref[...] = mid
    moe_in = unit(mid)[0] * moe_gain_ref[...]
    logits = exact(moe_in, router_ref[...], NT)
    grown = jnp.exp(logits - jnp.max(logits, axis=1, keepdims=True))
    probs = grown / jnp.sum(grown, axis=1, keepdims=True)
    probs_ref[...] = probs
    gates, _ = gates_of(probs, picks(pairs_ref[...].T))
    upstream = cot_ref[...].astype(F32)
    rows = [moe_in.astype(BF16)] + [(g * upstream).astype(BF16) for g in gates]
    row = lax.broadcasted_iota(jnp.int32, (16 * ROWS, 128), 0).astype(F32)
    at = [places(pairs_ref[j : j + 1], pairs_ref[2 + j : 3 + j]) for j in range(2)]
    hot = [((row == at[0]) | (row == at[1]))] + [row == jnp.where(a < 0, a, a + ROWS) for a in at]
    hot = jnp.concatenate([h.astype(F32) for h in hot], axis=1).astype(BF16)
    sent = dot(hot, jnp.concatenate(rows, axis=0))
    send_ref[...] = sent.astype(BF16).reshape(8, 2 * ROWS, 1024)
    results = (
        (send_ref, send_out),
        (mid_ref, mid_out),
        (probs_ref, probs_out),
        (ctx_ref, ctx_out_ref),
        (qkv_ref, qkv_out),
        (ctx_here_ref, ctx_here_out),
        (lse_ref, lse_out),
        (down_ref, down_out),
    )
    results = [
        pltpu.make_async_copy(src, dst, here.at[11 + i]) for i, (src, dst) in enumerate(results)
    ]
    for copy in results:
        copy.start()

    for i in range(6):
        save(i).wait()
    save_o.wait()
    fan_wait(0, 1)
    fan_wait(1, 1)
    for d in (1, 3):
        far(0, d, z_from[d]).wait_recv()
        far(1, d, y_from[d]).wait_recv()
    for d in (1, 2, 3):
        near(0, d)(m).wait_send()
        near(1, d)(m).wait_send()
    for d in (1, 3):
        far(0, d, m).wait_send()
        far(1, d, m).wait_send()
    for i in range(2):
        fan_own(i).wait()
        for d in (1, 3):
            for step in range(2):
                fan(i, d, step, x).wait_send()
    tally(some, a_send.at[0], a_recv.at[0]).wait_send()
    tally(lot, c_send.at[0], c_recv.at[0]).wait_send()
    for i in range(3):
        each_block(lambda el, i=i: block(i, el, y).wait_send())
    for copy in results:
        copy.wait()


def attend(
    block_input,
    gain,
    gate_weight,
    up_weight,
    down_weight,
    moe_gain,
    router,
    pairs,
    cotangent,
    qkv_weight,
    out_weight,
):
    dma = pltpu.SemaphoreType.DMA
    vm = pl.BlockSpec(memory_space=VMEM)
    hbm = pl.BlockSpec(memory_space=pl.ANY)
    shape = jax.ShapeDtypeStruct
    return pl.pallas_call(
        attend_kernel,
        out_shape=(
            shape((8, 2 * ROWS, 1024), BF16),
            shape((128, 1024), F32),
            shape((128, 8), F32),
            shape((1024, 128), BF16),
            shape((3, 64, 2048), BF16),
            shape((64, 2048), F32),
            shape((1, 2048), F32),
            shape((FFQ, DB), BF16),
            shape((4, 4, 128, 1024), BF16),
            shape((2, FFQ, 4 * DB), BF16),
            shape((1024, 3072), BF16),
            shape((1024, 1024), BF16),
        ),
        in_specs=[vm] * 9 + [hbm] * 2,
        out_specs=(hbm,) * 12,
        scratch_shapes=[
            VMEM((8, 2 * ROWS, 1024), BF16),
            VMEM((128, 1024), F32),
            VMEM((128, 8), F32),
            VMEM((1024, 128), BF16),
            VMEM((3, 64, 2048), BF16),
            VMEM((64, 2048), F32),
            VMEM((1, 2048), F32),
            VMEM((FFQ, DB), BF16),
            VMEM((1024, 3072), F32),
            VMEM((1024, 1024), F32),
            VMEM((1024, 3072), BF16),
            VMEM((1024, 1024), BF16),
            VMEM((128, 1024), BF16),
            VMEM((3, 16, 64, 128), BF16),
            VMEM((4, 3, FFB, DB), BF16),
            VMEM((3, FFQ, DB), BF16),
            VMEM((2048, 64), BF16),
            VMEM((64, 2048), BF16),
            dma((19,)),
            dma((3, 4)),
            dma((3, 4)),
            dma((2, 2, 4)),
            dma((2, 2, 4)),
            dma((1,)),
            dma((1,)),
            dma((2, 2, 4)),
            dma((2, 2, 4)),
            dma((1,)),
            dma((1,)),
        ],
        compiler_params=params(1, 62),
    )(
        block_input,
        gain.reshape(1, -1),
        jnp.swapaxes(gate_weight, 1, 2),
        jnp.swapaxes(up_weight, 1, 2),
        down_weight,
        moe_gain.reshape(1, -1),
        router.T,
        pairs,
        cotangent,
        qkv_weight,
        out_weight,
    )


GELU_A = 0.7978845608
GELU_B = 0.044715


def experts_back_kernel(
    mid_hbm,
    probs_hbm,
    pairs_hbm,
    cot_hbm,
    moe_gain_hbm,
    router_hbm,
    tok_hbm,
    qkv_hbm,
    ctx_hbm,
    lse_hbm,
    x_hbm,
    gain_hbm,
    down_hbm,
    send_hbm,
    w_hbm,
    near_hbm,
    wq_hbm,
    wo_hbm,
    y_ref,
    in_ref,
    gain_out_ref,
    g_out_ref,
    few_out_ref,
    full_out,
    ret_ref,
    mid_ref,
    probs_ref,
    pairs_ref,
    cot_ref,
    moe_gain_ref,
    router_ref,
    tok_ref,
    qkv_ref,
    ctx_ref,
    lse_ref,
    x_ref,
    gain_ref,
    down_ref,
    full_ref,
    nall_ref,
    weights,
    recv,
    rows,
    back,
    sib_recv,
    sib_send,
    own_part,
    hid,
    gcs,
    ucs,
    g_relay,
    g_near,
    dctx,
    few,
    o_sib,
    o_x,
    o_q,
    o_mp,
    few_mp,
    few_sum,
    few_done,
    few_rest,
    cot,
    key_values,
    row_dot,
    dkv,
    pc_here,
    pc_tok,
    slices,
    share,
    parts,
    gain_row,
    gain_mp,
    gain_rest,
    here,
    leave,
    d_send,
    d_recv,
    f_send,
    f_recv,
    p_send,
    p_recv,
    r_send,
    r_recv,
    w_send,
    w_recv,
    x_send,
    x_recv,
    s_send,
    s_recv,
    n_send,
    n_recv,
    a_send,
    a_recv,
    b_send,
    b_recv,
    q_send,
    q_recv,
    g_send,
    g_recv,
    t_send,
    t_recv,
    u_send,
    u_recv,
    v_send,
    v_recv,
    o_send,
    o_recv,
    ox_send,
    ox_recv,
    om_send,
    om_recv,
    fm_send,
    fm_recv,
    fr_send,
    fr_recv,
):
    x, c, m, z, y = spot()
    pc, pz = swapped(c, z)
    away = (pc - c) * (pc - c)
    barrier = pltpu.get_barrier_semaphore()

    def remote(el):
        return (away == 1) | (el != y)

    def partner(el):
        return {"expert": pc, "mp": pz * 4 + el}

    def rest(r):
        return {"dp": (x + r % 4) % 4, "expert": (c + r // 4) % 2}

    def each(lo, hi, f):
        def one(k, carry):
            f(k)
            return carry

        lax.fori_loop(lo, hi, one, 0)

    def local(src, dst, i):
        return pltpu.make_async_copy(src, dst, here.at[i])

    twin = {"expert": 1 - c}
    size = 2 * ROWS

    greet_mp(barrier, m)
    for el in range(4):

        @pl.when(remote(el))
        def _():
            pl.semaphore_signal(barrier, inc=1, device_id=partner(el), device_id_type=MESH)

    for r in range(1, 8):
        pl.semaphore_signal(barrier, inc=1, device_id=rest(r), device_id_type=MESH)
    operands = [
        local(src, dst, 14 + i)
        for i, (src, dst) in enumerate(
            (
                (down_hbm, down_ref),
                (mid_hbm, mid_ref),
                (probs_hbm, probs_ref),
                (pairs_hbm, pairs_ref),
                (cot_hbm, cot_ref),
                (moe_gain_hbm, moe_gain_ref),
                (router_hbm, router_ref),
                (tok_hbm, tok_ref),
                (qkv_hbm, qkv_ref),
                (ctx_hbm, ctx_ref),
                (lse_hbm, lse_ref),
                (x_hbm, x_ref),
                (gain_hbm, gain_ref),
            )
        )
    ]
    for copy in operands:
        copy.start()
    load_w = [local(w_hbm.at[i], weights.at[pl.ds(i * FFQ, FFQ)], i) for i in range(2)]
    for copy in load_w:
        copy.start()
    near = []
    for i, d in enumerate((0, 1, 3)):
        at = (z + d) % 4, slice(None), slice(None), pl.ds(0, 512)
        near.append(local(near_hbm.at[at], nall_ref.at[at], 8 + i))
        at = slice(None), (y + d) % 4, slice(None), pl.ds(512, 512)
        near.append(local(near_hbm.at[at], nall_ref.at[at], 11 + i))
    for copy in near:
        copy.start()
    pl.semaphore_wait(barrier, 15 + 3 + away + 7)

    def expert_of(t):
        return ((t // 4) % 2) * 4 + t % 4

    def slot(core, k, n=1):
        return pl.ds(pl.multiple_of((core * 16 + k) * size, size), n * size)

    def dispatch(k):
        t = (m + k) % 16
        return push(
            send_hbm.at[expert_of(t)],
            recv.at[slot(0, k)],
            d_send.at[0],
            d_recv.at[k],
            {"mp": t},
        )

    def forward(k):
        return push(
            recv.at[slot(0, k)], recv.at[slot(1, k)], f_send.at[0], f_recv.at[k // 4], twin
        )

    def partials(j):
        return push(
            sib_send.at[j % 2],
            sib_recv.at[pl.ds(pl.multiple_of(j * 4 * size, size), 4 * size)],
            p_send.at[j],
            p_recv.at[j],
            twin,
        )

    def spot_of(k, n=1):
        return pl.ds(pl.multiple_of(k * size, size), n * size)

    def giving(k, at):
        return push(
            back.at[spot_of(k)], ret_ref.at[at], r_send.at[0], r_recv.at[0], mp_at(m, 16 - k)
        )

    def down_fan(d, step, at):
        part = pl.ds(0, FFQ) if step == 0 else pl.ds(0 if d == 1 else FFQ // 2, FFQ // 2)
        units = pl.ds(2 * FFQ + part.start, part.size)
        there = weights.at[units, lanes(at, DB)]
        return push(
            down_ref if step == 0 else there,
            there,
            w_send.at[step, d // 2],
            w_recv.at[step, d // 2],
            {"dp": (x + d) % 4},
        )

    operands[0].wait()
    for d in (1, 3):
        down_fan(d, 0, x).start()
    each(1, 16, lambda k: dispatch(k).start())
    own = local(send_hbm.at[expert_of(m)], recv.at[slot(0, 0)], 4)
    own.start()
    weights[2 * FFQ :, lanes(x, DB)] = down_ref[...]
    own.wait()

    def finish(j):
        partials(j).wait_recv()
        span = spot_of(4 * j, 4)
        back[span] = (own_part[...] + sib_recv[span].astype(F32)).astype(BF16)
        for i in range(4):
            k = 4 * j + i

            @pl.when(k > 0)
            def _():
                giving(k, m).start()

            @pl.when(k == 0)
            def _():
                local(back.at[spot_of(0)], ret_ref.at[m], 4).start()

    gate_w, up_w, down_w = (slice(i * FFQ, (i + 1) * FFQ) for i in range(3))
    cot_rows = 32 * ROWS

    def chunk(j, carry):
        for i in range(4):
            k = 4 * j + i

            @pl.when(k > 0)
            def _():
                dispatch(k).wait_recv()

            forward(k).start()

        @pl.when(j > 0)
        def _():
            finish(j - 1)

        @pl.when(j == 0)
        def _():
            for copy in load_w:
                copy.wait()
            for d in (1, 3):
                down_fan(d, 1, (x + 2) % 4).wait_recv()

        tally(recv.at[slot(1, 4 * j, 4)], f_send.at[0], f_recv.at[j]).wait_recv()
        xs = pl.ds(pl.multiple_of(j * 8 * ROWS, 16), 8 * ROWS)
        cs = pl.ds(pl.multiple_of(cot_rows + j * 8 * ROWS, 16), 8 * ROWS)
        for r in range(2):
            blk = recv[slot(r, 4 * j, 4)].astype(F32).reshape(4, size, 4 * DB)
            for at, part in ((0, blk[:, :ROWS]), (cot_rows, blk[:, ROWS:])):
                span = pl.ds(pl.multiple_of(at + (2 * j + r) * 4 * ROWS, 16), 4 * ROWS)
                rows[span] = part.reshape(4 * ROWS, 4 * DB).astype(BF16)
        gate = dot_nt(rows[xs], weights[gate_w])
        up = dot_nt(rows[xs], weights[up_w])
        hid_cot = dot_nt(rows[cs], weights[down_w])
        sq = gate * gate
        th = jnp.tanh(GELU_A * (gate + GELU_B * (gate * sq)))
        half = 0.5 * (1.0 + th)
        act = gate * half
        slope = half + 0.5 * gate * (1.0 - th * th) * (GELU_A * (1.0 + 3.0 * GELU_B * sq))
        hid[xs] = (act * up).astype(BF16)
        gcs[xs] = (hid_cot * up * slope).astype(BF16)
        ucs[xs] = (hid_cot * act).astype(BF16)
        out = dot(hid[xs], weights[down_w]).reshape(2, 4, ROWS, 4 * DB)
        low = dot(gcs[xs], weights[gate_w]) + dot(ucs[xs], weights[up_w])
        low = low.reshape(2, 4, ROWS, 4 * DB)
        own_part[...] = jnp.concatenate([out[0], low[0]], axis=1).reshape(4 * size, 4 * DB)

        @pl.when(j > 1)
        def _():
            partials(j - 2).wait_send()

        sib_send[j % 2] = (
            jnp.concatenate([out[1], low[1]], axis=1).reshape(4 * size, 4 * DB).astype(BF16)
        )
        partials(j).start()
        return carry

    for d in (1, 3):
        down_fan(d, 0, (x + 4 - d) % 4).wait_recv()
        down_fan(d, 1, (x + 4 - d) % 4).start()
    lax.fori_loop(0, 4, chunk, 0)
    finish(3)
    tally(recv.at[slot(0, 0, 16)], f_send.at[0], f_recv.at[0]).wait_send()
    for d in (1, 3):
        down_fan(d, 0, x).wait_send()
        down_fan(d, 1, x).wait_send()
    load_o = local(wo_hbm, weights.at[pl.ds(0, 1024)], 0)
    load_o.start()

    unit_half = FFQ // 2

    def unit_rows(i, d):
        return pl.ds(i * FFQ + (0 if d == 1 else unit_half), unit_half)

    def relay(i, d):
        return push(
            recv.at[unit_rows(i, d), lanes((x + 2) % 4, DB)],
            g_relay.at[d // 2, i],
            x_send.at[0, i, d // 2],
            x_recv.at[0, i, d // 2],
            {"dp": (x + d) % 4},
        )

    def settle(i, d):
        return push(
            recv.at[pl.ds(i * FFQ, FFQ), lanes((x + d) % 4, DB)],
            g_near.at[d // 2, i],
            x_send.at[1, i, d // 2],
            x_recv.at[1, i, d // 2],
            {"dp": (x + d) % 4},
        )

    for i, (a, at) in enumerate(((gcs, 0), (ucs, 0), (hid, cot_rows))):
        g = dot_tn(a[...], rows[at : at + cot_rows])
        recv[i * FFQ : (i + 1) * FFQ] = g.astype(BF16)
        for d in (1, 3):
            relay(i, d).start()
    load_q = [
        local(wq_hbm.at[:, pl.ds(i * 1024, 1024)], rows.at[pl.ds(i * 1024, 1024)], 5 + i)
        for i in range(3)
    ]
    for copy in load_q:
        copy.start()
    for i in range(3):
        for d in (1, 3):
            relay(i, d).wait_recv()
            span, cols = unit_rows(i, d), lanes((x + d) % 4, DB)
            recv[span, cols] = (
                recv[span, cols].astype(F32) + g_relay[d // 2, i].astype(F32)
            ).astype(BF16)
            settle(i, d).start()

    def home(i, at, to):
        return push(
            recv.at[pl.ds(i * FFQ + at * FFB, FFB), lanes(x, DB)],
            g_out_ref.at[to, i],
            s_send.at[i, at],
            s_recv.at[i, to],
            partner(at),
        )

    def each_home(f):
        for at in range(4):

            @pl.when(remote(at))
            def _(at=at):
                f(at)

    def go_home(i):
        for d in (1, 3):
            settle(i, d).wait_recv()
        span, cols = pl.ds(i * FFQ, FFQ), lanes(x, DB)
        recv[span, cols] = (
            recv[span, cols].astype(F32) + g_near[0, i].astype(F32) + g_near[1, i].astype(F32)
        ).astype(BF16)
        each_home(lambda at: home(i, at, y).start())

        @pl.when(away == 0)
        def _():
            kept = local(
                recv.at[pl.ds(pl.multiple_of(i * FFQ + y * FFB, 16), FFB), cols], g_out_ref.at[y, i], 1
            )
            kept.start()
            kept.wait()

    local(back.at[spot_of(0)], ret_ref.at[m], 4).wait()
    tally(back.at[spot_of(1, 15)], r_send.at[0], r_recv.at[0]).wait_send()
    tally(ret_ref.at[pl.ds(0, 15)], r_send.at[0], r_recv.at[0]).wait_recv()
    load_r = local(ret_ref, back.reshape(16, size, 4 * DB), 4)
    load_r.start()
    load_r.wait()

    for copy in (*near, *operands[1:]):
        copy.wait()

    def far(part, d, hops):
        cols, some = pl.ds(part * 512, 512), pl.ds(0 if d == 1 else 2, 2)
        if part == 0:
            ref, device = nall_ref.at[(z + 8 - hops * d) % 4, some, :, cols], z_at(z, y, d)
        else:
            ref, device = nall_ref.at[some, (y + 8 - hops * d) % 4, :, cols], y_at(z, y, d)
        return push(ref, ref, n_send.at[part, d // 2], n_recv.at[part, d // 2], device)

    columns = pairs_ref[...].T
    hot = picks(columns)
    probs = probs_ref[...]
    gates, total = gates_of(probs, hot)
    at = places(columns[:, 0:2], columns[:, 2:4])
    lane = lax.broadcasted_iota(jnp.int32, (128, 16 * ROWS), 1).astype(F32)
    at = [at[:, j : j + 1] for j in range(2)]
    given = (back[: 8 * size].astype(F32) + back[8 * size :].astype(F32)).astype(BF16)
    fetched = [dot((lane == a).astype(F32).astype(BF16), given) for a in at]
    low = [lane == jnp.where(a < 0, a, a + ROWS) for a in at]
    moe_cot = dot((low[0] | low[1]).astype(F32).astype(BF16), given)
    mid = mid_ref[...]
    upstream = cot_ref[...].astype(F32)
    y_ref[...] = (mid + gates[0] * fetched[0] + gates[1] * fetched[1]).astype(BF16)
    gate_cot = [jnp.sum(upstream * f, axis=1, keepdims=True) for f in fetched]
    inner = gate_cot[0] * gates[0] + gate_cot[1] * gates[1]
    probs_cot = sum(h * ((g - inner) / total) for h, g in zip(hot, gate_cot))
    logit_cot = probs * (probs_cot - jnp.sum(probs * probs_cot, axis=1, keepdims=True))
    hat, scale = unit(mid)
    moe_cot += exact(logit_cot, router_ref[...], (((1,), (0,)), ((), ())))
    few[:8] = exact(logit_cot, hat * moe_gain_ref[...], TN)
    few[8:] = jnp.concatenate(
        [jnp.sum(moe_cot * hat, axis=0, keepdims=True), jnp.zeros((7, 1024), F32)], axis=0
    )
    gained = moe_cot * moe_gain_ref[...]
    in_ref[...] = upstream + scale * (gained - hat * jnp.mean(gained * hat, axis=-1, keepdims=True))
    branch_cot = in_ref[...].astype(BF16)
    load_o.wait()
    dctx[...] = dot_nt(weights[:1024], branch_cot).astype(BF16).reshape(16, 64, 128)

    def cot_out(k):
        t = (m + k) % 16
        return push(dctx.at[t], cot.at[:, lanes(m, 128)], a_send.at[0], a_recv.at[0], {"mp": t})

    each(1, 16, lambda k: cot_out(k).start())
    for d in (1, 3):
        far(0, d, 1).start()
        far(1, d, 1).start()
    cot[:, lanes(m, 128)] = dctx[m]

    weights[1024:2048] = dot(tok_ref[...], branch_cot).astype(BF16)

    def halves():
        rows_at = pl.ds(pl.multiple_of(1024 + (1 - c) * 512, 512), 512)
        return push(weights.at[rows_at], o_sib, o_send.at[0], o_recv.at[0], twin)

    def quarters(d):
        t = (x + d) % 4
        return push(
            weights.at[pl.ds(0, 512), lanes(t, DB)], o_x.at[d - 1], ox_send.at[0], ox_recv.at[0], {"dp": t}
        )

    def thirty(k):
        t = (m + k) % 16
        return push(
            o_q.at[pl.ds(pl.multiple_of(t * 32, 32), 32)],
            o_mp.at[k],
            om_send.at[0],
            om_recv.at[0],
            {"mp": t},
        )

    def few_share(r):
        t = 2 * ((x + r % 4) % 4) + (c + r // 4) % 2
        return push(
            few.at[:, lanes(t, 128)], few_rest.at[r], fr_send.at[0], fr_recv.at[0], rest(r)
        )

    def few_near(k):
        return push(few_sum, few_mp.at[k], fm_send.at[0], fm_recv.at[0], mp_at(m, k))

    def few_back(r, back_from):
        t = 2 * ((x + 4 - r % 4) % 4) + (c + r // 4) % 2 if back_from else 2 * x + c
        return push(
            few_done, few_out_ref.at[:, lanes(t, 128)], fr_send.at[1], fr_recv.at[1], rest(r)
        )

    halves().start()
    for r in range(1, 8):
        few_share(r).start()

    def along(axis, d):
        if axis == 0:
            return {"dp": (x + d) % 4}
        return z_at(z, y, d) if axis == 1 else y_at(z, y, d)

    orders = ((0, 2, 1), (1, 0, 2), (2, 1, 0), (0, 2, 1), (0, 1, 2))
    spans = [pl.ds(0, 64), pl.ds(64, 64), pl.ds(128, 64), pl.ds(192, 32), pl.ds(224, 32)]

    def spread(p, s, d, incoming):
        at = [x, z, y]
        axis = orders[p][s]
        if incoming:
            at[axis] = (at[axis] + 4 - d) % 4
        src = [x, z, y]
        for done in orders[p][:s]:
            at[done] = slice(None)
            src[done] = slice(None)
        return push(
            full_ref.at[(c, *src, spans[p])],
            full_ref.at[(c, *at, spans[p])],
            g_send.at[p, s],
            g_recv.at[p, s],
            along(axis, d),
        )

    def spread_start(p, s):
        for d in (2, 1, 3):
            spread(p, s, d, False).start()

    def last(p, d, hops):
        at = [slice(None)] * 3
        axis = orders[p][2]
        at[axis] = ((x, z, y)[axis] + 8 - hops * d) % 4
        return at

    def circle(p, d, step, incoming):
        at = last(p, d, step + incoming)
        if step:
            at[orders[p][0]] = pl.ds(0 if d == 1 else 2, 2)
        ref = full_ref.at[(c, *at, spans[p])]
        return push(ref, ref, g_send.at[p, 2 + step], g_recv.at[p, 2 + 2 * step + d // 2], along(orders[p][2], d))

    def blocks_of(p, s):
        at = ((0, 0, pl.ds(0, 3)), (0, pl.ds(0, 3), slice(None)), (pl.ds(0, 2),), (pl.ds(0, 1),))[s]
        at = (*at, *[slice(None)] * (3 - len(at)))
        return full_ref.at[(c, *at, spans[p])]

    def spread_wait(p, s):
        tally(blocks_of(p, s), g_send.at[p, s], g_recv.at[p, s]).wait_recv()

    def piece(p, i, core):
        d, hops = ((1, 0), (1, 1), (3, 1), (1, 2), (3, 2))[i]
        at = last(p, d, hops)
        if hops == 2:
            at[orders[p][0]] = pl.ds(0 if d == 1 else 2, 2)
        return (core, *at, spans[p])

    def share_twin(p, i, core):
        ref = full_ref.at[piece(p, i, core)]
        return push(ref, ref, t_send.at[0], t_recv.at[p, i], twin)

    def write(p, i, other):
        at = piece(p, i, 1 - c if other else c)
        return pltpu.make_async_copy(full_ref.at[at], full_out.at[at], leave.at[other])

    def hand_on(p, i):
        share_twin(p, i, c).start()
        write(p, i, 0).start()

    key_values[...] = qkv_ref[1:].reshape(128, 2048).astype(F32).T.astype(BF16)
    dkv[...] = jnp.zeros_like(dkv)
    halves().wait_recv()
    weights[:512] = (
        weights[pl.ds(pl.multiple_of(1024 + c * 512, 512), 512)].astype(F32) + o_sib[...].astype(F32)
    ).astype(BF16)
    for d in (2, 1, 3):
        quarters(d).start()
    go_home(0)
    cots = cot.at[:, pl.ds(0, 15 * 128)]
    tally(cots, a_send.at[0], a_recv.at[0]).wait_recv()
    row_dot[...] = jnp.sum(cot[...].astype(F32) * ctx_ref[...], axis=0, keepdims=True)

    def queries(b):
        cols = lanes(b, 256)
        q = (qkv_ref[0, :, cols].astype(F32) * 0.125).astype(BF16)
        none = jnp.zeros((64, 256), BF16)
        q = jnp.concatenate([q, none], axis=0)
        g = jnp.concatenate([none, cot[:, cols]], axis=0)
        p = jnp.exp(dot(key_values[...], q) - lse_ref[:, cols])
        dp = dot(key_values[...], g)
        ds = (p * (dp - row_dot[:, cols])).astype(BF16)
        pc_here[0, :, cols] = (dot(qkv_ref[1], ds) * 0.125).astype(BF16)
        dkv[...] += dot_nt(ds, q) + dot_nt(p.astype(BF16), g)

    def pair(i, carry):
        queries(2 * i)
        queries(2 * i + 1)

        @pl.when(i == 1)
        def _():
            go_home(1)

        @pl.when(i == 2)
        def _():
            few_all = few[:, lanes(2 * x + c, 128)]
            tally(few_rest.at[pl.ds(1, 7)], fr_send.at[0], fr_recv.at[0]).wait_recv()
            for r in range(1, 8):
                few_all += few_rest[r]
            few_sum[...] = few_all
            each(1, 16, lambda k: few_near(k).start())
            go_home(2)

        return carry

    lax.fori_loop(0, 4, pair, 0)
    pc_here[1:] = dkv[...].T.astype(BF16).reshape(2, 64, 2048)

    def pc_out(k):
        t = (m + k) % 16
        return push(
            pc_here.at[:, :, lanes(t, 128)], pc_tok.at[:, m], b_send.at[0], b_recv.at[0], {"mp": t}
        )

    for d in (1, 3):
        far(0, d, 2).wait_recv()
        far(1, d, 2).wait_recv()
    long = pc_here[...].reshape(192, 2048)
    slices[...] = dot(long, nall_ref[...].reshape(2048, 1024)).astype(BF16)

    def share_out(r):
        t = 2 * ((x + r % 4) % 4) + (c + r // 4) % 2
        return push(slices.at[:, lanes(t, 128)], parts.at[r], q_send.at[0], q_recv.at[0], rest(r))

    for r in range(1, 8):
        share_out(r).start()
    each(1, 16, lambda k: pc_out(k).start())
    pc_tok[:, m] = pc_here[:, :, lanes(m, 128)]

    tally(o_x, ox_send.at[0], ox_recv.at[0]).wait_recv()
    o_sum = weights[:512, lanes(x, DB)].astype(F32)
    for d in (1, 2, 3):
        o_sum += o_x[d - 1].astype(F32)
    o_q[...] = o_sum.astype(BF16)
    each(1, 16, lambda k: thirty(k).start())
    whole = slices[:, lanes(2 * x + c, 128)].astype(F32)
    seven = parts.at[pl.ds(1, 7)]
    tally(seven, q_send.at[0], q_recv.at[0]).wait_recv()
    for r in range(1, 8):
        whole += parts[r].astype(F32)
    share[:192] = whole.astype(BF16)
    lay = local(share.at[pl.ds(0, 192)], full_ref.at[c, x, z, y, pl.ds(0, 192)], 2)
    lay.start()
    lay.wait()
    for p in range(3):
        spread_start(p, 0)
    def circles(p):
        spread_wait(p, 1)
        for d in (1, 3):
            circle(p, d, 0, 0).start()
        hand_on(p, 0)

    for p in range(3):
        spread_wait(p, 0)
        spread_start(p, 1)
    fifteen = o_mp.at[pl.ds(1, 15)]
    tally(fifteen, om_send.at[0], om_recv.at[0]).wait_recv()
    o_sum = o_q[pl.ds(pl.multiple_of(m * 32, 32), 32)].astype(F32)
    for k in range(1, 16):
        o_sum += o_mp[k].astype(F32)
    o_low = o_sum.astype(BF16)
    share[192:224] = o_low[:, :128]
    share[224:] = o_low[:, 128:]
    lay = local(share.at[pl.ds(192, 64)], full_ref.at[c, x, z, y, pl.ds(192, 64)], 2)
    lay.start()
    lay.wait()
    for p in (3, 4):
        spread_start(p, 0)

    for p in range(3):
        circles(p)
    for p in (3, 4):
        spread_wait(p, 0)
        spread_start(p, 1)

    packs = pc_here.at[:, :, pl.ds(0, 15 * 128)]
    tally(packs, b_send.at[0], b_recv.at[0]).wait_recv()
    for copy in load_q:
        copy.wait()
    dn = sum(dot(rows[i * 1024 : (i + 1) * 1024], pc_tok[i].reshape(1024, 128)) for i in range(3)).T
    hat, scale = unit(x_ref[...].astype(F32))
    gained = dn * gain_ref[...]
    in_ref[...] = in_ref[...] + scale * (
        gained - hat * jnp.mean(gained * hat, axis=-1, keepdims=True)
    )
    gain_row[...] = jnp.sum(dn * hat, axis=0, keepdims=True)

    def gain_out(k):
        return push(gain_row, gain_mp.at[k], u_send.at[0], u_recv.at[0], mp_at(m, k))

    def gain_far(r):
        return push(gain_mp.at[0], gain_rest.at[r], v_send.at[0], v_recv.at[0], rest(r))

    each(1, 16, lambda k: gain_out(k).start())
    for p in (3, 4):
        circles(p)

    def onward(p):
        for i, d in ((1, 1), (2, 3)):
            circle(p, d, 0, 1).wait_recv()
            circle(p, d, 1, 0).start()
            hand_on(p, i)

    for p in range(3):
        onward(p)
    gains = gain_mp.at[pl.ds(1, 15)]
    tally(gains, u_send.at[0], u_recv.at[0]).wait_recv()
    got = gain_row[...]
    for k in range(1, 16):
        got += gain_mp[k]
    gain_mp[0] = got
    for r in range(1, 8):
        gain_far(r).start()
    for p in (3, 4):
        onward(p)
    fews = few_mp.at[pl.ds(1, 15)]
    tally(fews, fm_send.at[0], fm_recv.at[0]).wait_recv()
    few_all = few_sum[...]
    for k in range(1, 16):
        few_all += few_mp[k]
    few_done[...] = few_all
    few_out_ref[:, lanes(2 * x + c, 128)] = few_all
    for r in range(1, 8):
        few_back(r, False).start()
    for p in range(5):
        for i, d in ((3, 1), (4, 3)):
            circle(p, d, 1, 1).wait_recv()
            hand_on(p, i)
    rests = gain_rest.at[pl.ds(1, 7)]
    tally(rests, v_send.at[0], v_recv.at[0]).wait_recv()
    for r in range(1, 8):
        got += gain_rest[r]
    gain_out_ref[...] = got
    for i in range(3):
        each_home(lambda at, i=i: home(i, at, at).wait_recv())
    few_seven = few_rest.at[pl.ds(1, 7)]
    tally(few_seven, fr_send.at[1], fr_recv.at[1]).wait_recv()
    for p in range(5):
        for i in range(5):
            share_twin(p, i, 1 - c).wait_recv()
            write(p, i, 1).start()

    tally(full_ref.at[c], t_send.at[0], t_recv.at[0, 0]).wait_send()
    for i in range(2):
        pltpu.make_async_copy(full_ref.at[i], full_out.at[i], leave.at[i]).wait()
    for p in range(5):
        for s in range(4):
            tally(blocks_of(p, s), g_send.at[p, s], g_recv.at[p, s]).wait_send()
    tally(recv.at[pl.ds(0, 15 * size)], d_send.at[0], d_recv.at[0]).wait_send()
    tally(cots, a_send.at[0], a_recv.at[0]).wait_send()
    tally(packs, b_send.at[0], b_recv.at[0]).wait_send()
    tally(gains, u_send.at[0], u_recv.at[0]).wait_send()
    tally(fifteen, om_send.at[0], om_recv.at[0]).wait_send()
    tally(fews, fm_send.at[0], fm_recv.at[0]).wait_send()
    for j in (2, 3):
        partials(j).wait_send()
    halves().wait_send()
    tally(o_x, ox_send.at[0], ox_recv.at[0]).wait_send()
    for d in (1, 3):
        for i in range(3):
            relay(i, d).wait_send()
            settle(i, d).wait_send()
        far(0, d, 1).wait_send()
        far(1, d, 1).wait_send()
    tally(few_seven, fr_send.at[0], fr_recv.at[0]).wait_send()
    tally(few_seven, fr_send.at[1], fr_recv.at[1]).wait_send()
    tally(seven, q_send.at[0], q_recv.at[0]).wait_send()
    tally(rests, v_send.at[0], v_recv.at[0]).wait_send()
    for i in range(3):
        each_home(lambda at, i=i: home(i, at, y).wait_send())


def experts_back(*operands):
    dma = pltpu.SemaphoreType.DMA
    vm = pl.BlockSpec(memory_space=VMEM)
    hbm = pl.BlockSpec(memory_space=pl.ANY)
    shape = jax.ShapeDtypeStruct
    width = 4 * DB
    pairs_of = lambda *dims: [dma(dims), dma(dims)]
    return pl.pallas_call(
        experts_back_kernel,
        out_shape=(
            shape((128, 1024), BF16),
            shape((128, 1024), F32),
            shape((1, 1024), F32),
            shape((4, 3, FFB, DB), BF16),
            shape((16, 1024), F32),
            shape((2, 4, 4, 4, 256, 128), BF16),
            shape((16, 2 * ROWS, width), BF16),
        ),
        in_specs=[hbm] * 18,
        out_specs=(vm,) * 3 + (hbm, vm, hbm, hbm),
        scratch_shapes=[
            VMEM((128, 1024), F32),
            VMEM((128, 8), F32),
            VMEM((8, 128), F32),
            VMEM((128, 1024), BF16),
            VMEM((1, 1024), F32),
            VMEM((8, 1024), F32),
            VMEM((1024, 128), BF16),
            VMEM((3, 64, 2048), BF16),
            VMEM((64, 2048), F32),
            VMEM((1, 2048), F32),
            VMEM((128, 1024), BF16),
            VMEM((1, 1024), F32),
            VMEM((FFQ, DB), BF16),
            VMEM((2, 4, 4, 4, 256, 128), BF16),
            VMEM((4, 4, 128, 1024), BF16),
            VMEM((3 * FFQ, width), BF16),
            VMEM((64 * ROWS, width), BF16),
            VMEM((3072, width), BF16),
            VMEM((32 * ROWS, width), BF16),
            VMEM((32 * ROWS, width), BF16),
            VMEM((2, 8 * ROWS, width), BF16),
            VMEM((8 * ROWS, width), F32),
            VMEM((32 * ROWS, FFQ), BF16),
            VMEM((32 * ROWS, FFQ), BF16),
            VMEM((32 * ROWS, FFQ), BF16),
            VMEM((2, 3, FFQ // 2, DB), BF16),
            VMEM((2, 3, FFQ, DB), BF16),
            VMEM((16, 64, 128), BF16),
            VMEM((16, 1024), F32),
            VMEM((512, 1024), BF16),
            VMEM((3, 512, DB), BF16),
            VMEM((512, DB), BF16),
            VMEM((16, 32, DB), BF16),
            VMEM((16, 16, 128), F32),
            VMEM((16, 128), F32),
            VMEM((16, 128), F32),
            VMEM((8, 16, 128), F32),
            VMEM((64, 2048), BF16),
            VMEM((2048, 128), BF16),
            VMEM((1, 2048), F32),
            VMEM((2048, 128), F32),
            VMEM((3, 64, 2048), BF16),
            VMEM((3, 16, 64, 128), BF16),
            VMEM((192, 1024), BF16),
            VMEM((256, 128), BF16),
            VMEM((8, 192, 128), BF16),
            VMEM((1, 1024), F32),
            VMEM((16, 1, 1024), F32),
            VMEM((8, 1, 1024), F32),
            dma((27,)),
            dma((2,)),
            dma((1,)),
            dma((16,)),
            dma((1,)),
            dma((4,)),
            *pairs_of(4),
            *pairs_of(1),
            *pairs_of(2, 2),
            *pairs_of(2, 3, 2),
            *pairs_of(3, 4),
            *pairs_of(2, 2),
            *pairs_of(1),
            *pairs_of(1),
            *pairs_of(1),
            dma((5, 4)),
            dma((5, 6)),
            dma((1,)),
            dma((5, 5)),
            *pairs_of(1),
            *pairs_of(1),
            *pairs_of(1),
            *pairs_of(1),
            *pairs_of(1),
            *pairs_of(1),
            *pairs_of(2),
        ],
        compiler_params=params(2, 63),
    )(*operands)


def unfold_kernel(
    f_ref,
    o_ref,
    g_ref,
    few_ref,
    y_ref,
    in_ref,
    norm_ref,
    qkv_ref,
    out_ref,
    gate_ref,
    up_ref,
    down_ref,
    router_ref,
    gain_ref,
    y_out_ref,
    in_out_ref,
    norm_out_ref,
):
    y_out_ref[...] = y_ref[...]
    in_out_ref[...] = in_ref[...]
    norm_out_ref[...] = norm_ref[...]
    router_ref[...] = few_ref[:8]
    gain_ref[...] = few_ref[8:9]
    for i in range(3):
        part = f_ref[:, :, 64 * i : 64 * (i + 1)].reshape(1024, 128)
        qkv_ref[:, 1024 * i : 1024 * (i + 1)] = part.T.astype(F32)
    for i in range(4):
        for h in range(2):
            part = o_ref[i, :, 32 * h : 32 * (h + 1)].reshape(128, 128)
            out_ref[:, (2 * i + h) * 128 : (2 * i + h + 1) * 128] = part.astype(F32)
    gate_ref[...] = g_ref[0].astype(F32)
    up_ref[...] = g_ref[1].astype(F32)
    down_ref[...] = g_ref[2].astype(F32)


def unfold(full, blocks, few, block_output, input_grad, gain_grad):
    shape = jax.ShapeDtypeStruct
    share = pl.BlockSpec((None, FFB, 128), lambda i, j: (i, 0, j))
    return pl.pallas_call(
        unfold_kernel,
        out_shape=(
            shape((1024, 3072), F32),
            shape((1024, 1024), F32),
            *[shape((4, FFB, DB), F32)] * 3,
            shape((8, 1024), F32),
            shape((1, 1024), F32),
            shape((128, 1024), BF16),
            shape((128, 1024), F32),
            shape((1, 1024), F32),
        ),
        grid=(4, 2),
        in_specs=[
            pl.BlockSpec((None, None, 4, 4, 192, 128), lambda i, j: (j, i, 0, 0, 0, 0)),
            pl.BlockSpec((None, 4, None, 4, 64, 128), lambda i, j: (j, 0, i, 0, 3, 0)),
            pl.BlockSpec((None, 3, FFB, 128), lambda i, j: (i, 0, 0, j)),
            pl.BlockSpec((16, 1024), lambda i, j: (0, 0)),
            pl.BlockSpec((16, 1024), lambda i, j: (2 * i + j, 0)),
            pl.BlockSpec((16, 1024), lambda i, j: (2 * i + j, 0)),
            pl.BlockSpec((1, 1024), lambda i, j: (0, 0)),
        ],
        out_specs=(
            pl.BlockSpec((128, 3072), lambda i, j: (2 * i + j, 0)),
            pl.BlockSpec((128, 1024), lambda i, j: (4 * j + i, 0)),
            *[share] * 3,
            pl.BlockSpec((8, 1024), lambda i, j: (0, 0)),
            pl.BlockSpec((1, 1024), lambda i, j: (0, 0)),
            pl.BlockSpec((16, 1024), lambda i, j: (2 * i + j, 0)),
            pl.BlockSpec((16, 1024), lambda i, j: (2 * i + j, 0)),
            pl.BlockSpec((1, 1024), lambda i, j: (0, 0)),
        ),
        compiler_params=pltpu.CompilerParams(vmem_limit_bytes=62 * 1024 * 1024),
    )(full, full, blocks, few, block_output, input_grad, gain_grad)


def body(
    block_input,
    attn_gain,
    qkv_weight,
    out_weight,
    moe_gain,
    router_weight,
    gate_weight,
    up_weight,
    down_weight,
    routes,
    slot_index,
    cotangent,
):
    pairs = jnp.concatenate([routes.T, slot_index.T, jnp.zeros((4, 128), jnp.int32)]).astype(F32)
    (
        send,
        middle,
        probs,
        ctx_tok,
        qkv,
        ctx_here,
        lse,
        down,
        near,
        weights,
        qkv_low,
        out_low,
    ) = attend(
        block_input,
        attn_gain,
        gate_weight,
        up_weight,
        down_weight,
        moe_gain,
        router_weight,
        pairs,
        cotangent,
        qkv_weight,
        out_weight,
    )
    block_output, input_grad, gain_grad, mine, few, full, _ = experts_back(
        middle,
        probs,
        pairs,
        cotangent,
        moe_gain.reshape(1, -1),
        router_weight.T,
        ctx_tok,
        qkv,
        ctx_here,
        lse,
        block_input,
        attn_gain.reshape(1, -1),
        down,
        send,
        weights,
        near,
        qkv_low,
        out_low,
    )
    (
        qkv_grad,
        out_grad,
        gate_grad,
        up_grad,
        down_grad,
        router_grad,
        moe_gain_grad,
        block_output,
        input_grad,
        gain_grad,
    ) = unfold(full, mine, few, block_output, input_grad, gain_grad)
    return (
        block_output,
        input_grad,
        gain_grad.reshape(-1),
        qkv_grad,
        out_grad,
        moe_gain_grad.reshape(-1),
        router_grad.T,
        jnp.swapaxes(gate_grad, 1, 2),
        jnp.swapaxes(up_grad, 1, 2),
        down_grad,
    )


def solution(mesh):
    tokens = P(("dp", "expert", "mp"), None)
    cols = P("expert", "dp", "mp")
    rows = P("expert", "mp", "dp")
    return jax.shard_map(
        body,
        mesh=mesh,
        in_specs=(tokens, P(), P(), P(), P(), P(), cols, cols, rows, tokens, tokens, tokens),
        out_specs=(tokens, tokens, P(), P(), P(), P(), P(), cols, cols, rows),
        check_vma=False,
    )
```

```python
import jax
import jax.numpy as jnp
from jax import lax
from jax.experimental import pallas as pl
from jax.experimental.pallas import tpu as pltpu
from jax.sharding import PartitionSpec as P

EPSILON = 1e-06
HIGHEST = lax.Precision.HIGHEST
MESH = pl.DeviceIdType.MESH
F32 = jnp.float32
BF16 = jnp.bfloat16
VMEM = pltpu.VMEM
ROWS = 40
FFB = 176
FFQ = 704
DB = 256
NT = (((1,), (1,)), ((), ()))
TN = (((0,), (0,)), ((), ()))


def dot(a, b):
    return jnp.dot(a, b, preferred_element_type=F32)


def dot_nt(a, b):
    return lax.dot_general(a, b, NT, preferred_element_type=F32)


def dot_tn(a, b):
    return lax.dot_general(a, b, TN, preferred_element_type=F32)


def spot():
    m = lax.axis_index("mp")
    return lax.axis_index("dp"), lax.axis_index("expert"), m, m // 4, m % 4


def params(cid, mb=60):
    return pltpu.CompilerParams(
        collective_id=cid, has_side_effects=True, vmem_limit_bytes=mb * 1024 * 1024
    )


def swapped(c, z):
    return z % 2, 2 * (z // 2) + c


def mp_at(m, k):
    return {"mp": (m + k) % 16}


def ahead(z, y, k):
    return ((z + k % 4 + k // 4) % 4) * 4 + (y + k % 4) % 4


def behind(z, y, k):
    return ((z + 8 - k % 4 - k // 4) % 4) * 4 + (y + 4 - k % 4) % 4


def y_at(z, y, d):
    return {"mp": z * 4 + (y + d) % 4}


def z_at(z, y, d):
    return {"mp": ((z + d) % 4) * 4 + y}


def push(src, dst, send, recv, device):
    return pltpu.make_async_remote_copy(
        src_ref=src, dst_ref=dst, send_sem=send, recv_sem=recv, device_id=device, device_id_type=MESH
    )


def tally(ref, send, recv):
    return push(ref, ref, send, recv, {"expert": 1 - lax.axis_index("expert")})


def lanes(at, size):
    return pl.ds(pl.multiple_of(at * size, size), size)


def greet_mp(barrier, m):
    def one(k, carry):
        pl.semaphore_signal(barrier, inc=1, device_id=mp_at(m, k), device_id_type=MESH)
        return carry

    lax.fori_loop(1, 16, one, 0)


def places(routes, slots):
    return jnp.where(slots < ROWS, routes * (2 * ROWS) + slots, -1.0)


def picks(columns):
    lane = lax.broadcasted_iota(jnp.int32, (128, 8), 1).astype(F32)
    return [(columns[:, j : j + 1] == lane).astype(F32) for j in range(2)]


def gates_of(probs, hot):
    chosen = [jnp.sum(probs * h, axis=1, keepdims=True) for h in hot]
    total = chosen[0] + chosen[1]
    return [v / total for v in chosen], total


def exact(a, b, dims):
    return lax.dot_general(a, b, dims, precision=HIGHEST, preferred_element_type=F32)


def unit(v):
    scale = lax.rsqrt(jnp.mean(v * v, axis=-1, keepdims=True) + EPSILON)
    return v * scale, scale


def attend_kernel(
    x_ref,
    gain_ref,
    gate_ref,
    up_ref,
    downs_ref,
    moe_gain_ref,
    router_ref,
    routes_ref,
    slots_ref,
    cot_ref,
    wq_hbm,
    wo_hbm,
    send_out,
    pairs_out,
    mid_out,
    probs_out,
    ctx_out_ref,
    qkv_out,
    ctx_here_out,
    lse_out,
    down_out,
    nall_ref,
    w_out_ref,
    wq_out_ref,
    wo_out_ref,
    send_ref,
    pairs_ref,
    mid_ref,
    probs_ref,
    ctx_ref,
    qkv_ref,
    ctx_here_ref,
    lse_ref,
    down_ref,
    wq_wide,
    wo_wide,
    wq_ref,
    wo_ref,
    normed,
    heads,
    blocks,
    stage,
    key_rows,
    ctx_low,
    here,
    s_send,
    s_recv,
    x_send,
    x_recv,
    a_send,
    a_recv,
    n_send,
    n_recv,
    c_send,
    c_recv,
):
    x, c, m, z, y = spot()
    pc, pz = swapped(c, z)
    away = (pc - c) * (pc - c)
    barrier = pltpu.get_barrier_semaphore()

    def remote(el):
        return (away == 1) | (el != y)

    def partner(el):
        return {"expert": pc, "mp": pz * 4 + el}

    greet_mp(barrier, m)
    pairs_ref[0:2] = routes_ref[...].astype(F32)
    pairs_ref[2:4] = slots_ref[...].astype(F32)
    pairs_ref[4:8] = jnp.zeros((4, 128), F32)
    for el in range(4):

        @pl.when(remote(el))
        def _():
            pl.semaphore_signal(barrier, inc=1, device_id=partner(el), device_id_type=MESH)

    for d in range(1, 4):
        pl.semaphore_signal(barrier, inc=1, device_id={"dp": (x + d) % 4}, device_id_type=MESH)

    wide = 512

    def load(i):
        cols = pl.ds(i * wide, wide)
        return pltpu.make_async_copy(wq_hbm.at[:, cols], wq_wide.at[:, cols], here.at[4 + i])

    def save(i):
        cols = pl.ds(i * wide, wide)
        return pltpu.make_async_copy(wq_ref.at[:, cols], wq_out_ref.at[:, cols], here.at[4 + i])

    load_o = pltpu.make_async_copy(wo_hbm, wo_wide, here.at[10])
    save_o = pltpu.make_async_copy(wo_ref, wo_out_ref, here.at[10])
    for i in range(6):
        load(i).start()
    load_o.start()
    for el in range(4):
        blocks[el, 0] = gate_ref[el].astype(BF16)
        blocks[el, 1] = up_ref[el].astype(BF16)
        blocks[el, 2] = downs_ref[el].astype(BF16)
    pl.semaphore_wait(barrier, 15 + 6 + away)

    def units(at):
        return stage.at[:, pl.ds(pl.multiple_of(at * FFB, 16), FFB), :]

    def block(i, el, at):
        return push(
            blocks.at[el, i],
            stage.at[i, pl.ds(pl.multiple_of(at * FFB, 16), FFB), :],
            s_send.at[i, el],
            s_recv.at[i, at],
            partner(el),
        )

    def each_block(f):
        for el in range(4):

            @pl.when(remote(el))
            def _(el=el):
                f(el)

    def blocks_out(i):
        each_block(lambda el: block(i, el, y).start())

    def blocks_in(i):
        each_block(lambda el: block(i, el, el).wait_recv())

    blocks_out(0)

    @pl.when(away == 0)
    def _():
        kept = pltpu.make_async_copy(blocks.at[y], units(y), here.at[2])
        kept.start()
        kept.wait()

    normed[...] = (unit(x_ref[...].astype(F32))[0] * gain_ref[...]).astype(BF16)
    half = 512

    def near(part, d):
        cols = pl.ds(part * half, half)
        device = y_at(z, y, d) if part == 0 else z_at(z, y, d)
        return lambda at: push(
            normed.at[:, cols],
            nall_ref.at[at // 4, at % 4, :, cols],
            n_send.at[part, 0, d],
            n_recv.at[part, 0, d],
            device,
        )

    y_from = [z * 4 + (y + 4 - d) % 4 for d in range(4)]
    z_from = [((z + 4 - d) % 4) * 4 + y for d in range(4)]

    def far(part, d, origin):
        cols = pl.ds(part * half, half)
        if part == 0:
            ref, device = nall_ref.at[origin // 4, :, :, cols], z_at(z, y, d)
        else:
            ref, device = nall_ref.at[:, origin % 4, :, cols], y_at(z, y, d)
        return push(ref, ref, n_send.at[part, 1, d], n_recv.at[part, 1, d], device)

    for i in range(6):
        load(i).wait()
        cols = slice(i * wide, (i + 1) * wide)
        wq_ref[:, cols] = wq_wide[:, cols].astype(BF16)
        save(i).start()
        part = dot(normed[...], wq_ref[:, cols])
        heads[i // 2, (i % 2) * 8 : (i % 2) * 8 + 8] = part.T.astype(BF16).reshape(8, 64, 128)

    def head_out(k):
        t = ahead(z, y, k)
        return push(
            heads.at[:, t],
            qkv_ref.at[:, :, lanes(m, 128)],
            a_send.at[0],
            a_recv.at[0],
            {"mp": t},
        )

    def each(lo, hi, f):
        def one(k, carry):
            f(k)
            return carry

        lax.fori_loop(lo, hi, one, 0)

    each(1, 16, lambda k: head_out(k).start())
    own = pltpu.make_async_copy(heads.at[:, m], qkv_ref.at[:, :, lanes(m, 128)], here.at[0])
    own.start()
    mine = pltpu.make_async_copy(normed, nall_ref.at[z, y], here.at[1])
    mine.start()
    blocks_out(1)
    blocks_out(2)
    for d in (2, 1, 3):
        near(0, d)(m).start()
        near(1, d)(m).start()


    def fan(i, d, step, at):
        rows = pl.ds(0, FFQ) if step == 0 else pl.ds(0 if d == 1 else FFQ // 2, FFQ // 2)
        cols = w_out_ref.at[i, rows, lanes(at, DB)]
        return push(
            stage.at[i] if step == 0 else cols,
            cols,
            x_send.at[i, step, d],
            x_recv.at[i, step, d],
            {"dp": (x + d) % 4},
        )

    def fan_wait(i, step):
        for d in (1, 3):
            fan(i, d, step, (x + 8 - d * (1 + step)) % 4).wait_recv()

    def fan_start(i, step):
        for d in (1, 3):
            fan(i, d, step, x if step == 0 else (x + 4 - d) % 4).start()

    def fan_own(i):
        return pltpu.make_async_copy(stage.at[i], w_out_ref.at[i, :, lanes(x, DB)], here.at[2 + i])

    blocks_in(0)
    fan_start(0, 0)
    fan_own(0).start()
    load_o.wait()
    wo_ref[...] = wo_wide[...].astype(BF16)
    save_o.start()

    own.wait()
    some = qkv_ref.at[:, :, pl.ds(0, 15 * 128)]
    tally(some, a_send.at[0], a_recv.at[0]).wait_recv()

    key_rows[...] = qkv_ref[1].astype(F32).T.astype(BF16)

    def ctx_out(t):
        return push(
            ctx_low.at[:, lanes(t, 128)],
            ctx_ref.at[pl.ds(pl.multiple_of(m * 64, 64), 64), :],
            c_send.at[0],
            c_recv.at[0],
            {"mp": t},
        )

    def queries(i):
        b = (m // 2 + i) % 8
        cols = lanes(b, 256)
        q = (qkv_ref[0, :, cols].astype(F32) * 0.125).astype(BF16)
        s = dot(key_rows[...], q)
        top = jnp.max(s, axis=0, keepdims=True)
        p = jnp.exp(s - top)
        total = jnp.sum(p, axis=0, keepdims=True)
        ctx = dot(qkv_ref[2], p.astype(BF16)) / total
        lse_ref[:, cols] = top + jnp.log(total)
        ctx_here_ref[:, cols] = ctx
        ctx_low[:, cols] = ctx.astype(BF16)

    def pair(i, carry):
        queries(2 * i)
        queries(2 * i + 1)
        for u in range(2):
            b = (m // 2 + 2 * i + u) % 8
            for v in range(2):
                t = 2 * b + v

                @pl.when(t != m)
                def _():
                    ctx_out(t).start()

        @pl.when(i == 0)
        def _():
            blocks_in(1)
            fan_start(1, 0)
            fan_own(1).start()

        @pl.when(i == 1)
        def _():
            fan_wait(0, 0)
            fan_start(0, 1)
            blocks_in(2)
            down_ref[...] = stage[2]

        return carry

    lax.fori_loop(0, 4, pair, 0)
    for d in (1, 2, 3):
        near(0, d)(y_from[d]).wait_recv()
        near(1, d)(z_from[d]).wait_recv()
    mine.wait()
    for d in (1, 3):
        far(0, d, m).start()
        far(1, d, m).start()
    ctx_ref[pl.ds(pl.multiple_of(m * 64, 64), 64), :] = ctx_low[:, lanes(m, 128)]
    lot = ctx_ref.at[pl.ds(0, 15 * 64)]
    tally(lot, c_send.at[0], c_recv.at[0]).wait_recv()

    fan_wait(1, 0)
    fan_start(1, 1)

    mid = x_ref[...].astype(F32) + dot_tn(ctx_ref[...], wo_ref[...])
    mid_ref[...] = mid
    moe_in = unit(mid)[0] * moe_gain_ref[...]
    logits = exact(moe_in, router_ref[...], NT)
    grown = jnp.exp(logits - jnp.max(logits, axis=1, keepdims=True))
    probs = grown / jnp.sum(grown, axis=1, keepdims=True)
    probs_ref[...] = probs
    gates, _ = gates_of(probs, picks(pairs_ref[...].T))
    upstream = cot_ref[...].astype(F32)
    rows = [moe_in.astype(BF16)] + [(g * upstream).astype(BF16) for g in gates]
    row = lax.broadcasted_iota(jnp.int32, (16 * ROWS, 128), 0).astype(F32)
    at = [places(pairs_ref[j : j + 1], pairs_ref[2 + j : 3 + j]) for j in range(2)]
    hot = [((row == at[0]) | (row == at[1]))] + [row == jnp.where(a < 0, a, a + ROWS) for a in at]
    hot = jnp.concatenate([h.astype(F32) for h in hot], axis=1).astype(BF16)
    sent = dot(hot, jnp.concatenate(rows, axis=0))
    send_ref[...] = sent.astype(BF16).reshape(8, 2 * ROWS, 1024)
    results = (
        (send_ref, send_out),
        (pairs_ref, pairs_out),
        (mid_ref, mid_out),
        (probs_ref, probs_out),
        (ctx_ref, ctx_out_ref),
        (qkv_ref, qkv_out),
        (ctx_here_ref, ctx_here_out),
        (lse_ref, lse_out),
        (down_ref, down_out),
    )
    results = [
        pltpu.make_async_copy(src, dst, here.at[11 + i]) for i, (src, dst) in enumerate(results)
    ]
    for copy in results:
        copy.start()

    for i in range(6):
        save(i).wait()
    save_o.wait()
    fan_wait(0, 1)
    fan_wait(1, 1)
    for d in (1, 3):
        far(0, d, z_from[d]).wait_recv()
        far(1, d, y_from[d]).wait_recv()
    for d in (1, 2, 3):
        near(0, d)(m).wait_send()
        near(1, d)(m).wait_send()
    for d in (1, 3):
        far(0, d, m).wait_send()
        far(1, d, m).wait_send()
    for i in range(2):
        fan_own(i).wait()
        for d in (1, 3):
            for step in range(2):
                fan(i, d, step, x).wait_send()
    tally(some, a_send.at[0], a_recv.at[0]).wait_send()
    tally(lot, c_send.at[0], c_recv.at[0]).wait_send()
    for i in range(3):
        each_block(lambda el, i=i: block(i, el, y).wait_send())
    for copy in results:
        copy.wait()


def attend(
    block_input,
    gain,
    gate_weight,
    up_weight,
    down_weight,
    moe_gain,
    router,
    routes,
    slots,
    cotangent,
    qkv_weight,
    out_weight,
):
    dma = pltpu.SemaphoreType.DMA
    vm = pl.BlockSpec(memory_space=VMEM)
    hbm = pl.BlockSpec(memory_space=pl.ANY)
    shape = jax.ShapeDtypeStruct
    return pl.pallas_call(
        attend_kernel,
        out_shape=(
            shape((8, 2 * ROWS, 1024), BF16),
            shape((8, 128), F32),
            shape((128, 1024), F32),
            shape((128, 8), F32),
            shape((1024, 128), BF16),
            shape((3, 64, 2048), BF16),
            shape((64, 2048), F32),
            shape((1, 2048), F32),
            shape((FFQ, DB), BF16),
            shape((4, 4, 128, 1024), BF16),
            shape((2, FFQ, 4 * DB), BF16),
            shape((1024, 3072), BF16),
            shape((1024, 1024), BF16),
        ),
        in_specs=[vm] * 10 + [hbm] * 2,
        out_specs=(hbm,) * 13,
        scratch_shapes=[
            VMEM((8, 2 * ROWS, 1024), BF16),
            VMEM((8, 128), F32),
            VMEM((128, 1024), F32),
            VMEM((128, 8), F32),
            VMEM((1024, 128), BF16),
            VMEM((3, 64, 2048), BF16),
            VMEM((64, 2048), F32),
            VMEM((1, 2048), F32),
            VMEM((FFQ, DB), BF16),
            VMEM((1024, 3072), F32),
            VMEM((1024, 1024), F32),
            VMEM((1024, 3072), BF16),
            VMEM((1024, 1024), BF16),
            VMEM((128, 1024), BF16),
            VMEM((3, 16, 64, 128), BF16),
            VMEM((4, 3, FFB, DB), BF16),
            VMEM((3, FFQ, DB), BF16),
            VMEM((2048, 64), BF16),
            VMEM((64, 2048), BF16),
            dma((20,)),
            dma((3, 4)),
            dma((3, 4)),
            dma((2, 2, 4)),
            dma((2, 2, 4)),
            dma((1,)),
            dma((1,)),
            dma((2, 2, 4)),
            dma((2, 2, 4)),
            dma((1,)),
            dma((1,)),
        ],
        compiler_params=params(1, 62),
    )(
        block_input,
        gain.reshape(1, -1),
        jnp.swapaxes(gate_weight, 1, 2),
        jnp.swapaxes(up_weight, 1, 2),
        down_weight,
        moe_gain.reshape(1, -1),
        router.T,
        routes.T,
        slots.T,
        cotangent,
        qkv_weight,
        out_weight,
    )


GELU_A = 0.7978845608
GELU_B = 0.044715


def experts_back_kernel(
    mid_hbm,
    probs_hbm,
    pairs_hbm,
    cot_hbm,
    moe_gain_hbm,
    router_hbm,
    tok_hbm,
    qkv_hbm,
    ctx_hbm,
    lse_hbm,
    x_hbm,
    gain_hbm,
    down_hbm,
    send_hbm,
    w_hbm,
    near_hbm,
    wq_hbm,
    wo_hbm,
    y_ref,
    in_ref,
    gain_out_ref,
    g_out_ref,
    few_out_ref,
    full_out,
    ret_ref,
    mid_ref,
    probs_ref,
    pairs_ref,
    cot_ref,
    moe_gain_ref,
    router_ref,
    tok_ref,
    qkv_ref,
    ctx_ref,
    lse_ref,
    x_ref,
    gain_ref,
    down_ref,
    full_ref,
    nall_ref,
    weights,
    recv,
    rows,
    back,
    sib_recv,
    sib_send,
    own_part,
    hid,
    gcs,
    ucs,
    g_relay,
    g_near,
    dctx,
    few,
    o_sib,
    o_x,
    o_q,
    o_mp,
    few_mp,
    few_sum,
    few_done,
    few_rest,
    cot,
    key_values,
    row_dot,
    dkv,
    pc_here,
    pc_tok,
    slices,
    share,
    parts,
    gain_row,
    gain_mp,
    gain_rest,
    here,
    leave,
    d_send,
    d_recv,
    f_send,
    f_recv,
    p_send,
    p_recv,
    r_send,
    r_recv,
    w_send,
    w_recv,
    x_send,
    x_recv,
    s_send,
    s_recv,
    n_send,
    n_recv,
    a_send,
    a_recv,
    b_send,
    b_recv,
    q_send,
    q_recv,
    g_send,
    g_recv,
    t_send,
    t_recv,
    u_send,
    u_recv,
    v_send,
    v_recv,
    o_send,
    o_recv,
    ox_send,
    ox_recv,
    om_send,
    om_recv,
    fm_send,
    fm_recv,
    fr_send,
    fr_recv,
):
    x, c, m, z, y = spot()
    pc, pz = swapped(c, z)
    away = (pc - c) * (pc - c)
    barrier = pltpu.get_barrier_semaphore()

    def remote(el):
        return (away == 1) | (el != y)

    def partner(el):
        return {"expert": pc, "mp": pz * 4 + el}

    def rest(r):
        return {"dp": (x + r % 4) % 4, "expert": (c + r // 4) % 2}

    def each(lo, hi, f):
        def one(k, carry):
            f(k)
            return carry

        lax.fori_loop(lo, hi, one, 0)

    def local(src, dst, i):
        return pltpu.make_async_copy(src, dst, here.at[i])

    twin = {"expert": 1 - c}
    size = 2 * ROWS

    greet_mp(barrier, m)
    for el in range(4):

        @pl.when(remote(el))
        def _():
            pl.semaphore_signal(barrier, inc=1, device_id=partner(el), device_id_type=MESH)

    for r in range(1, 8):
        pl.semaphore_signal(barrier, inc=1, device_id=rest(r), device_id_type=MESH)
    operands = [
        local(src, dst, 14 + i)
        for i, (src, dst) in enumerate(
            (
                (down_hbm, down_ref),
                (mid_hbm, mid_ref),
                (probs_hbm, probs_ref),
                (pairs_hbm, pairs_ref),
                (cot_hbm, cot_ref),
                (moe_gain_hbm, moe_gain_ref),
                (router_hbm, router_ref),
                (tok_hbm, tok_ref),
                (qkv_hbm, qkv_ref),
                (ctx_hbm, ctx_ref),
                (lse_hbm, lse_ref),
                (x_hbm, x_ref),
                (gain_hbm, gain_ref),
            )
        )
    ]
    for copy in operands:
        copy.start()
    load_w = [local(w_hbm.at[i], weights.at[pl.ds(i * FFQ, FFQ)], i) for i in range(2)]
    for copy in load_w:
        copy.start()
    near = []
    for i, d in enumerate((0, 1, 3)):
        at = (z + d) % 4, slice(None), slice(None), pl.ds(0, 512)
        near.append(local(near_hbm.at[at], nall_ref.at[at], 8 + i))
        at = slice(None), (y + d) % 4, slice(None), pl.ds(512, 512)
        near.append(local(near_hbm.at[at], nall_ref.at[at], 11 + i))
    for copy in near:
        copy.start()
    pl.semaphore_wait(barrier, 15 + 3 + away + 7)

    def expert_of(t):
        return ((t // 4) % 2) * 4 + t % 4

    def slot(core, k, n=1):
        return pl.ds(pl.multiple_of((core * 16 + k) * size, size), n * size)

    def dispatch(k):
        t = ahead(z, y, k)
        return push(
            send_hbm.at[expert_of(t)],
            recv.at[slot(0, k)],
            d_send.at[0],
            d_recv.at[k],
            {"mp": t},
        )

    def forward(k):
        return push(
            recv.at[slot(0, k)], recv.at[slot(1, k)], f_send.at[0], f_recv.at[k // 4], twin
        )

    def partials(j):
        return push(
            sib_send.at[j % 2],
            sib_recv.at[pl.ds(pl.multiple_of(j * 4 * size, size), 4 * size)],
            p_send.at[j],
            p_recv.at[j],
            twin,
        )

    def spot_of(k, n=1):
        return pl.ds(pl.multiple_of(k * size, size), n * size)

    def giving(k, at):
        return push(
            back.at[spot_of(k)], ret_ref.at[at], r_send.at[0], r_recv.at[0], {"mp": behind(z, y, k)}
        )

    def down_fan(d, step, at):
        part = pl.ds(0, FFQ) if step == 0 else pl.ds(0 if d == 1 else FFQ // 2, FFQ // 2)
        units = pl.ds(2 * FFQ + part.start, part.size)
        there = weights.at[units, lanes(at, DB)]
        return push(
            down_ref if step == 0 else there,
            there,
            w_send.at[step, d // 2],
            w_recv.at[step, d // 2],
            {"dp": (x + d) % 4},
        )

    operands[0].wait()
    for d in (1, 3):
        down_fan(d, 0, x).start()
    each(1, 16, lambda k: dispatch(k).start())
    own = local(send_hbm.at[expert_of(m)], recv.at[slot(0, 0)], 4)
    own.start()
    weights[2 * FFQ :, lanes(x, DB)] = down_ref[...]
    own.wait()

    def finish(j):
        partials(j).wait_recv()
        span = spot_of(4 * j, 4)
        back[span] = (own_part[...] + sib_recv[span].astype(F32)).astype(BF16)
        for i in range(4):
            k = 4 * j + i

            @pl.when(k > 0)
            def _():
                giving(k, m).start()

            @pl.when(k == 0)
            def _():
                local(back.at[spot_of(0)], ret_ref.at[m], 4).start()

    gate_w, up_w, down_w = (slice(i * FFQ, (i + 1) * FFQ) for i in range(3))
    cot_rows = 32 * ROWS

    def chunk(j, carry):
        for i in range(4):
            k = 4 * j + i

            @pl.when(k > 0)
            def _():
                dispatch(k).wait_recv()

            forward(k).start()

        @pl.when(j > 0)
        def _():
            finish(j - 1)

        @pl.when(j == 0)
        def _():
            for copy in load_w:
                copy.wait()
            for d in (1, 3):
                down_fan(d, 1, (x + 2) % 4).wait_recv()

        tally(recv.at[slot(1, 4 * j, 4)], f_send.at[0], f_recv.at[j]).wait_recv()
        xs = pl.ds(pl.multiple_of(j * 8 * ROWS, 16), 8 * ROWS)
        cs = pl.ds(pl.multiple_of(cot_rows + j * 8 * ROWS, 16), 8 * ROWS)
        for r in range(2):
            blk = recv[slot(r, 4 * j, 4)].astype(F32).reshape(4, size, 4 * DB)
            for at, part in ((0, blk[:, :ROWS]), (cot_rows, blk[:, ROWS:])):
                span = pl.ds(pl.multiple_of(at + (2 * j + r) * 4 * ROWS, 16), 4 * ROWS)
                rows[span] = part.reshape(4 * ROWS, 4 * DB).astype(BF16)
        gate = dot_nt(rows[xs], weights[gate_w])
        up = dot_nt(rows[xs], weights[up_w])
        hid_cot = dot_nt(rows[cs], weights[down_w])
        sq = gate * gate
        th = jnp.tanh(GELU_A * (gate + GELU_B * (gate * sq)))
        half = 0.5 * (1.0 + th)
        act = gate * half
        slope = half + 0.5 * gate * (1.0 - th * th) * (GELU_A * (1.0 + 3.0 * GELU_B * sq))
        hid[xs] = (act * up).astype(BF16)
        gcs[xs] = (hid_cot * up * slope).astype(BF16)
        ucs[xs] = (hid_cot * act).astype(BF16)
        out = dot(hid[xs], weights[down_w]).reshape(2, 4, ROWS, 4 * DB)
        low = dot(gcs[xs], weights[gate_w]) + dot(ucs[xs], weights[up_w])
        low = low.reshape(2, 4, ROWS, 4 * DB)
        own_part[...] = jnp.concatenate([out[0], low[0]], axis=1).reshape(4 * size, 4 * DB)

        @pl.when(j > 1)
        def _():
            partials(j - 2).wait_send()

        sib_send[j % 2] = (
            jnp.concatenate([out[1], low[1]], axis=1).reshape(4 * size, 4 * DB).astype(BF16)
        )
        partials(j).start()
        return carry

    for d in (1, 3):
        down_fan(d, 0, (x + 4 - d) % 4).wait_recv()
        down_fan(d, 1, (x + 4 - d) % 4).start()
    lax.fori_loop(0, 4, chunk, 0)
    finish(3)
    tally(recv.at[slot(0, 0, 16)], f_send.at[0], f_recv.at[0]).wait_send()
    for d in (1, 3):
        down_fan(d, 0, x).wait_send()
        down_fan(d, 1, x).wait_send()
    load_o = local(wo_hbm, weights.at[pl.ds(0, 1024)], 0)
    load_o.start()

    unit_half = FFQ // 2

    def unit_rows(i, d):
        return pl.ds(i * FFQ + (0 if d == 1 else unit_half), unit_half)

    def relay(i, d):
        return push(
            recv.at[unit_rows(i, d), lanes((x + 2) % 4, DB)],
            g_relay.at[d // 2, i],
            x_send.at[0, i, d // 2],
            x_recv.at[0, i, d // 2],
            {"dp": (x + d) % 4},
        )

    def settle(i, d):
        return push(
            recv.at[pl.ds(i * FFQ, FFQ), lanes((x + d) % 4, DB)],
            g_near.at[d // 2, i],
            x_send.at[1, i, d // 2],
            x_recv.at[1, i, d // 2],
            {"dp": (x + d) % 4},
        )

    for i, (a, at) in enumerate(((gcs, 0), (ucs, 0), (hid, cot_rows))):
        g = dot_tn(a[...], rows[at : at + cot_rows])
        recv[i * FFQ : (i + 1) * FFQ] = g.astype(BF16)
        for d in (1, 3):
            relay(i, d).start()
    load_q = [
        local(wq_hbm.at[:, pl.ds(i * 1024, 1024)], rows.at[pl.ds(i * 1024, 1024)], 5 + i)
        for i in range(3)
    ]
    for copy in load_q:
        copy.start()
    for i in range(3):
        for d in (1, 3):
            relay(i, d).wait_recv()
            span, cols = unit_rows(i, d), lanes((x + d) % 4, DB)
            recv[span, cols] = (
                recv[span, cols].astype(F32) + g_relay[d // 2, i].astype(F32)
            ).astype(BF16)
            settle(i, d).start()

    def home(i, at, to):
        return push(
            recv.at[pl.ds(i * FFQ + at * FFB, FFB), lanes(x, DB)],
            g_out_ref.at[to, i],
            s_send.at[i, at],
            s_recv.at[i, to],
            partner(at),
        )

    def each_home(f):
        for at in range(4):

            @pl.when(remote(at))
            def _(at=at):
                f(at)

    def go_home(i):
        for d in (1, 3):
            settle(i, d).wait_recv()
        span, cols = pl.ds(i * FFQ, FFQ), lanes(x, DB)
        recv[span, cols] = (
            recv[span, cols].astype(F32) + g_near[0, i].astype(F32) + g_near[1, i].astype(F32)
        ).astype(BF16)
        each_home(lambda at: home(i, at, y).start())

        @pl.when(away == 0)
        def _():
            kept = local(
                recv.at[pl.ds(pl.multiple_of(i * FFQ + y * FFB, 16), FFB), cols], g_out_ref.at[y, i], 1
            )
            kept.start()
            kept.wait()

    local(back.at[spot_of(0)], ret_ref.at[m], 4).wait()
    tally(back.at[spot_of(1, 15)], r_send.at[0], r_recv.at[0]).wait_send()
    tally(ret_ref.at[pl.ds(0, 15)], r_send.at[0], r_recv.at[0]).wait_recv()
    load_r = local(ret_ref, back.reshape(16, size, 4 * DB), 4)
    load_r.start()
    load_r.wait()

    for copy in (*near, *operands[1:]):
        copy.wait()

    def far(part, d, hops):
        cols, some = pl.ds(part * 512, 512), pl.ds(0 if d == 1 else 2, 2)
        if part == 0:
            ref, device = nall_ref.at[(z + 8 - hops * d) % 4, some, :, cols], z_at(z, y, d)
        else:
            ref, device = nall_ref.at[some, (y + 8 - hops * d) % 4, :, cols], y_at(z, y, d)
        return push(ref, ref, n_send.at[part, d // 2], n_recv.at[part, d // 2], device)

    columns = pairs_ref[...].T
    hot = picks(columns)
    probs = probs_ref[...]
    gates, total = gates_of(probs, hot)
    at = places(columns[:, 0:2], columns[:, 2:4])
    lane = lax.broadcasted_iota(jnp.int32, (128, 16 * ROWS), 1).astype(F32)
    at = [at[:, j : j + 1] for j in range(2)]
    given = (back[: 8 * size].astype(F32) + back[8 * size :].astype(F32)).astype(BF16)
    fetched = [dot((lane == a).astype(F32).astype(BF16), given) for a in at]
    low = [lane == jnp.where(a < 0, a, a + ROWS) for a in at]
    moe_cot = dot((low[0] | low[1]).astype(F32).astype(BF16), given)
    mid = mid_ref[...]
    upstream = cot_ref[...].astype(F32)
    y_ref[...] = (mid + gates[0] * fetched[0] + gates[1] * fetched[1]).astype(BF16)
    gate_cot = [jnp.sum(upstream * f, axis=1, keepdims=True) for f in fetched]
    inner = gate_cot[0] * gates[0] + gate_cot[1] * gates[1]
    probs_cot = sum(h * ((g - inner) / total) for h, g in zip(hot, gate_cot))
    logit_cot = probs * (probs_cot - jnp.sum(probs * probs_cot, axis=1, keepdims=True))
    hat, scale = unit(mid)
    moe_cot += exact(logit_cot, router_ref[...], (((1,), (0,)), ((), ())))
    few[:8] = exact(logit_cot, hat * moe_gain_ref[...], TN)
    few[8:] = jnp.concatenate(
        [jnp.sum(moe_cot * hat, axis=0, keepdims=True), jnp.zeros((7, 1024), F32)], axis=0
    )
    gained = moe_cot * moe_gain_ref[...]
    in_ref[...] = upstream + scale * (gained - hat * jnp.mean(gained * hat, axis=-1, keepdims=True))
    branch_cot = in_ref[...].astype(BF16)
    load_o.wait()
    dctx[...] = dot_nt(weights[:1024], branch_cot).astype(BF16).reshape(16, 64, 128)

    def cot_out(k):
        t = ahead(z, y, k)
        return push(dctx.at[t], cot.at[:, lanes(m, 128)], a_send.at[0], a_recv.at[0], {"mp": t})

    each(1, 16, lambda k: cot_out(k).start())
    for d in (1, 3):
        far(0, d, 1).start()
        far(1, d, 1).start()
    cot[:, lanes(m, 128)] = dctx[m]

    weights[1024:2048] = dot(tok_ref[...], branch_cot).astype(BF16)

    def halves():
        rows_at = pl.ds(pl.multiple_of(1024 + (1 - c) * 512, 512), 512)
        return push(weights.at[rows_at], o_sib, o_send.at[0], o_recv.at[0], twin)

    def quarters(d):
        t = (x + d) % 4
        return push(
            weights.at[pl.ds(0, 512), lanes(t, DB)], o_x.at[d - 1], ox_send.at[0], ox_recv.at[0], {"dp": t}
        )

    def thirty(k):
        t = ahead(z, y, k)
        return push(
            o_q.at[pl.ds(pl.multiple_of(t * 32, 32), 32)],
            o_mp.at[k],
            om_send.at[0],
            om_recv.at[0],
            {"mp": t},
        )

    def few_share(r):
        t = 2 * ((x + r % 4) % 4) + (c + r // 4) % 2
        return push(
            few.at[:, lanes(t, 128)], few_rest.at[r], fr_send.at[0], fr_recv.at[0], rest(r)
        )

    def few_near(k):
        return push(few_sum, few_mp.at[k], fm_send.at[0], fm_recv.at[0], mp_at(m, k))

    def few_back(r, back_from):
        t = 2 * ((x + 4 - r % 4) % 4) + (c + r // 4) % 2 if back_from else 2 * x + c
        return push(
            few_done, few_out_ref.at[:, lanes(t, 128)], fr_send.at[1], fr_recv.at[1], rest(r)
        )

    halves().start()
    for r in range(1, 8):
        few_share(r).start()

    def along(axis, d):
        if axis == 0:
            return {"dp": (x + d) % 4}
        return z_at(z, y, d) if axis == 1 else y_at(z, y, d)

    orders = ((0, 2, 1), (0, 1, 2), (2, 1, 0), (0, 2, 1), (2, 1, 0))
    spans = [pl.ds(0, 64), pl.ds(64, 64), pl.ds(128, 64), pl.ds(192, 32), pl.ds(224, 32)]

    def spread(p, s, d, incoming):
        at = [x, z, y]
        axis = orders[p][s]
        if incoming:
            at[axis] = (at[axis] + 4 - d) % 4
        src = [x, z, y]
        for done in orders[p][:s]:
            at[done] = slice(None)
            src[done] = slice(None)
        return push(
            full_ref.at[(c, *src, spans[p])],
            full_ref.at[(c, *at, spans[p])],
            g_send.at[p, s],
            g_recv.at[p, s],
            along(axis, d),
        )

    def spread_start(p, s):
        for d in (2, 1, 3):
            spread(p, s, d, False).start()

    def last(p, d, hops):
        at = [slice(None)] * 3
        axis = orders[p][2]
        at[axis] = ((x, z, y)[axis] + 8 - hops * d) % 4
        return at

    def circle(p, d, step, incoming):
        at = last(p, d, step + incoming)
        if step:
            at[orders[p][0]] = pl.ds(0 if d == 1 else 2, 2)
        ref = full_ref.at[(c, *at, spans[p])]
        return push(ref, ref, g_send.at[p, 2 + step], g_recv.at[p, 2 + 2 * step + d // 2], along(orders[p][2], d))

    def blocks_of(p, s):
        at = ((0, 0, pl.ds(0, 3)), (0, pl.ds(0, 3), slice(None)), (pl.ds(0, 2),), (pl.ds(0, 1),))[s]
        at = (*at, *[slice(None)] * (3 - len(at)))
        return full_ref.at[(c, *at, spans[p])]

    def spread_wait(p, s):
        tally(blocks_of(p, s), g_send.at[p, s], g_recv.at[p, s]).wait_recv()

    def piece(p, i, core):
        d, hops = ((1, 0), (1, 1), (3, 1), (1, 2), (3, 2))[i]
        at = last(p, d, hops)
        if hops == 2:
            at[orders[p][0]] = pl.ds(0 if d == 1 else 2, 2)
        return (core, *at, spans[p])

    def share_twin(p, i, core):
        ref = full_ref.at[piece(p, i, core)]
        return push(ref, ref, t_send.at[0], t_recv.at[p, i], twin)

    def write(p, i, other):
        at = piece(p, i, 1 - c if other else c)
        return pltpu.make_async_copy(full_ref.at[at], full_out.at[at], leave.at[other])

    def hand_on(p, i):
        share_twin(p, i, c).start()
        write(p, i, 0).start()

    key_values[...] = qkv_ref[1:].reshape(128, 2048).astype(F32).T.astype(BF16)
    dkv[...] = jnp.zeros_like(dkv)
    halves().wait_recv()
    weights[:512] = (
        weights[pl.ds(pl.multiple_of(1024 + c * 512, 512), 512)].astype(F32) + o_sib[...].astype(F32)
    ).astype(BF16)
    for d in (2, 1, 3):
        quarters(d).start()
    go_home(0)
    cots = cot.at[:, pl.ds(0, 15 * 128)]
    tally(cots, a_send.at[0], a_recv.at[0]).wait_recv()
    row_dot[...] = jnp.sum(cot[...].astype(F32) * ctx_ref[...], axis=0, keepdims=True)

    def queries(b):
        cols = lanes(b, 256)
        q = (qkv_ref[0, :, cols].astype(F32) * 0.125).astype(BF16)
        none = jnp.zeros((64, 256), BF16)
        q = jnp.concatenate([q, none], axis=0)
        g = jnp.concatenate([none, cot[:, cols]], axis=0)
        p = jnp.exp(dot(key_values[...], q) - lse_ref[:, cols])
        dp = dot(key_values[...], g)
        ds = (p * (dp - row_dot[:, cols])).astype(BF16)
        pc_here[0, :, cols] = (dot(qkv_ref[1], ds) * 0.125).astype(BF16)
        dkv[...] += dot_nt(ds, q) + dot_nt(p.astype(BF16), g)

    def pair(i, carry):
        queries(2 * i)
        queries(2 * i + 1)

        @pl.when(i == 1)
        def _():
            go_home(1)

        @pl.when(i == 2)
        def _():
            few_all = few[:, lanes(2 * x + c, 128)]
            tally(few_rest.at[pl.ds(1, 7)], fr_send.at[0], fr_recv.at[0]).wait_recv()
            for r in range(1, 8):
                few_all += few_rest[r]
            few_sum[...] = few_all
            each(1, 16, lambda k: few_near(k).start())
            go_home(2)

        return carry

    lax.fori_loop(0, 4, pair, 0)
    pc_here[1:] = dkv[...].T.astype(BF16).reshape(2, 64, 2048)

    def pc_out(k):
        t = ahead(z, y, k)
        return push(
            pc_here.at[:, :, lanes(t, 128)], pc_tok.at[:, m], b_send.at[0], b_recv.at[0], {"mp": t}
        )

    for d in (1, 3):
        far(0, d, 2).wait_recv()
        far(1, d, 2).wait_recv()
    long = pc_here[...].reshape(192, 2048)
    slices[...] = dot(long, nall_ref[...].reshape(2048, 1024)).astype(BF16)

    def share_out(r):
        t = 2 * ((x + r % 4) % 4) + (c + r // 4) % 2
        return push(slices.at[:, lanes(t, 128)], parts.at[r], q_send.at[0], q_recv.at[0], rest(r))

    for r in range(1, 8):
        share_out(r).start()
    each(1, 16, lambda k: pc_out(k).start())
    pc_tok[:, m] = pc_here[:, :, lanes(m, 128)]

    tally(o_x, ox_send.at[0], ox_recv.at[0]).wait_recv()
    o_sum = weights[:512, lanes(x, DB)].astype(F32)
    for d in (1, 2, 3):
        o_sum += o_x[d - 1].astype(F32)
    o_q[...] = o_sum.astype(BF16)
    each(1, 16, lambda k: thirty(k).start())
    whole = slices[:, lanes(2 * x + c, 128)].astype(F32)
    seven = parts.at[pl.ds(1, 7)]
    tally(seven, q_send.at[0], q_recv.at[0]).wait_recv()
    for r in range(1, 8):
        whole += parts[r].astype(F32)
    share[:192] = whole.astype(BF16)
    lay = local(share.at[pl.ds(0, 192)], full_ref.at[c, x, z, y, pl.ds(0, 192)], 2)
    lay.start()
    lay.wait()
    for p in range(3):
        spread_start(p, 0)
    def circles(p):
        spread_wait(p, 1)
        for d in (1, 3):
            circle(p, d, 0, 0).start()
        hand_on(p, 0)

    for p in range(2):
        spread_wait(p, 0)
        spread_start(p, 1)
    fifteen = o_mp.at[pl.ds(1, 15)]
    tally(fifteen, om_send.at[0], om_recv.at[0]).wait_recv()
    o_sum = o_q[pl.ds(pl.multiple_of(m * 32, 32), 32)].astype(F32)
    for k in range(1, 16):
        o_sum += o_mp[k].astype(F32)
    o_low = o_sum.astype(BF16)
    share[192:224] = o_low[:, :128]
    share[224:] = o_low[:, 128:]
    lay = local(share.at[pl.ds(192, 64)], full_ref.at[c, x, z, y, pl.ds(192, 64)], 2)
    lay.start()
    lay.wait()
    for p in (3, 4):
        spread_start(p, 0)

    spread_wait(2, 0)
    spread_start(2, 1)
    for p in range(3):
        circles(p)
    for p in (3, 4):
        spread_wait(p, 0)
        spread_start(p, 1)

    packs = pc_here.at[:, :, pl.ds(0, 15 * 128)]
    tally(packs, b_send.at[0], b_recv.at[0]).wait_recv()
    for copy in load_q:
        copy.wait()
    dn = sum(dot(rows[i * 1024 : (i + 1) * 1024], pc_tok[i].reshape(1024, 128)) for i in range(3)).T
    hat, scale = unit(x_ref[...].astype(F32))
    gained = dn * gain_ref[...]
    in_ref[...] = in_ref[...] + scale * (
        gained - hat * jnp.mean(gained * hat, axis=-1, keepdims=True)
    )
    gain_row[...] = jnp.sum(dn * hat, axis=0, keepdims=True)

    def gain_out(k):
        return push(gain_row, gain_mp.at[k], u_send.at[0], u_recv.at[0], mp_at(m, k))

    def gain_far(r):
        return push(gain_mp.at[0], gain_rest.at[r], v_send.at[0], v_recv.at[0], rest(r))

    each(1, 16, lambda k: gain_out(k).start())
    for p in (3, 4):
        circles(p)

    def onward(p):
        for i, d in ((1, 1), (2, 3)):
            circle(p, d, 0, 1).wait_recv()
            circle(p, d, 1, 0).start()
            hand_on(p, i)

    for p in range(3):
        onward(p)
    gains = gain_mp.at[pl.ds(1, 15)]
    tally(gains, u_send.at[0], u_recv.at[0]).wait_recv()
    got = gain_row[...]
    for k in range(1, 16):
        got += gain_mp[k]
    gain_mp[0] = got
    for r in range(1, 8):
        gain_far(r).start()
    for p in (3, 4):
        onward(p)
    fews = few_mp.at[pl.ds(1, 15)]
    tally(fews, fm_send.at[0], fm_recv.at[0]).wait_recv()
    few_all = few_sum[...]
    for k in range(1, 16):
        few_all += few_mp[k]
    few_done[...] = few_all
    few_out_ref[:, lanes(2 * x + c, 128)] = few_all
    for r in range(1, 8):
        few_back(r, False).start()
    for p in range(5):
        for i, d in ((3, 1), (4, 3)):
            circle(p, d, 1, 1).wait_recv()
            hand_on(p, i)
    rests = gain_rest.at[pl.ds(1, 7)]
    tally(rests, v_send.at[0], v_recv.at[0]).wait_recv()
    for r in range(1, 8):
        got += gain_rest[r]
    gain_out_ref[...] = got
    for i in range(3):
        each_home(lambda at, i=i: home(i, at, at).wait_recv())
    few_seven = few_rest.at[pl.ds(1, 7)]
    tally(few_seven, fr_send.at[1], fr_recv.at[1]).wait_recv()
    for p in range(5):
        for i in range(5):
            share_twin(p, i, 1 - c).wait_recv()
            write(p, i, 1).start()

    tally(full_ref.at[c], t_send.at[0], t_recv.at[0, 0]).wait_send()
    for i in range(2):
        pltpu.make_async_copy(full_ref.at[i], full_out.at[i], leave.at[i]).wait()
    for p in range(5):
        for s in range(4):
            tally(blocks_of(p, s), g_send.at[p, s], g_recv.at[p, s]).wait_send()
    tally(recv.at[pl.ds(0, 15 * size)], d_send.at[0], d_recv.at[0]).wait_send()
    tally(cots, a_send.at[0], a_recv.at[0]).wait_send()
    tally(packs, b_send.at[0], b_recv.at[0]).wait_send()
    tally(gains, u_send.at[0], u_recv.at[0]).wait_send()
    tally(fifteen, om_send.at[0], om_recv.at[0]).wait_send()
    tally(fews, fm_send.at[0], fm_recv.at[0]).wait_send()
    for j in (2, 3):
        partials(j).wait_send()
    halves().wait_send()
    tally(o_x, ox_send.at[0], ox_recv.at[0]).wait_send()
    for d in (1, 3):
        for i in range(3):
            relay(i, d).wait_send()
            settle(i, d).wait_send()
        far(0, d, 1).wait_send()
        far(1, d, 1).wait_send()
    tally(few_seven, fr_send.at[0], fr_recv.at[0]).wait_send()
    tally(few_seven, fr_send.at[1], fr_recv.at[1]).wait_send()
    tally(seven, q_send.at[0], q_recv.at[0]).wait_send()
    tally(rests, v_send.at[0], v_recv.at[0]).wait_send()
    for i in range(3):
        each_home(lambda at, i=i: home(i, at, y).wait_send())


def experts_back(*operands):
    dma = pltpu.SemaphoreType.DMA
    vm = pl.BlockSpec(memory_space=VMEM)
    hbm = pl.BlockSpec(memory_space=pl.ANY)
    shape = jax.ShapeDtypeStruct
    width = 4 * DB
    pairs_of = lambda *dims: [dma(dims), dma(dims)]
    return pl.pallas_call(
        experts_back_kernel,
        out_shape=(
            shape((128, 1024), BF16),
            shape((128, 1024), F32),
            shape((1, 1024), F32),
            shape((4, 3, FFB, DB), BF16),
            shape((16, 1024), F32),
            shape((2, 4, 4, 4, 256, 128), BF16),
            shape((16, 2 * ROWS, width), BF16),
        ),
        in_specs=[hbm] * 18,
        out_specs=(vm,) * 3 + (hbm, vm, hbm, hbm),
        scratch_shapes=[
            VMEM((128, 1024), F32),
            VMEM((128, 8), F32),
            VMEM((8, 128), F32),
            VMEM((128, 1024), BF16),
            VMEM((1, 1024), F32),
            VMEM((8, 1024), F32),
            VMEM((1024, 128), BF16),
            VMEM((3, 64, 2048), BF16),
            VMEM((64, 2048), F32),
            VMEM((1, 2048), F32),
            VMEM((128, 1024), BF16),
            VMEM((1, 1024), F32),
            VMEM((FFQ, DB), BF16),
            VMEM((2, 4, 4, 4, 256, 128), BF16),
            VMEM((4, 4, 128, 1024), BF16),
            VMEM((3 * FFQ, width), BF16),
            VMEM((64 * ROWS, width), BF16),
            VMEM((3072, width), BF16),
            VMEM((32 * ROWS, width), BF16),
            VMEM((32 * ROWS, width), BF16),
            VMEM((2, 8 * ROWS, width), BF16),
            VMEM((8 * ROWS, width), F32),
            VMEM((32 * ROWS, FFQ), BF16),
            VMEM((32 * ROWS, FFQ), BF16),
            VMEM((32 * ROWS, FFQ), BF16),
            VMEM((2, 3, FFQ // 2, DB), BF16),
            VMEM((2, 3, FFQ, DB), BF16),
            VMEM((16, 64, 128), BF16),
            VMEM((16, 1024), F32),
            VMEM((512, 1024), BF16),
            VMEM((3, 512, DB), BF16),
            VMEM((512, DB), BF16),
            VMEM((16, 32, DB), BF16),
            VMEM((16, 16, 128), F32),
            VMEM((16, 128), F32),
            VMEM((16, 128), F32),
            VMEM((8, 16, 128), F32),
            VMEM((64, 2048), BF16),
            VMEM((2048, 128), BF16),
            VMEM((1, 2048), F32),
            VMEM((2048, 128), F32),
            VMEM((3, 64, 2048), BF16),
            VMEM((3, 16, 64, 128), BF16),
            VMEM((192, 1024), BF16),
            VMEM((256, 128), BF16),
            VMEM((8, 192, 128), BF16),
            VMEM((1, 1024), F32),
            VMEM((16, 1, 1024), F32),
            VMEM((8, 1, 1024), F32),
            dma((27,)),
            dma((2,)),
            dma((1,)),
            dma((16,)),
            dma((1,)),
            dma((4,)),
            *pairs_of(4),
            *pairs_of(1),
            *pairs_of(2, 2),
            *pairs_of(2, 3, 2),
            *pairs_of(3, 4),
            *pairs_of(2, 2),
            *pairs_of(1),
            *pairs_of(1),
            *pairs_of(1),
            dma((5, 4)),
            dma((5, 6)),
            dma((1,)),
            dma((5, 5)),
            *pairs_of(1),
            *pairs_of(1),
            *pairs_of(1),
            *pairs_of(1),
            *pairs_of(1),
            *pairs_of(1),
            *pairs_of(2),
        ],
        compiler_params=params(2, 63),
    )(*operands)


def unfold_kernel(
    f_ref,
    o_ref,
    g_ref,
    few_ref,
    y_ref,
    in_ref,
    norm_ref,
    qkv_ref,
    out_ref,
    gate_ref,
    up_ref,
    down_ref,
    router_ref,
    gain_ref,
    y_out_ref,
    in_out_ref,
    norm_out_ref,
):
    y_out_ref[...] = y_ref[...]
    in_out_ref[...] = in_ref[...]
    norm_out_ref[...] = norm_ref[...]
    router_ref[...] = few_ref[:8]
    gain_ref[...] = few_ref[8:9]
    for i in range(3):
        part = f_ref[:, :, 64 * i : 64 * (i + 1)].reshape(1024, 128)
        qkv_ref[:, 1024 * i : 1024 * (i + 1)] = part.T.astype(F32)
    for i in range(4):
        for h in range(2):
            part = o_ref[i, :, 32 * h : 32 * (h + 1)].reshape(128, 128)
            out_ref[:, (2 * i + h) * 128 : (2 * i + h + 1) * 128] = part.astype(F32)
    gate_ref[...] = g_ref[0].astype(F32)
    up_ref[...] = g_ref[1].astype(F32)
    down_ref[...] = g_ref[2].astype(F32)


def unfold(full, blocks, few, block_output, input_grad, gain_grad):
    shape = jax.ShapeDtypeStruct
    share = pl.BlockSpec((None, FFB, 128), lambda i, j: (i, 0, j))
    return pl.pallas_call(
        unfold_kernel,
        out_shape=(
            shape((1024, 3072), F32),
            shape((1024, 1024), F32),
            *[shape((4, FFB, DB), F32)] * 3,
            shape((8, 1024), F32),
            shape((1, 1024), F32),
            shape((128, 1024), BF16),
            shape((128, 1024), F32),
            shape((1, 1024), F32),
        ),
        grid=(4, 2),
        in_specs=[
            pl.BlockSpec((None, None, 4, 4, 192, 128), lambda i, j: (j, i, 0, 0, 0, 0)),
            pl.BlockSpec((None, 4, None, 4, 64, 128), lambda i, j: (j, 0, i, 0, 3, 0)),
            pl.BlockSpec((None, 3, FFB, 128), lambda i, j: (i, 0, 0, j)),
            pl.BlockSpec((16, 1024), lambda i, j: (0, 0)),
            pl.BlockSpec((16, 1024), lambda i, j: (2 * i + j, 0)),
            pl.BlockSpec((16, 1024), lambda i, j: (2 * i + j, 0)),
            pl.BlockSpec((1, 1024), lambda i, j: (0, 0)),
        ],
        out_specs=(
            pl.BlockSpec((128, 3072), lambda i, j: (2 * i + j, 0)),
            pl.BlockSpec((128, 1024), lambda i, j: (4 * j + i, 0)),
            *[share] * 3,
            pl.BlockSpec((8, 1024), lambda i, j: (0, 0)),
            pl.BlockSpec((1, 1024), lambda i, j: (0, 0)),
            pl.BlockSpec((16, 1024), lambda i, j: (2 * i + j, 0)),
            pl.BlockSpec((16, 1024), lambda i, j: (2 * i + j, 0)),
            pl.BlockSpec((1, 1024), lambda i, j: (0, 0)),
        ),
        compiler_params=pltpu.CompilerParams(vmem_limit_bytes=62 * 1024 * 1024),
    )(full, full, blocks, few, block_output, input_grad, gain_grad)


def body(
    block_input,
    attn_gain,
    qkv_weight,
    out_weight,
    moe_gain,
    router_weight,
    gate_weight,
    up_weight,
    down_weight,
    routes,
    slot_index,
    cotangent,
):
    (
        send,
        pairs,
        middle,
        probs,
        ctx_tok,
        qkv,
        ctx_here,
        lse,
        down,
        near,
        weights,
        qkv_low,
        out_low,
    ) = attend(
        block_input,
        attn_gain,
        gate_weight,
        up_weight,
        down_weight,
        moe_gain,
        router_weight,
        routes,
        slot_index,
        cotangent,
        qkv_weight,
        out_weight,
    )
    block_output, input_grad, gain_grad, mine, few, full, _ = experts_back(
        middle,
        probs,
        pairs,
        cotangent,
        moe_gain.reshape(1, -1),
        router_weight.T,
        ctx_tok,
        qkv,
        ctx_here,
        lse,
        block_input,
        attn_gain.reshape(1, -1),
        down,
        send,
        weights,
        near,
        qkv_low,
        out_low,
    )
    (
        qkv_grad,
        out_grad,
        gate_grad,
        up_grad,
        down_grad,
        router_grad,
        moe_gain_grad,
        block_output,
        input_grad,
        gain_grad,
    ) = unfold(full, mine, few, block_output, input_grad, gain_grad)
    return (
        block_output,
        input_grad,
        gain_grad.reshape(-1),
        qkv_grad,
        out_grad,
        moe_gain_grad.reshape(-1),
        router_grad.T,
        jnp.swapaxes(gate_grad, 1, 2),
        jnp.swapaxes(up_grad, 1, 2),
        down_grad,
    )


def solution(mesh):
    tokens = P(("dp", "expert", "mp"), None)
    cols = P("expert", "dp", "mp")
    rows = P("expert", "mp", "dp")
    return jax.shard_map(
        body,
        mesh=mesh,
        in_specs=(tokens, P(), P(), P(), P(), P(), cols, cols, rows, tokens, tokens, tokens),
        out_specs=(tokens, tokens, P(), P(), P(), P(), P(), cols, cols, rows),
        check_vma=False,
    )
```

```python
import jax
import jax.numpy as jnp
from jax import lax
from jax.experimental import pallas as pl
from jax.experimental.pallas import tpu as pltpu
from jax.sharding import PartitionSpec as P

EPSILON = 1e-06
HIGHEST = lax.Precision.HIGHEST
MESH = pl.DeviceIdType.MESH
F32 = jnp.float32
BF16 = jnp.bfloat16
VMEM = pltpu.VMEM
ROWS = 40
FFB = 176
FFQ = 704
DB = 256
NT = (((1,), (1,)), ((), ()))
TN = (((0,), (0,)), ((), ()))


def dot(a, b):
    return jnp.dot(a, b, preferred_element_type=F32)


def dot_nt(a, b):
    return lax.dot_general(a, b, NT, preferred_element_type=F32)


def dot_tn(a, b):
    return lax.dot_general(a, b, TN, preferred_element_type=F32)


def spot():
    m = lax.axis_index("mp")
    return lax.axis_index("dp"), lax.axis_index("expert"), m, m // 4, m % 4


def params(cid, mb=60):
    return pltpu.CompilerParams(
        collective_id=cid, has_side_effects=True, vmem_limit_bytes=mb * 1024 * 1024
    )


def swapped(c, z):
    return z % 2, 2 * (z // 2) + c


def mp_at(m, k):
    return {"mp": (m + k) % 16}


def ahead(z, y, k):
    return ((z + k % 4 + k // 4) % 4) * 4 + (y + k % 4) % 4


def behind(z, y, k):
    return ((z + 8 - k % 4 - k // 4) % 4) * 4 + (y + 4 - k % 4) % 4


def y_at(z, y, d):
    return {"mp": z * 4 + (y + d) % 4}


def z_at(z, y, d):
    return {"mp": ((z + d) % 4) * 4 + y}


def push(src, dst, send, recv, device):
    return pltpu.make_async_remote_copy(
        src_ref=src, dst_ref=dst, send_sem=send, recv_sem=recv, device_id=device, device_id_type=MESH
    )


def tally(ref, send, recv):
    return push(ref, ref, send, recv, {"expert": 1 - lax.axis_index("expert")})


def lanes(at, size):
    return pl.ds(pl.multiple_of(at * size, size), size)


def greet_mp(barrier, m):
    def one(k, carry):
        pl.semaphore_signal(barrier, inc=1, device_id=mp_at(m, k), device_id_type=MESH)
        return carry

    lax.fori_loop(1, 16, one, 0)


def places(routes, slots):
    return jnp.where(slots < ROWS, routes * (2 * ROWS) + slots, -1.0)


def picks(columns):
    lane = lax.broadcasted_iota(jnp.int32, (128, 8), 1).astype(F32)
    return [(columns[:, j : j + 1] == lane).astype(F32) for j in range(2)]


def gates_of(probs, hot):
    chosen = [jnp.sum(probs * h, axis=1, keepdims=True) for h in hot]
    total = chosen[0] + chosen[1]
    return [v / total for v in chosen], total


def exact(a, b, dims):
    return lax.dot_general(a, b, dims, precision=HIGHEST, preferred_element_type=F32)


def unit(v):
    scale = lax.rsqrt(jnp.mean(v * v, axis=-1, keepdims=True) + EPSILON)
    return v * scale, scale


def attend_kernel(
    x_ref,
    gain_ref,
    gate_ref,
    up_ref,
    downs_ref,
    moe_gain_ref,
    router_ref,
    routes_ref,
    slots_ref,
    cot_ref,
    wq_hbm,
    wo_hbm,
    send_out,
    pairs_out,
    mid_out,
    probs_out,
    ctx_out_ref,
    qkv_out,
    ctx_here_out,
    lse_out,
    down_out,
    nall_ref,
    w_out_ref,
    wq_out_ref,
    wo_out_ref,
    send_ref,
    pairs_ref,
    mid_ref,
    probs_ref,
    ctx_ref,
    qkv_ref,
    ctx_here_ref,
    lse_ref,
    down_ref,
    wq_wide,
    wo_wide,
    wq_ref,
    wo_ref,
    normed,
    heads,
    blocks,
    stage,
    key_rows,
    ctx_low,
    here,
    s_send,
    s_recv,
    x_send,
    x_recv,
    a_send,
    a_recv,
    n_send,
    n_recv,
    c_send,
    c_recv,
):
    x, c, m, z, y = spot()
    pc, pz = swapped(c, z)
    away = (pc - c) * (pc - c)
    barrier = pltpu.get_barrier_semaphore()

    def remote(el):
        return (away == 1) | (el != y)

    def partner(el):
        return {"expert": pc, "mp": pz * 4 + el}

    greet_mp(barrier, m)
    pairs_ref[0:2] = routes_ref[...].astype(F32)
    pairs_ref[2:4] = slots_ref[...].astype(F32)
    pairs_ref[4:8] = jnp.zeros((4, 128), F32)
    for el in range(4):

        @pl.when(remote(el))
        def _():
            pl.semaphore_signal(barrier, inc=1, device_id=partner(el), device_id_type=MESH)

    for d in range(1, 4):
        pl.semaphore_signal(barrier, inc=1, device_id={"dp": (x + d) % 4}, device_id_type=MESH)

    wide = 512

    def load(i):
        cols = pl.ds(i * wide, wide)
        return pltpu.make_async_copy(wq_hbm.at[:, cols], wq_wide.at[:, cols], here.at[4 + i])

    def save(i):
        cols = pl.ds(i * wide, wide)
        return pltpu.make_async_copy(wq_ref.at[:, cols], wq_out_ref.at[:, cols], here.at[4 + i])

    load_o = pltpu.make_async_copy(wo_hbm, wo_wide, here.at[10])
    save_o = pltpu.make_async_copy(wo_ref, wo_out_ref, here.at[10])
    for i in range(6):
        load(i).start()
    load_o.start()
    for el in range(4):
        blocks[el, 0] = gate_ref[el].astype(BF16)
        blocks[el, 1] = up_ref[el].astype(BF16)
        blocks[el, 2] = downs_ref[el].astype(BF16)
    pl.semaphore_wait(barrier, 15 + 6 + away)

    def units(at):
        return stage.at[:, pl.ds(pl.multiple_of(at * FFB, 16), FFB), :]

    def block(i, el, at):
        return push(
            blocks.at[el, i],
            stage.at[i, pl.ds(pl.multiple_of(at * FFB, 16), FFB), :],
            s_send.at[i, el],
            s_recv.at[i, at],
            partner(el),
        )

    def each_block(f):
        for el in range(4):

            @pl.when(remote(el))
            def _(el=el):
                f(el)

    def blocks_out(i):
        each_block(lambda el: block(i, el, y).start())

    def blocks_in(i):
        each_block(lambda el: block(i, el, el).wait_recv())

    blocks_out(0)

    @pl.when(away == 0)
    def _():
        kept = pltpu.make_async_copy(blocks.at[y], units(y), here.at[2])
        kept.start()
        kept.wait()

    normed[...] = (unit(x_ref[...].astype(F32))[0] * gain_ref[...]).astype(BF16)
    half = 512

    def near(part, d):
        cols = pl.ds(part * half, half)
        device = y_at(z, y, d) if part == 0 else z_at(z, y, d)
        return lambda at: push(
            normed.at[:, cols],
            nall_ref.at[at // 4, at % 4, :, cols],
            n_send.at[part, 0, d],
            n_recv.at[part, 0, d],
            device,
        )

    y_from = [z * 4 + (y + 4 - d) % 4 for d in range(4)]
    z_from = [((z + 4 - d) % 4) * 4 + y for d in range(4)]

    def far(part, d, origin):
        cols = pl.ds(part * half, half)
        if part == 0:
            ref, device = nall_ref.at[origin // 4, :, :, cols], z_at(z, y, d)
        else:
            ref, device = nall_ref.at[:, origin % 4, :, cols], y_at(z, y, d)
        return push(ref, ref, n_send.at[part, 1, d], n_recv.at[part, 1, d], device)

    for i in range(6):
        load(i).wait()
        cols = slice(i * wide, (i + 1) * wide)
        wq_ref[:, cols] = wq_wide[:, cols].astype(BF16)
        save(i).start()
        part = dot(normed[...], wq_ref[:, cols])
        heads[i // 2, (i % 2) * 8 : (i % 2) * 8 + 8] = part.T.astype(BF16).reshape(8, 64, 128)

    def head_out(k):
        t = ahead(z, y, k)
        return push(
            heads.at[:, t],
            qkv_ref.at[:, :, lanes(m, 128)],
            a_send.at[0],
            a_recv.at[0],
            {"mp": t},
        )

    def each(lo, hi, f):
        def one(k, carry):
            f(k)
            return carry

        lax.fori_loop(lo, hi, one, 0)

    each(1, 16, lambda k: head_out(k).start())
    own = pltpu.make_async_copy(heads.at[:, m], qkv_ref.at[:, :, lanes(m, 128)], here.at[0])
    own.start()
    mine = pltpu.make_async_copy(normed, nall_ref.at[z, y], here.at[1])
    mine.start()
    blocks_out(1)
    blocks_out(2)
    for d in (2, 1, 3):
        near(0, d)(m).start()
        near(1, d)(m).start()


    def fan(i, d, step, at):
        rows = pl.ds(0, FFQ) if step == 0 else pl.ds(0 if d == 1 else FFQ // 2, FFQ // 2)
        cols = w_out_ref.at[i, rows, lanes(at, DB)]
        return push(
            stage.at[i] if step == 0 else cols,
            cols,
            x_send.at[i, step, d],
            x_recv.at[i, step, d],
            {"dp": (x + d) % 4},
        )

    def fan_wait(i, step):
        for d in (1, 3):
            fan(i, d, step, (x + 8 - d * (1 + step)) % 4).wait_recv()

    def fan_start(i, step):
        for d in (1, 3):
            fan(i, d, step, x if step == 0 else (x + 4 - d) % 4).start()

    def fan_own(i):
        return pltpu.make_async_copy(stage.at[i], w_out_ref.at[i, :, lanes(x, DB)], here.at[2 + i])

    blocks_in(0)
    fan_start(0, 0)
    fan_own(0).start()
    load_o.wait()
    wo_ref[...] = wo_wide[...].astype(BF16)
    save_o.start()

    own.wait()
    some = qkv_ref.at[:, :, pl.ds(0, 15 * 128)]
    tally(some, a_send.at[0], a_recv.at[0]).wait_recv()

    key_rows[...] = qkv_ref[1].astype(F32).T.astype(BF16)

    def ctx_out(t):
        return push(
            ctx_low.at[:, lanes(t, 128)],
            ctx_ref.at[pl.ds(pl.multiple_of(m * 64, 64), 64), :],
            c_send.at[0],
            c_recv.at[0],
            {"mp": t},
        )

    def queries(i):
        b = (m // 2 + i) % 8
        cols = lanes(b, 256)
        q = (qkv_ref[0, :, cols].astype(F32) * 0.125).astype(BF16)
        s = dot(key_rows[...], q)
        top = jnp.max(s, axis=0, keepdims=True)
        p = jnp.exp(s - top)
        total = jnp.sum(p, axis=0, keepdims=True)
        ctx = dot(qkv_ref[2], p.astype(BF16)) / total
        lse_ref[:, cols] = top + jnp.log(total)
        ctx_here_ref[:, cols] = ctx
        ctx_low[:, cols] = ctx.astype(BF16)

    def pair(i, carry):
        queries(2 * i)
        queries(2 * i + 1)
        for u in range(2):
            b = (m // 2 + 2 * i + u) % 8
            for v in range(2):
                t = 2 * b + v

                @pl.when(t != m)
                def _():
                    ctx_out(t).start()

        @pl.when(i == 0)
        def _():
            blocks_in(1)
            fan_start(1, 0)
            fan_own(1).start()

        @pl.when(i == 1)
        def _():
            fan_wait(0, 0)
            fan_start(0, 1)
            blocks_in(2)
            down_ref[...] = stage[2]

        return carry

    lax.fori_loop(0, 4, pair, 0)
    for d in (1, 2, 3):
        near(0, d)(y_from[d]).wait_recv()
        near(1, d)(z_from[d]).wait_recv()
    mine.wait()
    for d in (1, 3):
        far(0, d, m).start()
        far(1, d, m).start()
    ctx_ref[pl.ds(pl.multiple_of(m * 64, 64), 64), :] = ctx_low[:, lanes(m, 128)]
    lot = ctx_ref.at[pl.ds(0, 15 * 64)]
    tally(lot, c_send.at[0], c_recv.at[0]).wait_recv()

    fan_wait(1, 0)
    fan_start(1, 1)

    mid = x_ref[...].astype(F32) + dot_tn(ctx_ref[...], wo_ref[...])
    mid_ref[...] = mid
    moe_in = unit(mid)[0] * moe_gain_ref[...]
    logits = exact(moe_in, router_ref[...], NT)
    grown = jnp.exp(logits - jnp.max(logits, axis=1, keepdims=True))
    probs = grown / jnp.sum(grown, axis=1, keepdims=True)
    probs_ref[...] = probs
    gates, _ = gates_of(probs, picks(pairs_ref[...].T))
    upstream = cot_ref[...].astype(F32)
    rows = [moe_in.astype(BF16)] + [(g * upstream).astype(BF16) for g in gates]
    row = lax.broadcasted_iota(jnp.int32, (16 * ROWS, 128), 0).astype(F32)
    at = [places(pairs_ref[j : j + 1], pairs_ref[2 + j : 3 + j]) for j in range(2)]
    hot = [((row == at[0]) | (row == at[1]))] + [row == jnp.where(a < 0, a, a + ROWS) for a in at]
    hot = jnp.concatenate([h.astype(F32) for h in hot], axis=1).astype(BF16)
    sent = dot(hot, jnp.concatenate(rows, axis=0))
    send_ref[...] = sent.astype(BF16).reshape(8, 2 * ROWS, 1024)
    results = (
        (send_ref, send_out),
        (pairs_ref, pairs_out),
        (mid_ref, mid_out),
        (probs_ref, probs_out),
        (ctx_ref, ctx_out_ref),
        (qkv_ref, qkv_out),
        (ctx_here_ref, ctx_here_out),
        (lse_ref, lse_out),
        (down_ref, down_out),
    )
    results = [
        pltpu.make_async_copy(src, dst, here.at[11 + i]) for i, (src, dst) in enumerate(results)
    ]
    for copy in results:
        copy.start()

    for i in range(6):
        save(i).wait()
    save_o.wait()
    fan_wait(0, 1)
    fan_wait(1, 1)
    for d in (1, 3):
        far(0, d, z_from[d]).wait_recv()
        far(1, d, y_from[d]).wait_recv()
    for d in (1, 2, 3):
        near(0, d)(m).wait_send()
        near(1, d)(m).wait_send()
    for d in (1, 3):
        far(0, d, m).wait_send()
        far(1, d, m).wait_send()
    for i in range(2):
        fan_own(i).wait()
        for d in (1, 3):
            for step in range(2):
                fan(i, d, step, x).wait_send()
    tally(some, a_send.at[0], a_recv.at[0]).wait_send()
    tally(lot, c_send.at[0], c_recv.at[0]).wait_send()
    for i in range(3):
        each_block(lambda el, i=i: block(i, el, y).wait_send())
    for copy in results:
        copy.wait()


def attend(
    block_input,
    gain,
    gate_weight,
    up_weight,
    down_weight,
    moe_gain,
    router,
    routes,
    slots,
    cotangent,
    qkv_weight,
    out_weight,
):
    dma = pltpu.SemaphoreType.DMA
    vm = pl.BlockSpec(memory_space=VMEM)
    hbm = pl.BlockSpec(memory_space=pl.ANY)
    shape = jax.ShapeDtypeStruct
    return pl.pallas_call(
        attend_kernel,
        out_shape=(
            shape((8, 2 * ROWS, 1024), BF16),
            shape((8, 128), F32),
            shape((128, 1024), F32),
            shape((128, 8), F32),
            shape((1024, 128), BF16),
            shape((3, 64, 2048), BF16),
            shape((64, 2048), F32),
            shape((1, 2048), F32),
            shape((FFQ, DB), BF16),
            shape((4, 4, 128, 1024), BF16),
            shape((2, FFQ, 4 * DB), BF16),
            shape((1024, 3072), BF16),
            shape((1024, 1024), BF16),
        ),
        in_specs=[vm] * 10 + [hbm] * 2,
        out_specs=(hbm,) * 13,
        scratch_shapes=[
            VMEM((8, 2 * ROWS, 1024), BF16),
            VMEM((8, 128), F32),
            VMEM((128, 1024), F32),
            VMEM((128, 8), F32),
            VMEM((1024, 128), BF16),
            VMEM((3, 64, 2048), BF16),
            VMEM((64, 2048), F32),
            VMEM((1, 2048), F32),
            VMEM((FFQ, DB), BF16),
            VMEM((1024, 3072), F32),
            VMEM((1024, 1024), F32),
            VMEM((1024, 3072), BF16),
            VMEM((1024, 1024), BF16),
            VMEM((128, 1024), BF16),
            VMEM((3, 16, 64, 128), BF16),
            VMEM((4, 3, FFB, DB), BF16),
            VMEM((3, FFQ, DB), BF16),
            VMEM((2048, 64), BF16),
            VMEM((64, 2048), BF16),
            dma((20,)),
            dma((3, 4)),
            dma((3, 4)),
            dma((2, 2, 4)),
            dma((2, 2, 4)),
            dma((1,)),
            dma((1,)),
            dma((2, 2, 4)),
            dma((2, 2, 4)),
            dma((1,)),
            dma((1,)),
        ],
        compiler_params=params(1, 62),
    )(
        block_input,
        gain.reshape(1, -1),
        jnp.swapaxes(gate_weight, 1, 2),
        jnp.swapaxes(up_weight, 1, 2),
        down_weight,
        moe_gain.reshape(1, -1),
        router.T,
        routes.T,
        slots.T,
        cotangent,
        qkv_weight,
        out_weight,
    )


GELU_A = 0.7978845608
GELU_B = 0.044715


def experts_back_kernel(
    mid_hbm,
    probs_hbm,
    pairs_hbm,
    cot_hbm,
    moe_gain_hbm,
    router_hbm,
    tok_hbm,
    qkv_hbm,
    ctx_hbm,
    lse_hbm,
    x_hbm,
    gain_hbm,
    down_hbm,
    send_hbm,
    w_hbm,
    near_hbm,
    wq_hbm,
    wo_hbm,
    y_ref,
    in_ref,
    gain_out_ref,
    g_out_ref,
    few_out_ref,
    full_out,
    ret_ref,
    mid_ref,
    probs_ref,
    pairs_ref,
    cot_ref,
    moe_gain_ref,
    router_ref,
    tok_ref,
    qkv_ref,
    ctx_ref,
    lse_ref,
    x_ref,
    gain_ref,
    down_ref,
    full_ref,
    nall_ref,
    weights,
    recv,
    rows,
    back,
    sib_recv,
    sib_send,
    own_part,
    hid,
    gcs,
    ucs,
    g_relay,
    g_near,
    dctx,
    few,
    o_sib,
    o_x,
    o_q,
    o_mp,
    few_mp,
    few_sum,
    few_done,
    few_rest,
    cot,
    key_values,
    row_dot,
    dkv,
    pc_here,
    pc_tok,
    slices,
    share,
    parts,
    gain_row,
    gain_mp,
    gain_rest,
    here,
    leave,
    d_send,
    d_recv,
    f_send,
    f_recv,
    p_send,
    p_recv,
    r_send,
    r_recv,
    w_send,
    w_recv,
    x_send,
    x_recv,
    s_send,
    s_recv,
    n_send,
    n_recv,
    a_send,
    a_recv,
    b_send,
    b_recv,
    q_send,
    q_recv,
    g_send,
    g_recv,
    t_send,
    t_recv,
    u_send,
    u_recv,
    v_send,
    v_recv,
    o_send,
    o_recv,
    ox_send,
    ox_recv,
    om_send,
    om_recv,
    fm_send,
    fm_recv,
    fr_send,
    fr_recv,
):
    x, c, m, z, y = spot()
    pc, pz = swapped(c, z)
    away = (pc - c) * (pc - c)
    barrier = pltpu.get_barrier_semaphore()

    def remote(el):
        return (away == 1) | (el != y)

    def partner(el):
        return {"expert": pc, "mp": pz * 4 + el}

    def rest(r):
        return {"dp": (x + r % 4) % 4, "expert": (c + r // 4) % 2}

    def each(lo, hi, f):
        def one(k, carry):
            f(k)
            return carry

        lax.fori_loop(lo, hi, one, 0)

    def local(src, dst, i):
        return pltpu.make_async_copy(src, dst, here.at[i])

    twin = {"expert": 1 - c}
    size = 2 * ROWS

    greet_mp(barrier, m)
    for el in range(4):

        @pl.when(remote(el))
        def _():
            pl.semaphore_signal(barrier, inc=1, device_id=partner(el), device_id_type=MESH)

    for r in range(1, 8):
        pl.semaphore_signal(barrier, inc=1, device_id=rest(r), device_id_type=MESH)
    operands = [
        local(src, dst, 14 + i)
        for i, (src, dst) in enumerate(
            (
                (down_hbm, down_ref),
                (mid_hbm, mid_ref),
                (probs_hbm, probs_ref),
                (pairs_hbm, pairs_ref),
                (cot_hbm, cot_ref),
                (moe_gain_hbm, moe_gain_ref),
                (router_hbm, router_ref),
                (tok_hbm, tok_ref),
                (qkv_hbm, qkv_ref),
                (ctx_hbm, ctx_ref),
                (lse_hbm, lse_ref),
                (x_hbm, x_ref),
                (gain_hbm, gain_ref),
            )
        )
    ]
    for copy in operands:
        copy.start()
    load_w = [local(w_hbm.at[i], weights.at[pl.ds(i * FFQ, FFQ)], i) for i in range(2)]
    for copy in load_w:
        copy.start()
    near = []
    for i, d in enumerate((0, 1, 3)):
        at = (z + d) % 4, slice(None), slice(None), pl.ds(0, 512)
        near.append(local(near_hbm.at[at], nall_ref.at[at], 8 + i))
        at = slice(None), (y + d) % 4, slice(None), pl.ds(512, 512)
        near.append(local(near_hbm.at[at], nall_ref.at[at], 11 + i))
    for copy in near:
        copy.start()
    pl.semaphore_wait(barrier, 15 + 3 + away + 7)

    def expert_of(t):
        return ((t // 4) % 2) * 4 + t % 4

    def slot(core, k, n=1):
        return pl.ds(pl.multiple_of((core * 16 + k) * size, size), n * size)

    def dispatch(k):
        t = ahead(z, y, k)
        return push(
            send_hbm.at[expert_of(t)],
            recv.at[slot(0, k)],
            d_send.at[0],
            d_recv.at[k],
            {"mp": t},
        )

    def forward(k):
        return push(
            recv.at[slot(0, k)], recv.at[slot(1, k)], f_send.at[0], f_recv.at[k // 4], twin
        )

    def partials(j):
        return push(
            sib_send.at[j % 2],
            sib_recv.at[pl.ds(pl.multiple_of(j * 4 * size, size), 4 * size)],
            p_send.at[j],
            p_recv.at[j],
            twin,
        )

    def spot_of(k, n=1):
        return pl.ds(pl.multiple_of(k * size, size), n * size)

    def giving(k, at):
        return push(
            back.at[spot_of(k)], ret_ref.at[at], r_send.at[0], r_recv.at[0], {"mp": behind(z, y, k)}
        )

    def down_fan(d, step, at):
        part = pl.ds(0, FFQ) if step == 0 else pl.ds(0 if d == 1 else FFQ // 2, FFQ // 2)
        units = pl.ds(2 * FFQ + part.start, part.size)
        there = weights.at[units, lanes(at, DB)]
        return push(
            down_ref if step == 0 else there,
            there,
            w_send.at[step, d // 2],
            w_recv.at[step, d // 2],
            {"dp": (x + d) % 4},
        )

    each(1, 16, lambda k: dispatch(k).start())
    operands[0].wait()
    for d in (1, 3):
        down_fan(d, 0, x).start()
    own = local(send_hbm.at[expert_of(m)], recv.at[slot(0, 0)], 4)
    own.start()
    weights[2 * FFQ :, lanes(x, DB)] = down_ref[...]

    def finish(j):
        partials(j).wait_recv()
        span = spot_of(4 * j, 4)
        back[span] = (own_part[...] + sib_recv[span].astype(F32)).astype(BF16)
        for i in range(4):
            k = 4 * j + i

            @pl.when(k > 0)
            def _():
                giving(k, m).start()

            @pl.when(k == 0)
            def _():
                local(back.at[spot_of(0)], ret_ref.at[m], 4).start()

    gate_w, up_w, down_w = (slice(i * FFQ, (i + 1) * FFQ) for i in range(3))
    cot_rows = 32 * ROWS

    def chunk(j, carry):
        for i in range(4):
            k = 4 * j + i

            @pl.when(k > 0)
            def _():
                dispatch(k).wait_recv()

            @pl.when(k == 0)
            def _():
                own.wait()

            forward(k).start()

        @pl.when(j > 0)
        def _():
            finish(j - 1)

        @pl.when(j == 0)
        def _():
            for copy in load_w:
                copy.wait()
            for d in (1, 3):
                down_fan(d, 1, (x + 2) % 4).wait_recv()

        tally(recv.at[slot(1, 4 * j, 4)], f_send.at[0], f_recv.at[j]).wait_recv()
        xs = pl.ds(pl.multiple_of(j * 8 * ROWS, 16), 8 * ROWS)
        cs = pl.ds(pl.multiple_of(cot_rows + j * 8 * ROWS, 16), 8 * ROWS)
        for r in range(2):
            blk = recv[slot(r, 4 * j, 4)].astype(F32).reshape(4, size, 4 * DB)
            for at, part in ((0, blk[:, :ROWS]), (cot_rows, blk[:, ROWS:])):
                span = pl.ds(pl.multiple_of(at + (2 * j + r) * 4 * ROWS, 16), 4 * ROWS)
                rows[span] = part.reshape(4 * ROWS, 4 * DB).astype(BF16)
        gate = dot_nt(rows[xs], weights[gate_w])
        up = dot_nt(rows[xs], weights[up_w])
        hid_cot = dot_nt(rows[cs], weights[down_w])
        sq = gate * gate
        th = jnp.tanh(GELU_A * (gate + GELU_B * (gate * sq)))
        half = 0.5 * (1.0 + th)
        act = gate * half
        slope = half + 0.5 * gate * (1.0 - th * th) * (GELU_A * (1.0 + 3.0 * GELU_B * sq))
        hid[xs] = (act * up).astype(BF16)
        gcs[xs] = (hid_cot * up * slope).astype(BF16)
        ucs[xs] = (hid_cot * act).astype(BF16)
        out = dot(hid[xs], weights[down_w]).reshape(2, 4, ROWS, 4 * DB)
        low = dot(gcs[xs], weights[gate_w]) + dot(ucs[xs], weights[up_w])
        low = low.reshape(2, 4, ROWS, 4 * DB)
        own_part[...] = jnp.concatenate([out[0], low[0]], axis=1).reshape(4 * size, 4 * DB)

        @pl.when(j > 1)
        def _():
            partials(j - 2).wait_send()

        sib_send[j % 2] = (
            jnp.concatenate([out[1], low[1]], axis=1).reshape(4 * size, 4 * DB).astype(BF16)
        )
        partials(j).start()
        return carry

    for d in (1, 3):
        down_fan(d, 0, (x + 4 - d) % 4).wait_recv()
        down_fan(d, 1, (x + 4 - d) % 4).start()
    lax.fori_loop(0, 4, chunk, 0)
    finish(3)
    tally(recv.at[slot(0, 0, 16)], f_send.at[0], f_recv.at[0]).wait_send()
    for d in (1, 3):
        down_fan(d, 0, x).wait_send()
        down_fan(d, 1, x).wait_send()
    load_o = local(wo_hbm, weights.at[pl.ds(0, 1024)], 0)
    load_o.start()

    unit_half = FFQ // 2

    def unit_rows(i, d):
        return pl.ds(i * FFQ + (0 if d == 1 else unit_half), unit_half)

    def relay(i, d):
        return push(
            recv.at[unit_rows(i, d), lanes((x + 2) % 4, DB)],
            g_relay.at[d // 2, i],
            x_send.at[0, i, d // 2],
            x_recv.at[0, i, d // 2],
            {"dp": (x + d) % 4},
        )

    def settle(i, d):
        return push(
            recv.at[pl.ds(i * FFQ, FFQ), lanes((x + d) % 4, DB)],
            g_near.at[d // 2, i],
            x_send.at[1, i, d // 2],
            x_recv.at[1, i, d // 2],
            {"dp": (x + d) % 4},
        )

    for i, (a, at) in enumerate(((gcs, 0), (ucs, 0), (hid, cot_rows))):
        g = dot_tn(a[...], rows[at : at + cot_rows])
        recv[i * FFQ : (i + 1) * FFQ] = g.astype(BF16)
        for d in (1, 3):
            relay(i, d).start()
    load_q = [
        local(wq_hbm.at[:, pl.ds(i * 1024, 1024)], rows.at[pl.ds(i * 1024, 1024)], 5 + i)
        for i in range(3)
    ]
    for copy in load_q:
        copy.start()
    for i in range(3):
        for d in (1, 3):
            relay(i, d).wait_recv()
            span, cols = unit_rows(i, d), lanes((x + d) % 4, DB)
            recv[span, cols] = (
                recv[span, cols].astype(F32) + g_relay[d // 2, i].astype(F32)
            ).astype(BF16)
            settle(i, d).start()

    def home(i, at, to):
        return push(
            recv.at[pl.ds(i * FFQ + at * FFB, FFB), lanes(x, DB)],
            g_out_ref.at[to, i],
            s_send.at[i, at],
            s_recv.at[i, to],
            partner(at),
        )

    def each_home(f):
        for at in range(4):

            @pl.when(remote(at))
            def _(at=at):
                f(at)

    def go_home(i):
        for d in (1, 3):
            settle(i, d).wait_recv()
        span, cols = pl.ds(i * FFQ, FFQ), lanes(x, DB)
        recv[span, cols] = (
            recv[span, cols].astype(F32) + g_near[0, i].astype(F32) + g_near[1, i].astype(F32)
        ).astype(BF16)
        each_home(lambda at: home(i, at, y).start())

        @pl.when(away == 0)
        def _():
            kept = local(
                recv.at[pl.ds(pl.multiple_of(i * FFQ + y * FFB, 16), FFB), cols], g_out_ref.at[y, i], 1
            )
            kept.start()
            kept.wait()

    local(back.at[spot_of(0)], ret_ref.at[m], 4).wait()
    tally(back.at[spot_of(1, 15)], r_send.at[0], r_recv.at[0]).wait_send()
    tally(ret_ref.at[pl.ds(0, 15)], r_send.at[0], r_recv.at[0]).wait_recv()
    load_r = local(ret_ref, back.reshape(16, size, 4 * DB), 4)
    load_r.start()
    load_r.wait()

    for copy in (*near, *operands[1:]):
        copy.wait()

    def far(part, d, hops):
        cols, some = pl.ds(part * 512, 512), pl.ds(0 if d == 1 else 2, 2)
        if part == 0:
            ref, device = nall_ref.at[(z + 8 - hops * d) % 4, some, :, cols], z_at(z, y, d)
        else:
            ref, device = nall_ref.at[some, (y + 8 - hops * d) % 4, :, cols], y_at(z, y, d)
        return push(ref, ref, n_send.at[part, d // 2], n_recv.at[part, d // 2], device)

    columns = pairs_ref[...].T
    hot = picks(columns)
    probs = probs_ref[...]
    gates, total = gates_of(probs, hot)
    at = places(columns[:, 0:2], columns[:, 2:4])
    lane = lax.broadcasted_iota(jnp.int32, (128, 16 * ROWS), 1).astype(F32)
    at = [at[:, j : j + 1] for j in range(2)]
    given = (back[: 8 * size].astype(F32) + back[8 * size :].astype(F32)).astype(BF16)
    fetched = [dot((lane == a).astype(F32).astype(BF16), given) for a in at]
    low = [lane == jnp.where(a < 0, a, a + ROWS) for a in at]
    moe_cot = dot((low[0] | low[1]).astype(F32).astype(BF16), given)
    mid = mid_ref[...]
    upstream = cot_ref[...].astype(F32)
    y_ref[...] = (mid + gates[0] * fetched[0] + gates[1] * fetched[1]).astype(BF16)
    gate_cot = [jnp.sum(upstream * f, axis=1, keepdims=True) for f in fetched]
    inner = gate_cot[0] * gates[0] + gate_cot[1] * gates[1]
    probs_cot = sum(h * ((g - inner) / total) for h, g in zip(hot, gate_cot))
    logit_cot = probs * (probs_cot - jnp.sum(probs * probs_cot, axis=1, keepdims=True))
    hat, scale = unit(mid)
    moe_cot += exact(logit_cot, router_ref[...], (((1,), (0,)), ((), ())))
    few[:8] = exact(logit_cot, hat * moe_gain_ref[...], TN)
    few[8:] = jnp.concatenate(
        [jnp.sum(moe_cot * hat, axis=0, keepdims=True), jnp.zeros((7, 1024), F32)], axis=0
    )
    gained = moe_cot * moe_gain_ref[...]
    in_ref[...] = upstream + scale * (gained - hat * jnp.mean(gained * hat, axis=-1, keepdims=True))
    branch_cot = in_ref[...].astype(BF16)
    load_o.wait()
    dctx[...] = dot_nt(weights[:1024], branch_cot).astype(BF16).reshape(16, 64, 128)

    def cot_out(k):
        t = ahead(z, y, k)
        return push(dctx.at[t], cot.at[:, lanes(m, 128)], a_send.at[0], a_recv.at[0], {"mp": t})

    each(1, 16, lambda k: cot_out(k).start())
    for d in (1, 3):
        far(0, d, 1).start()
        far(1, d, 1).start()
    cot[:, lanes(m, 128)] = dctx[m]

    weights[1024:2048] = dot(tok_ref[...], branch_cot).astype(BF16)

    def halves():
        rows_at = pl.ds(pl.multiple_of(1024 + (1 - c) * 512, 512), 512)
        return push(weights.at[rows_at], o_sib, o_send.at[0], o_recv.at[0], twin)

    def quarters(d):
        t = (x + d) % 4
        return push(
            weights.at[pl.ds(0, 512), lanes(t, DB)], o_x.at[d - 1], ox_send.at[0], ox_recv.at[0], {"dp": t}
        )

    def thirty(k):
        t = ahead(z, y, k)
        return push(
            o_q.at[pl.ds(pl.multiple_of(t * 32, 32), 32)],
            o_mp.at[k],
            om_send.at[0],
            om_recv.at[0],
            {"mp": t},
        )

    def few_share(r):
        t = 2 * ((x + r % 4) % 4) + (c + r // 4) % 2
        return push(
            few.at[:, lanes(t, 128)], few_rest.at[r], fr_send.at[0], fr_recv.at[0], rest(r)
        )

    def few_near(k):
        return push(few_sum, few_mp.at[k], fm_send.at[0], fm_recv.at[0], mp_at(m, k))

    def few_back(r, back_from):
        t = 2 * ((x + 4 - r % 4) % 4) + (c + r // 4) % 2 if back_from else 2 * x + c
        return push(
            few_done, few_out_ref.at[:, lanes(t, 128)], fr_send.at[1], fr_recv.at[1], rest(r)
        )

    halves().start()
    for r in range(1, 8):
        few_share(r).start()

    def along(axis, d):
        if axis == 0:
            return {"dp": (x + d) % 4}
        return z_at(z, y, d) if axis == 1 else y_at(z, y, d)

    orders = ((0, 2, 1), (0, 1, 2), (2, 1, 0), (0, 2, 1), (2, 1, 0))
    spans = [pl.ds(0, 64), pl.ds(64, 64), pl.ds(128, 64), pl.ds(192, 32), pl.ds(224, 32)]

    def spread(p, s, d, incoming):
        at = [x, z, y]
        axis = orders[p][s]
        if incoming:
            at[axis] = (at[axis] + 4 - d) % 4
        src = [x, z, y]
        for done in orders[p][:s]:
            at[done] = slice(None)
            src[done] = slice(None)
        return push(
            full_ref.at[(c, *src, spans[p])],
            full_ref.at[(c, *at, spans[p])],
            g_send.at[p, s],
            g_recv.at[p, s],
            along(axis, d),
        )

    def spread_start(p, s):
        for d in (2, 1, 3):
            spread(p, s, d, False).start()

    def last(p, d, hops):
        at = [slice(None)] * 3
        axis = orders[p][2]
        at[axis] = ((x, z, y)[axis] + 8 - hops * d) % 4
        return at

    def circle(p, d, step, incoming):
        at = last(p, d, step + incoming)
        if step:
            at[orders[p][0]] = pl.ds(0 if d == 1 else 2, 2)
        ref = full_ref.at[(c, *at, spans[p])]
        return push(ref, ref, g_send.at[p, 2 + step], g_recv.at[p, 2 + 2 * step + d // 2], along(orders[p][2], d))

    def blocks_of(p, s):
        at = ((0, 0, pl.ds(0, 3)), (0, pl.ds(0, 3), slice(None)), (pl.ds(0, 2),), (pl.ds(0, 1),))[s]
        at = (*at, *[slice(None)] * (3 - len(at)))
        return full_ref.at[(c, *at, spans[p])]

    def spread_wait(p, s):
        tally(blocks_of(p, s), g_send.at[p, s], g_recv.at[p, s]).wait_recv()

    def piece(p, i, core):
        d, hops = ((1, 0), (1, 1), (3, 1), (1, 2), (3, 2))[i]
        at = last(p, d, hops)
        if hops == 2:
            at[orders[p][0]] = pl.ds(0 if d == 1 else 2, 2)
        return (core, *at, spans[p])

    def share_twin(p, i, core):
        ref = full_ref.at[piece(p, i, core)]
        return push(ref, ref, t_send.at[0], t_recv.at[p, i], twin)

    def write(p, i, other):
        at = piece(p, i, 1 - c if other else c)
        return pltpu.make_async_copy(full_ref.at[at], full_out.at[at], leave.at[other])

    def hand_on(p, i):
        share_twin(p, i, c).start()
        write(p, i, 0).start()

    key_values[...] = qkv_ref[1:].reshape(128, 2048).astype(F32).T.astype(BF16)
    dkv[...] = jnp.zeros_like(dkv)
    halves().wait_recv()
    weights[:512] = (
        weights[pl.ds(pl.multiple_of(1024 + c * 512, 512), 512)].astype(F32) + o_sib[...].astype(F32)
    ).astype(BF16)
    for d in (2, 1, 3):
        quarters(d).start()
    go_home(0)
    cots = cot.at[:, pl.ds(0, 15 * 128)]
    tally(cots, a_send.at[0], a_recv.at[0]).wait_recv()
    row_dot[...] = jnp.sum(cot[...].astype(F32) * ctx_ref[...], axis=0, keepdims=True)

    def queries(b):
        cols = lanes(b, 256)
        q = (qkv_ref[0, :, cols].astype(F32) * 0.125).astype(BF16)
        none = jnp.zeros((64, 256), BF16)
        q = jnp.concatenate([q, none], axis=0)
        g = jnp.concatenate([none, cot[:, cols]], axis=0)
        p = jnp.exp(dot(key_values[...], q) - lse_ref[:, cols])
        dp = dot(key_values[...], g)
        ds = (p * (dp - row_dot[:, cols])).astype(BF16)
        pc_here[0, :, cols] = (dot(qkv_ref[1], ds) * 0.125).astype(BF16)
        dkv[...] += dot_nt(ds, q) + dot_nt(p.astype(BF16), g)

    def pair(i, carry):
        queries(2 * i)
        queries(2 * i + 1)

        @pl.when(i == 1)
        def _():
            go_home(1)

        @pl.when(i == 2)
        def _():
            few_all = few[:, lanes(2 * x + c, 128)]
            tally(few_rest.at[pl.ds(1, 7)], fr_send.at[0], fr_recv.at[0]).wait_recv()
            for r in range(1, 8):
                few_all += few_rest[r]
            few_sum[...] = few_all
            each(1, 16, lambda k: few_near(k).start())
            go_home(2)

        return carry

    lax.fori_loop(0, 4, pair, 0)
    pc_here[1:] = dkv[...].T.astype(BF16).reshape(2, 64, 2048)

    def pc_out(k):
        t = ahead(z, y, k)
        return push(
            pc_here.at[:, :, lanes(t, 128)], pc_tok.at[:, m], b_send.at[0], b_recv.at[0], {"mp": t}
        )

    for d in (1, 3):
        far(0, d, 2).wait_recv()
        far(1, d, 2).wait_recv()
    long = pc_here[...].reshape(192, 2048)
    slices[...] = dot(long, nall_ref[...].reshape(2048, 1024)).astype(BF16)

    def share_out(r):
        t = 2 * ((x + r % 4) % 4) + (c + r // 4) % 2
        return push(slices.at[:, lanes(t, 128)], parts.at[r], q_send.at[0], q_recv.at[0], rest(r))

    for r in range(1, 8):
        share_out(r).start()
    each(1, 16, lambda k: pc_out(k).start())
    pc_tok[:, m] = pc_here[:, :, lanes(m, 128)]

    tally(o_x, ox_send.at[0], ox_recv.at[0]).wait_recv()
    o_sum = weights[:512, lanes(x, DB)].astype(F32)
    for d in (1, 2, 3):
        o_sum += o_x[d - 1].astype(F32)
    o_q[...] = o_sum.astype(BF16)
    each(1, 16, lambda k: thirty(k).start())
    whole = slices[:, lanes(2 * x + c, 128)].astype(F32)
    seven = parts.at[pl.ds(1, 7)]
    tally(seven, q_send.at[0], q_recv.at[0]).wait_recv()
    for r in range(1, 8):
        whole += parts[r].astype(F32)
    share[:192] = whole.astype(BF16)
    lay = local(share.at[pl.ds(0, 192)], full_ref.at[c, x, z, y, pl.ds(0, 192)], 2)
    lay.start()
    lay.wait()
    for p in range(3):
        spread_start(p, 0)
    def circles(p):
        spread_wait(p, 1)
        for d in (1, 3):
            circle(p, d, 0, 0).start()
        hand_on(p, 0)

    for p in range(2):
        spread_wait(p, 0)
        spread_start(p, 1)
    fifteen = o_mp.at[pl.ds(1, 15)]
    tally(fifteen, om_send.at[0], om_recv.at[0]).wait_recv()
    o_sum = o_q[pl.ds(pl.multiple_of(m * 32, 32), 32)].astype(F32)
    for k in range(1, 16):
        o_sum += o_mp[k].astype(F32)
    o_low = o_sum.astype(BF16)
    share[192:224] = o_low[:, :128]
    share[224:] = o_low[:, 128:]
    lay = local(share.at[pl.ds(192, 64)], full_ref.at[c, x, z, y, pl.ds(192, 64)], 2)
    lay.start()
    lay.wait()
    for p in (3, 4):
        spread_start(p, 0)

    spread_wait(2, 0)
    spread_start(2, 1)
    for p in range(3):
        circles(p)
    for p in (3, 4):
        spread_wait(p, 0)
        spread_start(p, 1)

    packs = pc_here.at[:, :, pl.ds(0, 15 * 128)]
    tally(packs, b_send.at[0], b_recv.at[0]).wait_recv()
    for copy in load_q:
        copy.wait()
    dn = sum(dot(rows[i * 1024 : (i + 1) * 1024], pc_tok[i].reshape(1024, 128)) for i in range(3)).T
    hat, scale = unit(x_ref[...].astype(F32))
    gained = dn * gain_ref[...]
    in_ref[...] = in_ref[...] + scale * (
        gained - hat * jnp.mean(gained * hat, axis=-1, keepdims=True)
    )
    gain_row[...] = jnp.sum(dn * hat, axis=0, keepdims=True)

    def gain_out(k):
        return push(gain_row, gain_mp.at[k], u_send.at[0], u_recv.at[0], mp_at(m, k))

    def gain_far(r):
        return push(gain_mp.at[0], gain_rest.at[r], v_send.at[0], v_recv.at[0], rest(r))

    each(1, 16, lambda k: gain_out(k).start())
    for p in (3, 4):
        circles(p)

    def onward(p):
        for i, d in ((1, 1), (2, 3)):
            circle(p, d, 0, 1).wait_recv()
            circle(p, d, 1, 0).start()
            hand_on(p, i)

    for p in range(3):
        onward(p)
    gains = gain_mp.at[pl.ds(1, 15)]
    tally(gains, u_send.at[0], u_recv.at[0]).wait_recv()
    got = gain_row[...]
    for k in range(1, 16):
        got += gain_mp[k]
    gain_mp[0] = got
    for r in range(1, 8):
        gain_far(r).start()
    for p in (3, 4):
        onward(p)
    fews = few_mp.at[pl.ds(1, 15)]
    tally(fews, fm_send.at[0], fm_recv.at[0]).wait_recv()
    few_all = few_sum[...]
    for k in range(1, 16):
        few_all += few_mp[k]
    few_done[...] = few_all
    few_out_ref[:, lanes(2 * x + c, 128)] = few_all
    for r in range(1, 8):
        few_back(r, False).start()
    for p in range(5):
        for i, d in ((3, 1), (4, 3)):
            circle(p, d, 1, 1).wait_recv()
            hand_on(p, i)
    rests = gain_rest.at[pl.ds(1, 7)]
    tally(rests, v_send.at[0], v_recv.at[0]).wait_recv()
    for r in range(1, 8):
        got += gain_rest[r]
    gain_out_ref[...] = got
    for i in range(3):
        each_home(lambda at, i=i: home(i, at, at).wait_recv())
    few_seven = few_rest.at[pl.ds(1, 7)]
    tally(few_seven, fr_send.at[1], fr_recv.at[1]).wait_recv()
    for p in range(5):
        for i in range(5):
            share_twin(p, i, 1 - c).wait_recv()
            write(p, i, 1).start()

    tally(full_ref.at[c], t_send.at[0], t_recv.at[0, 0]).wait_send()
    for i in range(2):
        pltpu.make_async_copy(full_ref.at[i], full_out.at[i], leave.at[i]).wait()
    for p in range(5):
        for s in range(4):
            tally(blocks_of(p, s), g_send.at[p, s], g_recv.at[p, s]).wait_send()
    tally(recv.at[pl.ds(0, 15 * size)], d_send.at[0], d_recv.at[0]).wait_send()
    tally(cots, a_send.at[0], a_recv.at[0]).wait_send()
    tally(packs, b_send.at[0], b_recv.at[0]).wait_send()
    tally(gains, u_send.at[0], u_recv.at[0]).wait_send()
    tally(fifteen, om_send.at[0], om_recv.at[0]).wait_send()
    tally(fews, fm_send.at[0], fm_recv.at[0]).wait_send()
    for j in (2, 3):
        partials(j).wait_send()
    halves().wait_send()
    tally(o_x, ox_send.at[0], ox_recv.at[0]).wait_send()
    for d in (1, 3):
        for i in range(3):
            relay(i, d).wait_send()
            settle(i, d).wait_send()
        far(0, d, 1).wait_send()
        far(1, d, 1).wait_send()
    tally(few_seven, fr_send.at[0], fr_recv.at[0]).wait_send()
    tally(few_seven, fr_send.at[1], fr_recv.at[1]).wait_send()
    tally(seven, q_send.at[0], q_recv.at[0]).wait_send()
    tally(rests, v_send.at[0], v_recv.at[0]).wait_send()
    for i in range(3):
        each_home(lambda at, i=i: home(i, at, y).wait_send())


def experts_back(*operands):
    dma = pltpu.SemaphoreType.DMA
    vm = pl.BlockSpec(memory_space=VMEM)
    hbm = pl.BlockSpec(memory_space=pl.ANY)
    shape = jax.ShapeDtypeStruct
    width = 4 * DB
    pairs_of = lambda *dims: [dma(dims), dma(dims)]
    return pl.pallas_call(
        experts_back_kernel,
        out_shape=(
            shape((128, 1024), BF16),
            shape((128, 1024), F32),
            shape((1, 1024), F32),
            shape((4, 3, FFB, DB), BF16),
            shape((16, 1024), F32),
            shape((2, 4, 4, 4, 256, 128), BF16),
            shape((16, 2 * ROWS, width), BF16),
        ),
        in_specs=[hbm] * 18,
        out_specs=(vm,) * 3 + (hbm, vm, hbm, hbm),
        scratch_shapes=[
            VMEM((128, 1024), F32),
            VMEM((128, 8), F32),
            VMEM((8, 128), F32),
            VMEM((128, 1024), BF16),
            VMEM((1, 1024), F32),
            VMEM((8, 1024), F32),
            VMEM((1024, 128), BF16),
            VMEM((3, 64, 2048), BF16),
            VMEM((64, 2048), F32),
            VMEM((1, 2048), F32),
            VMEM((128, 1024), BF16),
            VMEM((1, 1024), F32),
            VMEM((FFQ, DB), BF16),
            VMEM((2, 4, 4, 4, 256, 128), BF16),
            VMEM((4, 4, 128, 1024), BF16),
            VMEM((3 * FFQ, width), BF16),
            VMEM((64 * ROWS, width), BF16),
            VMEM((3072, width), BF16),
            VMEM((32 * ROWS, width), BF16),
            VMEM((32 * ROWS, width), BF16),
            VMEM((2, 8 * ROWS, width), BF16),
            VMEM((8 * ROWS, width), F32),
            VMEM((32 * ROWS, FFQ), BF16),
            VMEM((32 * ROWS, FFQ), BF16),
            VMEM((32 * ROWS, FFQ), BF16),
            VMEM((2, 3, FFQ // 2, DB), BF16),
            VMEM((2, 3, FFQ, DB), BF16),
            VMEM((16, 64, 128), BF16),
            VMEM((16, 1024), F32),
            VMEM((512, 1024), BF16),
            VMEM((3, 512, DB), BF16),
            VMEM((512, DB), BF16),
            VMEM((16, 32, DB), BF16),
            VMEM((16, 16, 128), F32),
            VMEM((16, 128), F32),
            VMEM((16, 128), F32),
            VMEM((8, 16, 128), F32),
            VMEM((64, 2048), BF16),
            VMEM((2048, 128), BF16),
            VMEM((1, 2048), F32),
            VMEM((2048, 128), F32),
            VMEM((3, 64, 2048), BF16),
            VMEM((3, 16, 64, 128), BF16),
            VMEM((192, 1024), BF16),
            VMEM((256, 128), BF16),
            VMEM((8, 192, 128), BF16),
            VMEM((1, 1024), F32),
            VMEM((16, 1, 1024), F32),
            VMEM((8, 1, 1024), F32),
            dma((27,)),
            dma((2,)),
            dma((1,)),
            dma((16,)),
            dma((1,)),
            dma((4,)),
            *pairs_of(4),
            *pairs_of(1),
            *pairs_of(2, 2),
            *pairs_of(2, 3, 2),
            *pairs_of(3, 4),
            *pairs_of(2, 2),
            *pairs_of(1),
            *pairs_of(1),
            *pairs_of(1),
            dma((5, 4)),
            dma((5, 6)),
            dma((1,)),
            dma((5, 5)),
            *pairs_of(1),
            *pairs_of(1),
            *pairs_of(1),
            *pairs_of(1),
            *pairs_of(1),
            *pairs_of(1),
            *pairs_of(2),
        ],
        compiler_params=params(2, 63),
    )(*operands)


def unfold_kernel(
    f_ref,
    o_ref,
    g_ref,
    few_ref,
    y_ref,
    in_ref,
    norm_ref,
    qkv_ref,
    out_ref,
    gate_ref,
    up_ref,
    down_ref,
    router_ref,
    gain_ref,
    y_out_ref,
    in_out_ref,
    norm_out_ref,
):
    y_out_ref[...] = y_ref[...]
    in_out_ref[...] = in_ref[...]
    norm_out_ref[...] = norm_ref[...]
    router_ref[...] = few_ref[:8]
    gain_ref[...] = few_ref[8:9]
    for i in range(3):
        part = f_ref[:, :, 64 * i : 64 * (i + 1)].reshape(1024, 128)
        qkv_ref[:, 1024 * i : 1024 * (i + 1)] = part.T.astype(F32)
    for i in range(4):
        for h in range(2):
            part = o_ref[i, :, 32 * h : 32 * (h + 1)].reshape(128, 128)
            out_ref[:, (2 * i + h) * 128 : (2 * i + h + 1) * 128] = part.astype(F32)
    gate_ref[...] = g_ref[0].astype(F32)
    up_ref[...] = g_ref[1].astype(F32)
    down_ref[...] = g_ref[2].astype(F32)


def unfold(full, blocks, few, block_output, input_grad, gain_grad):
    shape = jax.ShapeDtypeStruct
    share = pl.BlockSpec((None, FFB, 128), lambda i, j: (i, 0, j))
    return pl.pallas_call(
        unfold_kernel,
        out_shape=(
            shape((1024, 3072), F32),
            shape((1024, 1024), F32),
            *[shape((4, FFB, DB), F32)] * 3,
            shape((8, 1024), F32),
            shape((1, 1024), F32),
            shape((128, 1024), BF16),
            shape((128, 1024), F32),
            shape((1, 1024), F32),
        ),
        grid=(4, 2),
        in_specs=[
            pl.BlockSpec((None, None, 4, 4, 192, 128), lambda i, j: (j, i, 0, 0, 0, 0)),
            pl.BlockSpec((None, 4, None, 4, 64, 128), lambda i, j: (j, 0, i, 0, 3, 0)),
            pl.BlockSpec((None, 3, FFB, 128), lambda i, j: (i, 0, 0, j)),
            pl.BlockSpec((16, 1024), lambda i, j: (0, 0)),
            pl.BlockSpec((16, 1024), lambda i, j: (2 * i + j, 0)),
            pl.BlockSpec((16, 1024), lambda i, j: (2 * i + j, 0)),
            pl.BlockSpec((1, 1024), lambda i, j: (0, 0)),
        ],
        out_specs=(
            pl.BlockSpec((128, 3072), lambda i, j: (2 * i + j, 0)),
            pl.BlockSpec((128, 1024), lambda i, j: (4 * j + i, 0)),
            *[share] * 3,
            pl.BlockSpec((8, 1024), lambda i, j: (0, 0)),
            pl.BlockSpec((1, 1024), lambda i, j: (0, 0)),
            pl.BlockSpec((16, 1024), lambda i, j: (2 * i + j, 0)),
            pl.BlockSpec((16, 1024), lambda i, j: (2 * i + j, 0)),
            pl.BlockSpec((1, 1024), lambda i, j: (0, 0)),
        ),
        compiler_params=pltpu.CompilerParams(vmem_limit_bytes=62 * 1024 * 1024),
    )(full, full, blocks, few, block_output, input_grad, gain_grad)


def body(
    block_input,
    attn_gain,
    qkv_weight,
    out_weight,
    moe_gain,
    router_weight,
    gate_weight,
    up_weight,
    down_weight,
    routes,
    slot_index,
    cotangent,
):
    (
        send,
        pairs,
        middle,
        probs,
        ctx_tok,
        qkv,
        ctx_here,
        lse,
        down,
        near,
        weights,
        qkv_low,
        out_low,
    ) = attend(
        block_input,
        attn_gain,
        gate_weight,
        up_weight,
        down_weight,
        moe_gain,
        router_weight,
        routes,
        slot_index,
        cotangent,
        qkv_weight,
        out_weight,
    )
    block_output, input_grad, gain_grad, mine, few, full, _ = experts_back(
        middle,
        probs,
        pairs,
        cotangent,
        moe_gain.reshape(1, -1),
        router_weight.T,
        ctx_tok,
        qkv,
        ctx_here,
        lse,
        block_input,
        attn_gain.reshape(1, -1),
        down,
        send,
        weights,
        near,
        qkv_low,
        out_low,
    )
    (
        qkv_grad,
        out_grad,
        gate_grad,
        up_grad,
        down_grad,
        router_grad,
        moe_gain_grad,
        block_output,
        input_grad,
        gain_grad,
    ) = unfold(full, mine, few, block_output, input_grad, gain_grad)
    return (
        block_output,
        input_grad,
        gain_grad.reshape(-1),
        qkv_grad,
        out_grad,
        moe_gain_grad.reshape(-1),
        router_grad.T,
        jnp.swapaxes(gate_grad, 1, 2),
        jnp.swapaxes(up_grad, 1, 2),
        down_grad,
    )


def solution(mesh):
    tokens = P(("dp", "expert", "mp"), None)
    cols = P("expert", "dp", "mp")
    rows = P("expert", "mp", "dp")
    return jax.shard_map(
        body,
        mesh=mesh,
        in_specs=(tokens, P(), P(), P(), P(), P(), cols, cols, rows, tokens, tokens, tokens),
        out_specs=(tokens, tokens, P(), P(), P(), P(), P(), cols, cols, rows),
        check_vma=False,
    )
```
